128 devices in a mesh: rep: 8 (over z, core), dp: 16 (over y, x).
Axes of the slice: x: 4, y: 4, z: 4, core: 2. Of those that a mesh axis runs over, the one named last changes fastest.
Arguments:
- pixels: float32 [131072, 384], P(('rep', 'dp')), may hold values from -6 to 6
- valid_mask: int32 [131072, 384], P(('rep', 'dp')), may hold values from 0 to 1, as said below
- bottom_codes: int32 [1048576], P(('rep', 'dp')), may hold values from 0 to 511
- top_codes: int32 [262144], P(('rep', 'dp')), may hold values from 0 to 511
- params: float32 [736, 128], replicated, may hold values from -1 to 1, as said below
- first_moment: float32 [8, 736, 128], P('rep', 'dp'), may hold values from -0.00390625 to 0.00390625
- second_moment: float32 [8, 736, 128], P('rep', 'dp'), may hold values from 1e-08 to 4e-08
- outer_momentum: float32 [736, 128], P('dp'), may hold values from -0.3125 to 0.3125
- ema_counts: float32 [2, 512], replicated, may hold values from 128 to 512
- ema_sums: float32 [2, 512, 64], replicated, may hold values from -1536 to 1536
- codebooks: float32 [2, 512, 64], replicated, may hold values from -6 to 6
Outputs:
- total_loss: float32 [8], P('rep')
- valid_count: float32 [8], P('rep')
- new_params: float32 [736, 128], P('dp')
- new_first: float32 [8, 736, 128], P('rep', 'dp')
- new_second: float32 [8, 736, 128], P('rep', 'dp')
- new_momentum: float32 [736, 128], P('dp')
- new_counts: float32 [8, 2, 512], P('rep')
- new_sums: float32 [8, 2, 512, 64], P('rep')
- new_codebooks: float32 [8, 2, 512, 64], P('rep')
The draws below stay inside these ranges and needn't reach their ends.
Inputs may be any that keep to these rules, and one draw needn't show every extreme that they name: `valid_mask`: 1 marks a valid pixel. `params`: fan-in scaled weights.
All inputs are finite; a program needn't handle non-finite values.
Results may differ from the reference program's by a relative error of at most 0.0003.
Values sent between devices are 32-bit elements; how exact they have to be, the bound alone decides.
A program may use at most 128 MiB of HBM per device.

```python
import math
import jax
import jax.numpy as jnp
import numpy as np
from jax import lax

PF = 48
C = 128
RES = 64
EMB = 64
K = 512
STEP = 10
PATCH_DEV = 8192
PROWS = 736
GROUP_ROWS = 131072
TOTAL = 1048576
N_REP = 8
N_DP = 16


def draw_valid_mask(key, part):
    key = jax.random.fold_in(key, 3)
    draws = jax.random.randint(key, (TOTAL, PF), 0, 100)
    position = jnp.arange(TOTAL, dtype=jnp.int32) % GROUP_ROWS
    threshold = 25 + 50 * position // GROUP_ROWS
    return (draws < threshold[:, None]).astype(jnp.int32).reshape(TOTAL // 8, 8 * PF)


def draw_params(key, part):
    key = jax.random.fold_in(key, 11)
    counts = [PF, RES, 4 * EMB, EMB, EMB, RES, EMB, EMB, PF]
    fanins = [PF, RES, 4 * EMB, 2 * EMB, 2 * EMB, C, C, C, C]
    table = np.concatenate([np.full(count, fanin ** (-0.5), dtype=np.float32) for count, fanin in zip(counts, fanins)])
    values = jnp.clip(jax.random.normal(key, (PROWS, C), jnp.float32), -4.0, 4.0)
    return values * jnp.asarray(table)[:, None]


def plant(entries, rng, least, high):
    longest = entries.shape.index(max(entries.shape))
    spots = []
    for shift in (0, 1):
        where = [jax.random.randint(jax.random.fold_in(rng, axis), (), 0, length) for axis, length in enumerate(entries.shape)]
        where[longest] = (where[longest] + shift) % entries.shape[longest]
        spots.append(tuple(where))
    return entries.at[spots[0]].set(least).at[spots[1]].set(high)


def levels(own_key, shape, cuts, smallest, largest):
    def one(axis_at, blocks):
        heights = jax.random.uniform(jax.random.fold_in(jax.random.fold_in(own_key, 6), axis_at), (blocks,), jnp.float32, smallest / len(cuts), largest / len(cuts))
        return jnp.repeat(jnp.exp(heights), shape[axis_at] // blocks).reshape((-1,) + (1,) * (len(shape) - axis_at - 1))

    factor_of = one(*cuts[0])
    for cut in cuts[1:]:
        factor_of = factor_of * one(*cut)
    return factor_of


def centred(own_key, dims, spread, bound, shards=(), kind=jnp.bfloat16):
    loudness = levels(own_key, dims, shards, -0.22, 0.18) if shards else 1.0
    entries = jax.random.normal(own_key, dims, jnp.float32) * spread * loudness
    return jnp.minimum(jnp.maximum(entries, -bound), bound).astype(kind)


def setup_inputs(seed: int = 0) -> dict:
    arg_keys = jax.random.split(jax.random.key(seed), 12)
    return {
        "pixels": centred(arg_keys[0], (TOTAL // 8, 8 * PF), 1.0, 6.0, ((0, 128),), jnp.float32),
        "valid_mask": draw_valid_mask(jax.random.fold_in(arg_keys[11], 71), 0),
        "bottom_codes": plant(jax.random.randint(arg_keys[2], (TOTAL,), 0, K), jax.random.fold_in(arg_keys[2], 1), 0, K - 1).astype(jnp.int32),
        "top_codes": plant(jax.random.randint(arg_keys[3], (TOTAL // 4,), 0, K), jax.random.fold_in(arg_keys[3], 1), 0, K - 1).astype(jnp.int32),
        "params": draw_params(jax.random.fold_in(arg_keys[11], 71), 0),
        "first_moment": centred(arg_keys[5], (N_REP, PROWS, C), 0.0003, 0.00390625, ((0, 8), (1, 16)), jnp.float32),
        "second_moment": jnp.clip(jnp.exp(math.log(3.999999975690116e-08) - 1.3862944 * jax.random.uniform(arg_keys[6], (N_REP, PROWS, C), jnp.float32) ** levels(arg_keys[6], (N_REP, PROWS, C), ((0, 8), (1, 16)), -0.2, 0.2)), 9.99999993922529e-09, 3.999999975690116e-08),
        "outer_momentum": centred(arg_keys[7], (PROWS, C), 0.02, 0.3125, ((0, 16),), jnp.float32),
        "ema_counts": jnp.clip(jnp.exp(jax.random.uniform(arg_keys[8], (2, K), jnp.float32, math.log(128.0), math.log(512.0))), 128.0, 512.0),
        "ema_sums": centred(arg_keys[9], (2, K, EMB), (PATCH_DEV * N_DP / K), 1536.0, (), jnp.float32),
        "codebooks": centred(arg_keys[10], (2, K, EMB), 1.0, 6.0, (), jnp.float32),
    }


@jax.custom_vjp
def low(v):
    return lax.optimization_barrier(v.astype(jnp.bfloat16)).astype(jnp.float32)

@jax.custom_vjp
def low_back(v):
    return v

def low_keep(v):
    return (low(v), None)

def low_pass(kept, grad):
    return (grad,)

def back_keep(v):
    return (v, None)

def back_low(kept, grad):
    return (low(grad),)
low.defvjp(low_keep, low_pass)
low_back.defvjp(back_keep, back_low)
beta_commit = 0.25
ema_decay = 0.8
laplace_eps = 1e-05
inner_rate = 0.03
beta_first = 0.9
beta_second = 0.999
adam_eps = 1e-08
weight_decay = 0.01
outer_rate = 0.7
outer_moment = 0.9

def matmul_hi(left, right):
    return jnp.dot(left, right, precision=lax.Precision.HIGHEST)

def silu_act(value):
    return value * jax.nn.sigmoid(value)

def unpack(params):
    counts = [PF, RES, 4 * EMB, EMB, EMB, RES, EMB, EMB, PF]
    pieces = []
    start = 0
    for count in counts:
        pieces.append(params[start:start + count])
        start = start + count
    return pieces

def encode(params, pixels):
    pieces = unpack(params)
    hid_enc = silu_act(matmul_hi(pixels, pieces[0]))
    hid_res = hid_enc + matmul_hi(silu_act(matmul_hi(hid_enc, pieces[5].T)), pieces[1])
    latent_b = matmul_hi(hid_res, pieces[6].T)
    top_in = latent_b.reshape(-1, 4 * EMB)
    latent_t = matmul_hi(silu_act(matmul_hi(top_in, pieces[2])), pieces[7].T)
    return (latent_b, latent_t)

def objective(params, pixels, weight_mask, quant_b, quant_t, shift_b, shift_t, valid_count):
    latent_b, latent_t = encode(params, pixels)
    pieces = unpack(params)
    pre_dec = matmul_hi(latent_b + shift_b, pieces[3]) + jnp.repeat(matmul_hi(latent_t + shift_t, pieces[4]), 4, axis=0)
    recon = matmul_hi(silu_act(pre_dec), pieces[8].T)
    squared = jnp.sum(weight_mask * (recon - pixels) * (recon - pixels))
    commit_b = jnp.sum((latent_b - quant_b) * (latent_b - quant_b)) / (GROUP_ROWS * EMB)
    commit_t = jnp.sum((latent_t - quant_t) * (latent_t - quant_t)) / (GROUP_ROWS // 4 * EMB)
    return squared / valid_count + beta_commit * (commit_b + commit_t)

def reference(pixels, valid_mask, bottom_codes, top_codes, params, first_moment, second_moment, outer_momentum, ema_counts, ema_sums, codebooks):
    pixels = pixels.reshape(-1, PF)
    valid_mask = valid_mask.reshape(-1, PF)
    book_range = jnp.arange(K, dtype=jnp.int32)
    bias_first = 1.0 - beta_first ** STEP
    bias_second = 1.0 - beta_second ** STEP
    delta_sum = jnp.zeros_like(params)
    losses, valids, firsts, seconds, counts_out, sums_out, books_out = ([], [], [], [], [], [], [])
    for group in range(N_REP):
        start = group * GROUP_ROWS
        patch_rows = pixels[start:start + GROUP_ROWS]
        weight_mask = valid_mask[start:start + GROUP_ROWS].astype(pixels.dtype)
        codes_b = bottom_codes[start:start + GROUP_ROWS]
        codes_t = top_codes[start // 4:(start + GROUP_ROWS) // 4]
        onehot_b = (codes_b[:, None] == book_range[None, :]).astype(pixels.dtype)
        onehot_t = (codes_t[:, None] == book_range[None, :]).astype(pixels.dtype)
        quant_b = matmul_hi(onehot_b, codebooks[0])
        quant_t = matmul_hi(onehot_t, codebooks[1])
        latent_b, latent_t = encode(params, patch_rows)
        count_here = jnp.sum(weight_mask)

        def loss_of(weights):
            return objective(weights, patch_rows, weight_mask, quant_b, quant_t, quant_b - latent_b, quant_t - latent_t, count_here)
        loss_value, pullback = jax.vjp(loss_of, params)
        grads = pullback(jnp.ones_like(loss_value))[0]
        seen = jnp.stack([lax.optimization_barrier(jnp.sum(onehot_b, axis=0)), lax.optimization_barrier(jnp.sum(onehot_t, axis=0))])
        summed = jnp.stack([matmul_hi(onehot_b.T, latent_b), matmul_hi(onehot_t.T, latent_t)])
        counts_new = ema_decay * ema_counts + (1.0 - ema_decay) * seen
        sums_new = ema_decay * ema_sums + (1.0 - ema_decay) * summed
        totals = lax.optimization_barrier(jnp.sum(counts_new, axis=1, keepdims=True))
        smooth = (counts_new + laplace_eps) / (totals + K * laplace_eps) * totals
        first_new = beta_first * first_moment[group] + (1.0 - beta_first) * grads
        second_new = beta_second * second_moment[group] + (1.0 - beta_second) * grads * grads
        step_here = inner_rate * (first_new / bias_first / (jnp.sqrt(second_new / bias_second) + adam_eps) + weight_decay * params)
        delta_sum = delta_sum + step_here
        losses.append(loss_value)
        valids.append(count_here)
        firsts.append(first_new)
        seconds.append(second_new)
        counts_out.append(counts_new)
        sums_out.append(sums_new)
        books_out.append(sums_new / smooth[:, :, None])
    mean_delta = delta_sum / N_REP
    momentum_new = outer_moment * outer_momentum + mean_delta
    params_new = params - outer_rate * (mean_delta + outer_moment * momentum_new)
    return (jnp.stack(losses), jnp.stack(valids), params_new, jnp.stack(firsts), jnp.stack(seconds), momentum_new, jnp.stack(counts_out), jnp.stack(sums_out), jnp.stack(books_out))
```

```python
import functools
import jax
import jax.numpy as jnp
from jax import lax
from jax.experimental import pallas as pl
from jax.experimental.pallas import tpu as pltpu
from jax.sharding import PartitionSpec as P

PF = 48
EMB = 64
K = 512
STEP = 10
beta_commit = 0.25
ema_decay = 0.8
laplace_eps = 1e-05
inner_rate = 0.03
beta_first = 0.9
beta_second = 0.999
adam_eps = 1e-08
weight_decay = 0.01
outer_rate = 0.7
outer_moment = 0.9

bf16 = jnp.bfloat16
f32 = jnp.float32
O_ENC, O_RU, O_TI, O_DB, O_DT, O_RD, O_L, O_TO, O_OUT, O_END = 0, 48, 112, 368, 432, 496, 560, 624, 688, 736


def nn(a, b):
    return lax.dot_general(a, b, (((1,), (0,)), ((), ())), preferred_element_type=f32)


def nt(a, b):
    return lax.dot_general(a, b, (((1,), (1,)), ((), ())), preferred_element_type=f32)


def tn(a, b):
    return lax.dot_general(a, b, (((0,), (0,)), ((), ())), preferred_element_type=f32)


def split(v):
    hi = v.astype(bf16)
    return hi, (v - hi.astype(f32)).astype(bf16)


def pair(v):
    hi, lo = split(v)
    return jnp.concatenate([hi, lo], axis=1)


def quad(v):
    hi, lo = split(v)
    return jnp.concatenate([hi, hi, lo, lo], axis=1)


def twice(v):
    return jnp.concatenate([v, v], axis=0)


def silu_and_slope(v):
    s = 0.5 * jnp.tanh(0.5 * v) + 0.5
    a = v * s
    return a, s + a * (1.0 - s)


def lanes(parts):
    return jnp.concatenate(parts, axis=1)


def spread_codes(codes, per_row):
    a = codes.shape[0]
    rows = a * 128 // per_row
    span = 128 // per_row
    lo = (codes & 255).astype(f32).astype(bf16)
    hi = (codes >> 8).astype(f32).astype(bf16)
    up = (lax.broadcasted_iota(jnp.int32, (a, rows), 0) == lax.broadcasted_iota(jnp.int32, (a, rows), 1) // span)
    up = up.astype(f32).astype(bf16)
    keep = (
        lax.broadcasted_iota(jnp.int32, (128, rows), 0) // per_row
        == lax.broadcasted_iota(jnp.int32, (128, rows), 1) % span
    )
    pick = (
        lax.broadcasted_iota(jnp.int32, (8, 128), 0)
        == lax.broadcasted_iota(jnp.int32, (8, 128), 1) % per_row
    )
    pick = pick.astype(f32).astype(bf16)
    out = []
    for part in (lo, hi):
        wide = jnp.where(keep, tn(part, up), 0.0).astype(bf16)
        out.append(nn(pick, wide))
    return out


def swap_start(axis, n, src_at, buf, sems):
    me = lax.axis_index(axis)

    def go(k, carry):
        peer = lax.rem(me + k, n)
        pltpu.make_async_remote_copy(
            src_ref=src_at(peer), dst_ref=buf.at[me], send_sem=sems[0].at[peer], recv_sem=sems[1].at[me],
            device_id={axis: peer}, device_id_type=pl.DeviceIdType.MESH,
        ).start()
        return carry

    lax.fori_loop(1, n, go, 0)


def swap_wait(axis, n, src_at, buf, sems, recv):
    me = lax.axis_index(axis)

    def go(k, carry):
        peer = lax.rem(me + k, n)
        copy = pltpu.make_async_remote_copy(
            src_ref=src_at(peer), dst_ref=buf.at[peer], send_sem=sems[0].at[peer], recv_sem=sems[1].at[peer],
            device_id={axis: peer}, device_id_type=pl.DeviceIdType.MESH,
        )
        if recv:
            copy.wait_recv()
        else:
            copy.wait_send()
        return carry

    lax.fori_loop(1, n, go, 0)


def total(v):
    return jnp.sum(jnp.sum(v, axis=1, keepdims=True), axis=0, keepdims=True)


def in_order(buf, n):
    out = buf[0]
    for s in range(1, n):
        out = out + buf[s]
    return out


WS = {
    "enc_f": (128, 96), "ru_f": (128, 128), "ti_f": (128, 512), "db_f": (128, 256), "dt_f": (128, 256), "rd_f": (64, 256),
    "l_f": (64, 256), "to_f": (64, 256), "out_f": (48, 256), "out_b": (128, 96), "db_b": (64, 256), "dt_b": (64, 256),
    "to_b": (128, 128), "ti_b": (256, 256), "l_b": (128, 128), "ru_b": (64, 256), "rd_b": (128, 128), "book": (2, 128, 512),
}
N_DP = 16
N_REP = 8
SHARE = 46


def kernel(
    x_ref, m_ref, cb_ref, ct_ref, p_ref, first_ref, second_ref, mom_ref, cnt_ref, ema_ref, book_ref,
    loss_out, valid_out, params_out, first_out, second_out, mom_out, counts_out, sums_out, books_out,
    *scratch, R,
):
    w = dict(zip(WS, scratch))
    (
        codes_b, codes_t, acc, sacc, lacc, valid_own, valid_all, stat_own, stat_all, grad_own, grad_all, part_all,
        sums_all, step_all, par_share, *sems,
    ) = scratch[len(WS):]
    codes = (codes_b, codes_t)
    sems = [(sems[2 * i], sems[2 * i + 1]) for i in range(6)]
    sem_valid, sem_stat, sem_grad, sem_part, sem_sums, sem_step = sems
    dp = lax.axis_index("dp")
    rep = lax.axis_index("rep")

    barrier = pltpu.get_barrier_semaphore()
    for axis, n, me in (("dp", N_DP, dp), ("rep", N_REP, rep)):
        def hello(k, carry):
            pl.semaphore_signal(
                barrier, inc=1, device_id={axis: lax.rem(me + k, n)}, device_id_type=pl.DeviceIdType.MESH
            )
            return carry

        lax.fori_loop(1, n, hello, 0)

    rows = x_ref.shape[0]
    valid_own[...] = jnp.broadcast_to(total(m_ref[...].astype(f32)), (8, 128))
    valid_all[dp] = valid_own[...]
    pl.semaphore_wait(barrier, N_DP + N_REP - 2)
    valid_src = lambda peer: valid_own
    swap_start("dp", N_DP, valid_src, valid_all, sem_valid)

    par = p_ref[...]
    part = par.T
    f = lambda lo, hi: par[lo:hi]
    t = lambda lo, hi: part[:, lo:hi]
    w["enc_f"][...] = pair(t(O_ENC, O_RU))
    w["ru_f"][...] = pair(t(O_RU, O_TI))
    w["ti_f"][...] = pair(t(O_TI, O_DB))
    w["db_f"][...] = quad(t(O_DB, O_DT))
    w["dt_f"][...] = quad(t(O_DT, O_RD))
    w["rd_f"][...] = pair(f(O_RD, O_L))
    w["l_f"][...] = pair(f(O_L, O_TO))
    w["to_f"][...] = pair(f(O_TO, O_OUT))
    w["out_f"][...] = pair(f(O_OUT, O_END))
    w["out_b"][...] = pair(t(O_OUT, O_END))
    w["db_b"][...] = pair(f(O_DB, O_DT))
    w["dt_b"][...] = pair(f(O_DT, O_RD))
    w["to_b"][...] = pair(t(O_TO, O_OUT))
    w["ti_b"][...] = pair(f(O_TI, O_DB))
    w["l_b"][...] = pair(t(O_L, O_TO))
    w["ru_b"][...] = pair(f(O_RU, O_TI))
    w["rd_b"][...] = pair(t(O_RD, O_L))
    for level in (0, 1):
        hi, lo = split(book_ref[level])
        w["book"][level] = jnp.concatenate([hi, lo], axis=0)
    for ref, src, per in ((codes[0], cb_ref, 8), (codes[1], ct_ref, 2)):
        lo, hi = spread_codes(src[...], per)
        ref[0] = lo + 256.0 * hi
        ref[1] = lo + 256.0 * (1.0 - hi)
    for s in range(N_DP):
        par_share[s, 0:SHARE] = p_ref[SHARE * s : SHARE * s + SHARE]
    acc[...] = jnp.zeros_like(acc)
    sacc[...] = jnp.zeros_like(sacc)
    lacc[...] = jnp.zeros_like(lacc)
    group_rows = rows * 8 * N_DP
    swap_wait("dp", N_DP, valid_src, valid_all, sem_valid, True)
    count = in_order(valid_all, N_DP)[0:1, 0:1]
    kb = beta_commit / (group_rows * EMB) * count
    kt = beta_commit / (group_rows // 4 * EMB) * count
    ids = lax.broadcasted_iota(jnp.int32, (256, R), 0).astype(f32)

    def onehot(keys, n):
        cols = []
        for p in range(n):
            halves = [
                jnp.where(ids == keys[h][p : p + 1, :], 1.0, 0.0).astype(bf16)
                for h in (0, 1)
            ]
            cols.append(jnp.concatenate(halves, axis=0))
        return lanes(cols)

    def step(i, carry):
        at = pl.multiple_of(i * R, R)
        xt = x_ref[pl.ds(at, R), :].T
        mt = m_ref[pl.ds(at, R), :].astype(f32).T
        x = lanes([xt[48 * p : 48 * p + 48] for p in range(8)])
        m = lanes([mt[48 * p : 48 * p + 48] for p in range(8)])
        xb = x.astype(bf16)
        he, de = silu_and_slope(nn(w["enc_f"][...], twice(xb)))
        heb = he.astype(bf16)
        ar, dr = silu_and_slope(nn(w["rd_f"][...], twice(heb)))
        arb = ar.astype(bf16)
        hrb = (he + nn(w["ru_f"][...], twice(arb))).astype(bf16)
        lb = nn(w["l_f"][...], twice(hrb))
        lbb = lb.astype(bf16)
        ti = lanes([
            jnp.concatenate([lbb[:, R * p : R * p + R] for p in range(4 * g, 4 * g + 4)], axis=0) for g in (0, 1)
        ])
        ht, dt = silu_and_slope(nn(w["ti_f"][...], twice(ti)))
        htb = ht.astype(bf16)
        lt = nn(w["to_f"][...], twice(htb))
        ob = onehot([codes[0][h, :, pl.ds(at, R)] for h in (0, 1)], 8)
        ot = onehot([codes[1][h, :, pl.ds(at, R)] for h in (0, 1)], 2)
        qb2 = nn(w["book"][0], ob).astype(bf16)
        qt2 = nn(w["book"][1], ot).astype(bf16)
        ones = jnp.ones((16, 8 * R), bf16)
        sacc[0] += nt(jnp.concatenate([lbb, ones], axis=0), ob)
        sacc[1] += nt(jnp.concatenate([lt.astype(bf16), ones[:, : 2 * R]], axis=0), ot)
        gap_b = lb - (qb2[:64].astype(f32) + qb2[64:].astype(f32))
        gap_t = lt - (qt2[:64].astype(f32) + qt2[64:].astype(f32))
        top = nn(w["dt_f"][...], twice(qt2))
        pre = nn(w["db_f"][...], twice(qb2)) + lanes([top[:, R * (p // 4) : R * (p // 4) + R] for p in range(8)])
        hd, dd = silu_and_slope(pre)
        hdb = hd.astype(bf16)
        err = nn(w["out_f"][...], twice(hdb)) - x
        me = m * err
        lacc[0:48] += sum((me * err)[:, R * p : R * p + R] for p in range(8))
        lacc[48:112] += sum((gap_b * gap_b)[:, R * p : R * p + R] for p in range(8))
        lacc[112:176] += sum((gap_t * gap_t)[:, R * p : R * p + R] for p in range(2))
        grb = me.astype(bf16)
        acc[O_OUT:O_END] += nt(grb, hdb)
        gpd = nn(w["out_b"][...], twice(grb)) * dd
        gpdb = gpd.astype(bf16)
        g = nt(qb2, gpdb)
        acc[O_DB:O_DT] += g[:64] + g[64:]
        gtrb = lanes([sum(gpd[:, R * p : R * p + R] for p in range(4 * g_, 4 * g_ + 4)) for g_ in (0, 1)]).astype(bf16)
        g = nt(qt2, gtrb)
        acc[O_DT:O_RD] += g[:64] + g[64:]
        gltb = (nn(w["dt_b"][...], twice(gtrb)) + kt * gap_t).astype(bf16)
        acc[O_TO:O_OUT] += nt(gltb, htb)
        gptb = (nn(w["to_b"][...], twice(gltb)) * dt).astype(bf16)
        acc[O_TI:O_DB] += nt(ti, gptb)
        gti = nn(w["ti_b"][...], twice(gptb))
        gti = lanes([gti[64 * (p % 4) : 64 * (p % 4) + 64, R * (p // 4) : R * (p // 4) + R] for p in range(8)])
        glbb = (nn(w["db_b"][...], twice(gpdb)) + gti + kb * gap_b).astype(bf16)
        acc[O_L:O_TO] += nt(glbb, hrb)
        ghr = nn(w["l_b"][...], twice(glbb))
        ghrb = ghr.astype(bf16)
        acc[O_RU:O_TI] += nt(arb, ghrb)
        gprb = (nn(w["ru_b"][...], twice(ghrb)) * dr).astype(bf16)
        acc[O_RD:O_L] += nt(gprb, heb)
        gpeb = ((ghr + nn(w["rd_b"][...], twice(gprb))) * de).astype(bf16)
        acc[O_ENC:O_RU] += nt(xb, gpeb)
        return carry

    lax.fori_loop(0, rows // R, step, 0)

    scale = 2.0 / count
    for s in range(N_DP):
        grad_own[s, 0:SHARE] = acc[SHARE * s : SHARE * s + SHARE] * scale
    grad_src = lambda peer: grad_own.at[peer]
    swap_start("dp", N_DP, grad_src, grad_all, sem_grad)
    part_src = lambda peer: sacc.at[peer // 8, pl.ds(pl.multiple_of(8 * lax.rem(peer, 8), 8), 8)]
    swap_start("dp", N_DP, part_src, part_all, sem_part)
    one = lambda v: jnp.broadcast_to(total(v), (1, 128))
    stat_own[...] = jnp.concatenate(
        [sacc[level][64:65, 128 * j : 128 * j + 128] for level in (0, 1) for j in range(4)]
        + [one(lacc[0:48]), one(lacc[48:112]), one(lacc[112:176]), jnp.zeros((5, 128), f32)], axis=0
    )
    stat_src = lambda peer: stat_own
    swap_start("dp", N_DP, stat_src, stat_all, sem_stat)
    grad_all[dp] = grad_own[dp]
    part_all[dp] = part_src(dp)[...]
    stat_all[dp] = stat_own[...]

    swap_wait("dp", N_DP, grad_src, grad_all, sem_grad, True)
    grads = in_order(grad_all, N_DP)[0:SHARE]
    own = par_share[dp][0:SHARE]
    first_new = beta_first * first_ref[0] + (1.0 - beta_first) * grads
    second_new = beta_second * second_ref[0] + (1.0 - beta_second) * grads * grads
    first_out[0] = first_new
    second_out[0] = second_new
    bias_first = 1.0 - beta_first**STEP
    bias_second = 1.0 - beta_second**STEP
    step_here = inner_rate * (
        first_new / bias_first / (jnp.sqrt(second_new / bias_second) + adam_eps) + weight_decay * own
    )
    step_all[rep, 0:SHARE] = step_here
    step_src = lambda peer: step_all.at[rep]
    swap_start("rep", N_REP, step_src, step_all, sem_step)

    swap_wait("dp", N_DP, part_src, part_all, sem_part, True)
    sums_all[dp] = in_order(part_all, N_DP)
    sums_src = lambda peer: sums_all.at[dp]
    swap_start("dp", N_DP, sums_src, sums_all, sem_sums)
    swap_wait("dp", N_DP, stat_src, stat_all, sem_stat, True)
    stats = in_order(stat_all, N_DP)
    seen = jnp.concatenate([lanes([stats[4 * level + j : 4 * level + j + 1] for j in range(4)]) for level in (0, 1)], axis=0)
    counts_new = ema_decay * cnt_ref[...] + (1.0 - ema_decay) * seen
    counts_out[0] = counts_new
    totals = jnp.sum(counts_new, axis=1, keepdims=True)
    smooth = (counts_new + laplace_eps) / (totals + K * laplace_eps) * totals
    loss = stats[8:9, 0:1] / count + beta_commit * (
        stats[9:10, 0:1] / (group_rows * EMB) + stats[10:11, 0:1] / (group_rows // 4 * EMB)
    )
    loss_out[0] = jnp.sum(loss)
    valid_out[0] = jnp.sum(count)

    swap_wait("rep", N_REP, step_src, step_all, sem_step, True)
    mean_delta = in_order(step_all, N_REP)[0:SHARE] * (1.0 / N_REP)
    momentum_new = outer_moment * mom_ref[...] + mean_delta
    mom_out[...] = momentum_new
    params_out[...] = own - outer_rate * (mean_delta + outer_moment * momentum_new)

    swap_wait("dp", N_DP, sums_src, sums_all, sem_sums, True)
    for level in (0, 1):
        inverse = 1.0 / smooth[level : level + 1]
        for j in range(8):
            rows_j = slice(8 * j, 8 * j + 8)
            sums_new = ema_decay * ema_ref[level, rows_j] + (1.0 - ema_decay) * sums_all[8 * level + j]
            sums_out[0, level, rows_j] = sums_new
            books_out[0, level, rows_j] = sums_new * inverse

    for axis, n, src, buf, sem in (
        ("dp", N_DP, valid_src, valid_all, sem_valid), ("dp", N_DP, grad_src, grad_all, sem_grad),
        ("dp", N_DP, part_src, part_all, sem_part), ("dp", N_DP, stat_src, stat_all, sem_stat),
        ("rep", N_REP, step_src, step_all, sem_step), ("dp", N_DP, sums_src, sums_all, sem_sums),
    ):
        swap_wait(axis, n, src, buf, sem, False)


def shards(
    pixels, valid_mask, bottom_codes, top_codes, params, first_moment, second_moment, outer_momentum, ema_counts,
    ema_sums, codebooks, *, R,
):
    rows = pixels.shape[0]
    vm = pl.BlockSpec(memory_space=pltpu.VMEM)
    sm = pl.BlockSpec(memory_space=pltpu.SMEM)
    shape = lambda *s: jax.ShapeDtypeStruct(s, f32)
    dma = pltpu.SemaphoreType.DMA
    outs = pl.pallas_call(
        functools.partial(kernel, R=R),
        out_shape=(
            shape(1), shape(1), shape(SHARE, 128), shape(1, SHARE, 128), shape(1, SHARE, 128), shape(SHARE, 128),
            shape(1, 2, K), shape(1, 2, EMB, K), shape(1, 2, EMB, K),
        ),
        in_specs=[vm] * 11,
        out_specs=(sm, sm) + (vm,) * 7,
        scratch_shapes=[pltpu.VMEM(s, bf16) for s in WS.values()]
        + [pltpu.VMEM((2, 8, rows), f32)] * 2
        + [
            pltpu.VMEM((736, 128), f32), pltpu.VMEM((2, 80, 512), f32), pltpu.VMEM((176, R), f32),
            pltpu.VMEM((8, 128), f32), pltpu.VMEM((N_DP, 8, 128), f32),
            pltpu.VMEM((16, 128), f32), pltpu.VMEM((N_DP, 16, 128), f32),
            pltpu.VMEM((N_DP, 48, 128), f32), pltpu.VMEM((N_DP, 48, 128), f32),
            pltpu.VMEM((N_DP, 8, 512), f32), pltpu.VMEM((N_DP, 8, 512), f32),
            pltpu.VMEM((N_REP, 48, 128), f32), pltpu.VMEM((N_DP, 48, 128), f32),
        ]
        + [dma((N_DP,))] * 10 + [dma((N_REP,))] * 2,
        compiler_params=pltpu.CompilerParams(
            vmem_limit_bytes=56 * 2**20, collective_id=0, has_side_effects=True
        ),
    )(
        pixels, valid_mask, bottom_codes.reshape(-1, 128), top_codes.reshape(-1, 128), params, first_moment,
        second_moment, outer_momentum, ema_counts, jnp.swapaxes(ema_sums, 1, 2), jnp.swapaxes(codebooks, 1, 2),
    )
    return outs[:7] + (jnp.swapaxes(outs[7], 2, 3), jnp.swapaxes(outs[8], 2, 3))


def solution(mesh):
    return jax.shard_map(
        functools.partial(shards, R=256),
        mesh=mesh,
        in_specs=(
            P(("rep", "dp"), None),
            P(("rep", "dp"), None),
            P(("rep", "dp")),
            P(("rep", "dp")),
            P(),
            P("rep", "dp", None),
            P("rep", "dp", None),
            P("dp", None),
            P(),
            P(),
            P(),
        ),
        out_specs=(
            P("rep"),
            P("rep"),
            P("dp", None),
            P("rep", "dp", None),
            P("rep", "dp", None),
            P("dp", None),
            P("rep", None, None),
            P("rep", None, None, None),
            P("rep", None, None, None),
        ),
        check_vma=False,
    )
```

```python
import functools
import jax
import jax.numpy as jnp
from jax import lax
from jax.experimental import pallas as pl
from jax.experimental.pallas import tpu as pltpu
from jax.sharding import PartitionSpec as P

PF = 48
EMB = 64
K = 512
STEP = 10
beta_commit = 0.25
ema_decay = 0.8
laplace_eps = 1e-05
inner_rate = 0.03
beta_first = 0.9
beta_second = 0.999
adam_eps = 1e-08
weight_decay = 0.01
outer_rate = 0.7
outer_moment = 0.9

bf16 = jnp.bfloat16
f32 = jnp.float32
O_ENC, O_RU, O_TI, O_DB, O_DT, O_RD, O_L, O_TO, O_OUT, O_END = 0, 48, 112, 368, 432, 496, 560, 624, 688, 736


def nn(a, b):
    return lax.dot_general(a, b, (((1,), (0,)), ((), ())), preferred_element_type=f32)


def nt(a, b):
    return lax.dot_general(a, b, (((1,), (1,)), ((), ())), preferred_element_type=f32)


def tn(a, b):
    return lax.dot_general(a, b, (((0,), (0,)), ((), ())), preferred_element_type=f32)


def split(v):
    hi = v.astype(bf16)
    return hi, (v - hi.astype(f32)).astype(bf16)


def pair(v):
    hi, lo = split(v)
    return jnp.concatenate([hi, lo], axis=1)


def quad(v):
    hi, lo = split(v)
    return jnp.concatenate([hi, hi, lo, lo], axis=1)


def twice(v):
    return jnp.concatenate([v, v], axis=0)


def silu_and_slope(v):
    s = 0.5 * jnp.tanh(0.5 * v) + 0.5
    a = v * s
    return a, s + a * (1.0 - s)


def lanes(parts):
    return jnp.concatenate(parts, axis=1)


def spread_codes(codes, per_row):
    a = codes.shape[0]
    rows = a * 128 // per_row
    span = 128 // per_row
    lo = (codes & 255).astype(f32).astype(bf16)
    hi = (codes >> 8).astype(f32).astype(bf16)
    up = (lax.broadcasted_iota(jnp.int32, (a, rows), 0) == lax.broadcasted_iota(jnp.int32, (a, rows), 1) // span)
    up = up.astype(f32).astype(bf16)
    keep = (
        lax.broadcasted_iota(jnp.int32, (128, rows), 0) // per_row
        == lax.broadcasted_iota(jnp.int32, (128, rows), 1) % span
    )
    pick = (
        lax.broadcasted_iota(jnp.int32, (8, 128), 0)
        == lax.broadcasted_iota(jnp.int32, (8, 128), 1) % per_row
    )
    pick = pick.astype(f32).astype(bf16)
    out = []
    for part in (lo, hi):
        wide = jnp.where(keep, tn(part, up), 0.0).astype(bf16)
        out.append(nn(pick, wide))
    return out


def stack(v):
    hi, lo = split(v)
    return jnp.concatenate([hi, lo], axis=0)


def halves(v):
    n = v.shape[0] // 2
    return v[:n] + v[n:]


def exact(a, b, dims):
    return lax.dot_general(a, b, ((dims), ((), ())), precision=lax.Precision.HIGHEST, preferred_element_type=f32)


WS = {
    "enc_f": (128, 96), "rd_f": (128, 128), "l_f": (128, 192), "ti_f": (128, 512), "to_f": (128, 128), "db_f": (128, 256),
    "dt_f": (128, 256), "out_f": (96, 128), "out_b": (128, 96), "db_b": (128, 128), "dt_b": (128, 128), "to_b": (128, 128),
    "ti_b": (256, 256), "ru_b": (64, 128), "he_b": (128, 256), "book_b": (128, 512), "book_t": (128, 512),
}
KEEP = {
    "x": (48, 8, bf16), "he": (128, 8, bf16), "de": (128, 8, bf16), "ar": (64, 8, bf16), "dr": (64, 8, bf16),
    "gap_b": (64, 8, bf16), "gl": (64, 8, f32),
}
KEEP_TOP = {
    "ti": (256, bf16), "ht": (128, bf16), "dt": (128, bf16), "gap_t": (64, f32), "gt": (64, f32),
}
ACC = {
    "e": (128, 48), "he": (128, 128), "ar": (64, 64), "ti": (256, 128), "to": (128, 64), "db": (128, 128), "dt": (128, 128),
    "out": (128, 48), "sum_b": (80, 512), "sum_t": (80, 512),
}


def weights(par, book_ref, w):
    part = par.T
    f = lambda lo, hi: par[lo:hi]
    t = lambda lo, hi: part[:, lo:hi]
    w["enc_f"][...] = pair(t(O_ENC, O_RU))
    w["rd_f"][...] = stack(f(O_RD, O_L))
    cross = exact(f(O_L, O_TO), f(O_RU, O_TI), ((1,), (1,)))
    w["l_f"][...] = stack(lanes([f(O_L, O_TO), cross]))
    w["ti_f"][...] = pair(t(O_TI, O_DB))
    w["to_f"][...] = stack(f(O_TO, O_OUT))
    w["db_f"][...] = quad(t(O_DB, O_DT))
    w["dt_f"][...] = quad(t(O_DT, O_RD))
    w["out_f"][...] = stack(f(O_OUT, O_END))
    w["out_b"][...] = pair(t(O_OUT, O_END))
    w["db_b"][...] = stack(f(O_DB, O_DT))
    w["dt_b"][...] = stack(f(O_DT, O_RD))
    w["to_b"][...] = pair(t(O_TO, O_OUT))
    w["ti_b"][...] = pair(f(O_TI, O_DB))
    w["ru_b"][...] = pair(exact(f(O_RU, O_TI), f(O_L, O_TO), ((1,), (1,))))
    w["he_b"][...] = pair(lanes([t(O_L, O_TO), t(O_RD, O_L)]))
    w["book_b"][...] = stack(book_ref[0])
    w["book_t"][...] = stack(book_ref[1])


def code_keys(rows_ref, cols_ref, src, per):
    lo, hi = spread_codes(src[...], per)
    for h, key in ((0, lo + 256.0 * hi), (1, lo + 256.0 * (1.0 - hi))):
        rows_ref[h] = key
        cols_ref[h] = key.T


def hot(equal):
    return jnp.where(equal, jnp.ones((), bf16), jnp.zeros((), bf16))


def forward(i, R, x_ref, m_ref, codes, w, keep, acc, lacc):
    down = lax.broadcasted_iota(jnp.int32, (256, R), 0).astype(f32).astype(bf16)
    along = lax.broadcasted_iota(jnp.int32, (R, 256), 1).astype(f32).astype(bf16)
    at = pl.multiple_of(i * R, R)
    tops = pl.ds(pl.multiple_of(i * 2 * R, 2 * R), 2 * R)

    def by_code(level, n):
        key = [codes[level][0][h, :, pl.ds(at, R)] for h in (0, 1)]
        return lanes([
            jnp.concatenate([hot(down == key[h][p : p + 1, :].astype(bf16)) for h in (0, 1)], axis=0) for p in range(n)
        ])

    def by_patch(level, n):
        key = [codes[level][1][h, pl.ds(at, R), :] for h in (0, 1)]
        return jnp.concatenate([
            lanes([hot(along == jnp.broadcast_to(key[h][:, p : p + 1], (R, 256)).astype(bf16)) for h in (0, 1)]) for p in range(n)
        ], axis=0)

    xt = x_ref[pl.ds(at, R), :].T
    mt = m_ref[pl.ds(at, R), :].astype(f32).T
    x = lanes([xt[48 * p : 48 * p + 48] for p in range(8)])
    m = lanes([mt[48 * p : 48 * p + 48] for p in range(8)])
    xb = x.astype(bf16)
    keep["x"][i] = xb
    he, de = silu_and_slope(nn(w["enc_f"][...], twice(xb)))
    heb = he.astype(bf16)
    keep["he"][i] = heb
    keep["de"][i] = de.astype(bf16)
    ar, dr = silu_and_slope(halves(nn(w["rd_f"][...], heb)))
    arb = ar.astype(bf16)
    keep["ar"][i] = arb
    keep["dr"][i] = dr.astype(bf16)
    lb = halves(nn(w["l_f"][...], jnp.concatenate([heb, arb], axis=0)))
    lbb = lb.astype(bf16)
    ti = lanes([
        jnp.concatenate([lbb[:, R * p : R * p + R] for p in range(4 * g, 4 * g + 4)], axis=0) for g in (0, 1)
    ])
    keep["ti"][:, tops] = ti
    ht, dt = silu_and_slope(nn(w["ti_f"][...], twice(ti)))
    htb = ht.astype(bf16)
    keep["ht"][:, tops] = htb
    keep["dt"][:, tops] = dt.astype(bf16)
    lt = halves(nn(w["to_f"][...], htb))
    qb2 = nn(w["book_b"][...], by_code(0, 8)).astype(bf16)
    qt2 = nn(w["book_t"][...], by_code(1, 2)).astype(bf16)
    ones = jnp.ones((16, 8 * R), bf16)
    acc["sum_b"][...] += nn(jnp.concatenate([lbb, ones], axis=0), by_patch(0, 8))
    acc["sum_t"][...] += nn(jnp.concatenate([lt.astype(bf16), ones[:, : 2 * R]], axis=0), by_patch(1, 2))
    gap_b = lb - halves(qb2.astype(f32))
    gap_t = lt - halves(qt2.astype(f32))
    keep["gap_b"][i] = gap_b.astype(bf16)
    keep["gap_t"][:, tops] = gap_t
    top = nn(w["dt_f"][...], twice(qt2))
    pre = nn(w["db_f"][...], twice(qb2)) + lanes([top[:, R * (p // 4) : R * (p // 4) + R] for p in range(8)])
    hd, dd = silu_and_slope(pre)
    hdb = hd.astype(bf16)
    err = halves(nn(w["out_f"][...], hdb)) - x
    me = m * err
    lacc[0:48] += sum((me * err)[:, R * p : R * p + R] for p in range(8))
    lacc[48:112] += sum((gap_b * gap_b)[:, R * p : R * p + R] for p in range(8))
    lacc[112:176] += sum((gap_t * gap_t)[:, R * p : R * p + R] for p in range(2))
    grb = me.astype(bf16)
    acc["out"][...] += nt(hdb, grb)
    gpd = nn(w["out_b"][...], twice(grb)) * dd
    gpdb = gpd.astype(bf16)
    acc["db"][...] += nt(qb2, gpdb)
    gtrb = lanes([sum(gpd[:, R * p : R * p + R] for p in range(4 * g_, 4 * g_ + 4)) for g_ in (0, 1)]).astype(bf16)
    acc["dt"][...] += nt(qt2, gtrb)
    keep["gt"][:, tops] = halves(nn(w["dt_b"][...], gtrb))
    keep["gl"][i] = halves(nn(w["db_b"][...], gpdb))


def top_backward(n, R, kt, w, keep, acc):
    gltb = (keep["gt"][...] + kt * keep["gap_t"][...]).astype(bf16)
    acc["to"][...] = nt(keep["ht"][...], gltb)
    gptb = (nn(w["to_b"][...], twice(gltb)) * keep["dt"][...].astype(f32)).astype(bf16)
    acc["ti"][...] = nt(keep["ti"][...], gptb)
    gti = nn(w["ti_b"][...], twice(gptb))
    for i in range(n):
        for p in range(8):
            at = 2 * R * i + R * (p // 4)
            keep["gl"][i, :, R * p : R * p + R] += gti[64 * (p % 4) : 64 * (p % 4) + 64, at : at + R]


def backward(i, kb, w, keep, acc):
    glbb = (keep["gl"][i] + kb * keep["gap_b"][i].astype(f32)).astype(bf16)
    gprb = (nn(w["ru_b"][...], twice(glbb)) * keep["dr"][i].astype(f32)).astype(bf16)
    both = jnp.concatenate([glbb, gprb], axis=0)
    acc["he"][...] += nt(both, keep["he"][i])
    acc["ar"][...] += nt(glbb, keep["ar"][i])
    gpeb = (nn(w["he_b"][...], twice(both)) * keep["de"][i].astype(f32)).astype(bf16)
    acc["e"][...] += nt(gpeb, keep["x"][i])


def gradients(par, acc, scale):
    cross = acc["ar"][...]
    w_ru, w_l = par[O_RU:O_TI], par[O_L:O_TO]
    pieces = [
        acc["e"][...].T,
        exact(cross, w_l, ((0,), (0,))),
        acc["ti"][...],
        halves(acc["db"][...]),
        halves(acc["dt"][...]),
        acc["he"][64:128],
        acc["he"][0:64] + exact(cross, w_ru, ((1,), (0,))),
        acc["to"][...].T,
        acc["out"][...].T,
    ]
    return jnp.concatenate(pieces, axis=0) * scale


def scratches(rows, R):
    return (
        [pltpu.VMEM(s, bf16) for s in WS.values()]
        + [pltpu.VMEM((rows // R, c, n * R), t) for c, n, t in KEEP.values()]
        + [pltpu.VMEM((c, rows * 2), t) for c, t in KEEP_TOP.values()]
        + [pltpu.VMEM(s, f32) for s in ACC.values()]
        + [pltpu.VMEM((2, 8, rows), f32), pltpu.VMEM((2, rows, 8), f32)] * 2
        + [pltpu.VMEM((176, R), f32)]
    )


def unscratch(scratch):
    scratch = list(scratch)
    take = lambda names: {k: scratch.pop(0) for k in names}
    w, keep, acc = take(WS), take(list(KEEP) + list(KEEP_TOP)), take(ACC)
    codes = ((scratch.pop(0), scratch.pop(0)), (scratch.pop(0), scratch.pop(0)))
    return w, keep, acc, codes, scratch


def swap_start(axis, n, src_at, buf, sems):
    me = lax.axis_index(axis)

    def go(k, carry):
        peer = lax.rem(me + k, n)
        pltpu.make_async_remote_copy(
            src_ref=src_at(peer), dst_ref=buf.at[me], send_sem=sems[0].at[peer], recv_sem=sems[1].at[me],
            device_id={axis: peer}, device_id_type=pl.DeviceIdType.MESH,
        ).start()
        return carry

    lax.fori_loop(1, n, go, 0)


def swap_wait(axis, n, src_at, buf, sems, recv):
    me = lax.axis_index(axis)

    def go(k, carry):
        peer = lax.rem(me + k, n)
        copy = pltpu.make_async_remote_copy(
            src_ref=src_at(peer), dst_ref=buf.at[peer], send_sem=sems[0].at[peer], recv_sem=sems[1].at[peer],
            device_id={axis: peer}, device_id_type=pl.DeviceIdType.MESH,
        )
        if recv:
            copy.wait_recv()
        else:
            copy.wait_send()
        return carry

    lax.fori_loop(1, n, go, 0)


def total(v):
    return jnp.sum(jnp.sum(v, axis=1, keepdims=True), axis=0, keepdims=True)


def in_order(buf, n):
    out = buf[0]
    for s in range(1, n):
        out = out + buf[s]
    return out

N_DP = 16
N_REP = 8
SHARE = 46
EARLY = (3, 4, 5, 6, 7, 8, 9, 14, 15)
LATE = (0, 1, 2, 10, 11, 12, 13)


def share_start(shares, src, buf, sems):
    me = lax.axis_index("dp")
    for s in shares:
        @pl.when(me != s)
        def _():
            pltpu.make_async_remote_copy(
                src_ref=src.at[s], dst_ref=buf.at[me], send_sem=sems[0].at[s], recv_sem=sems[1].at[me],
                device_id={"dp": s}, device_id_type=pl.DeviceIdType.MESH,
            ).start()


def grad_pieces(par, acc, scale, late):
    if late:
        cross = acc["ar"][...]
        w_ru, w_l = par[O_RU:O_TI], par[O_L:O_TO]
        pieces = [
            (O_ENC, acc["e"][...].T),
            (O_RU, exact(cross, w_l, ((0,), (0,)))),
            (O_RD, acc["he"][64:128]),
            (O_L, acc["he"][0:64] + exact(cross, w_ru, ((1,), (0,)))),
        ]
    else:
        pieces = [
            (O_TI, acc["ti"][...]),
            (O_DB, halves(acc["db"][...])),
            (O_DT, halves(acc["dt"][...])),
            (O_TO, acc["to"][...].T),
            (O_OUT, acc["out"][...].T),
        ]
    return [(at, v * scale) for at, v in pieces]


def put_rows(ref, at, v):
    end = at + v.shape[0]
    for s in range(N_DP):
        lo, hi = max(at, SHARE * s), min(end, SHARE * s + SHARE)
        if lo < hi:
            ref[s, lo - SHARE * s : hi - SHARE * s] = v[lo - at : hi - at]


def kernel(
    x_hbm, m_hbm, cb_ref, ct_ref, p_ref, first_ref, second_ref, mom_ref, cnt_ref, ema_ref, book_ref,
    scal_out, params_out, first_out, second_out, mom_out, counts_out, sums_out, books_out,
    *scratch, R,
):
    w, keep, acc, codes, scratch = unscratch(scratch)
    (
        lacc, x_ref, m_ref, valid_own, valid_all, stat_own, stat_all, grad_own, grad_all, part_own, part_all, sums_all, step_all,
        par_share, in_sems, *sems,
    ) = scratch
    sems = [(sems[2 * i], sems[2 * i + 1]) for i in range(6)]
    sem_valid, sem_stat, sem_grad, sem_part, sem_sums, sem_step = sems
    dp = lax.axis_index("dp")
    rep = lax.axis_index("rep")
    rows = x_ref.shape[0]
    n = rows // R

    m_copy = pltpu.make_async_copy(m_hbm, m_ref, in_sems.at[0])
    x_copy = pltpu.make_async_copy(x_hbm, x_ref, in_sems.at[1])
    m_copy.start()
    x_copy.start()

    barrier = pltpu.get_barrier_semaphore()
    for axis, size, me in (("dp", N_DP, dp), ("rep", N_REP, rep)):
        def hello(k, carry):
            pl.semaphore_signal(
                barrier, inc=1, device_id={axis: lax.rem(me + k, size)}, device_id_type=pl.DeviceIdType.MESH
            )
            return carry

        lax.fori_loop(1, size, hello, 0)

    weights(p_ref[...], book_ref, w)
    code_keys(*codes[0], cb_ref, 8)
    code_keys(*codes[1], ct_ref, 2)
    for v in acc.values():
        v[...] = jnp.zeros_like(v)
    lacc[...] = jnp.zeros_like(lacc)
    for s in range(N_DP):
        par_share[s, 0:SHARE] = p_ref[SHARE * s : SHARE * s + SHARE]
        grad_own[s] = jnp.zeros((48, 128), f32)
    m_copy.wait()
    valid_own[...] = jnp.broadcast_to(total(m_ref[...].astype(f32)), (8, 128))
    valid_all[dp] = valid_own[...]
    valid_src = lambda peer: valid_own
    x_copy.wait()

    def go_forward(i, carry):
        @pl.when(i == 1)
        def _():
            pl.semaphore_wait(barrier, N_DP + N_REP - 2)
            swap_start("dp", N_DP, valid_src, valid_all, sem_valid)

        forward(i, R, x_ref, m_ref, codes, w, keep, acc, lacc)
        return carry

    lax.fori_loop(0, n, go_forward, 0)

    for d in range(N_DP):
        part_own[d] = acc["sum_b" if d < 8 else "sum_t"][8 * (d % 8) : 8 * (d % 8) + 8]
    part_src = lambda peer: part_own.at[peer]
    swap_start("dp", N_DP, part_src, part_all, sem_part)
    one = lambda v: jnp.broadcast_to(total(v), (1, 128))
    stat_own[...] = jnp.concatenate(
        [acc[name][64:65, 128 * j : 128 * j + 128] for name in ("sum_b", "sum_t") for j in range(4)]
        + [one(lacc[0:48]), one(lacc[48:112]), one(lacc[112:176]), jnp.zeros((5, 128), f32)], axis=0
    )
    stat_src = lambda peer: stat_own
    swap_start("dp", N_DP, stat_src, stat_all, sem_stat)
    part_all[dp] = part_own[dp]
    stat_all[dp] = stat_own[...]

    group_rows = rows * 8 * N_DP
    swap_wait("dp", N_DP, valid_src, valid_all, sem_valid, True)
    count = in_order(valid_all, N_DP)[0:1, 0:1]
    scale = 2.0 / count
    kb = beta_commit / (group_rows * EMB) * count
    kt = beta_commit / (group_rows // 4 * EMB) * count
    top_backward(n, R, kt, w, keep, acc)
    for at, v in grad_pieces(p_ref, acc, scale, False):
        put_rows(grad_own, at, v)
    share_start(EARLY, grad_own, grad_all, sem_grad)

    def go_backward(i, carry):
        backward(i, kb, w, keep, acc)
        return carry

    lax.fori_loop(0, n, go_backward, 0)
    for at, v in grad_pieces(p_ref, acc, scale, True):
        put_rows(grad_own, at, v)
    share_start(LATE, grad_own, grad_all, sem_grad)
    grad_src = lambda peer: grad_own.at[peer]
    grad_all[dp] = grad_own[dp]

    swap_wait("dp", N_DP, part_src, part_all, sem_part, True)
    sums_all[dp] = in_order(part_all, N_DP)
    sums_src = lambda peer: sums_all.at[dp]
    swap_start("dp", N_DP, sums_src, sums_all, sem_sums)

    swap_wait("dp", N_DP, grad_src, grad_all, sem_grad, True)
    grads = in_order(grad_all, N_DP)[0:SHARE]
    own = par_share[dp][0:SHARE]
    first_new = beta_first * first_ref[:, 0, :] + (1.0 - beta_first) * grads
    second_new = beta_second * second_ref[:, 0, :] + (1.0 - beta_second) * grads * grads
    bias_first = 1.0 - beta_first**STEP
    bias_second = 1.0 - beta_second**STEP
    step_here = inner_rate * (
        first_new / bias_first / (jnp.sqrt(second_new / bias_second) + adam_eps) + weight_decay * own
    )
    step_all[rep, 0:SHARE] = step_here
    step_all[rep, SHARE:48] = jnp.zeros((48 - SHARE, 128), f32)
    step_src = lambda peer: step_all.at[rep]
    swap_start("rep", N_REP, step_src, step_all, sem_step)
    first_out[:, 0, :] = first_new
    second_out[:, 0, :] = second_new

    swap_wait("dp", N_DP, stat_src, stat_all, sem_stat, True)
    stats = in_order(stat_all, N_DP)
    seen = jnp.concatenate([lanes([stats[4 * level + j : 4 * level + j + 1] for j in range(4)]) for level in (0, 1)], axis=0)
    counts_new = ema_decay * cnt_ref[...] + (1.0 - ema_decay) * seen
    counts_out[0] = counts_new
    totals = jnp.sum(counts_new, axis=1, keepdims=True)
    smooth = (counts_new + laplace_eps) / (totals + K * laplace_eps) * totals
    loss = stats[8:9, 0:1] / count + beta_commit * (
        stats[9:10, 0:1] / (group_rows * EMB) + stats[10:11, 0:1] / (group_rows // 4 * EMB)
    )
    scal_out[...] = jnp.concatenate([jnp.broadcast_to(loss, (1, 128)), jnp.broadcast_to(count, (1, 128)), jnp.zeros((6, 128), f32)], axis=0)

    swap_wait("dp", N_DP, sums_src, sums_all, sem_sums, True)
    for level in (0, 1):
        inverse = 1.0 / smooth[level : level + 1]
        for j in range(8):
            rows_j = slice(8 * j, 8 * j + 8)
            sums_new = ema_decay * ema_ref[level, rows_j] + (1.0 - ema_decay) * sums_all[8 * level + j]
            sums_out[0, level, rows_j] = sums_new
            books_out[0, level, rows_j] = sums_new * inverse

    swap_wait("rep", N_REP, step_src, step_all, sem_step, True)
    mean_delta = in_order(step_all, N_REP)[0:SHARE] * (1.0 / N_REP)
    momentum_new = outer_moment * mom_ref[...] + mean_delta
    mom_out[...] = momentum_new
    params_out[...] = own - outer_rate * (mean_delta + outer_moment * momentum_new)

    for axis, size, src, buf, sem in (
        ("dp", N_DP, valid_src, valid_all, sem_valid), ("dp", N_DP, grad_src, grad_all, sem_grad),
        ("dp", N_DP, part_src, part_all, sem_part), ("dp", N_DP, stat_src, stat_all, sem_stat),
        ("rep", N_REP, step_src, step_all, sem_step), ("dp", N_DP, sums_src, sums_all, sem_sums),
    ):
        swap_wait(axis, size, src, buf, sem, False)


def hand_over(scal, *refs):
    n = (len(refs) - 3) // 2
    ins, (loss_out, valid_out), outs, sems = refs[:n], refs[n : n + 2], refs[n + 2 : -1], refs[-1]
    copies = [pltpu.make_async_copy(a, b, sems.at[i]) for i, (a, b) in enumerate(zip(ins, outs))]
    for c in copies:
        c.start()
    loss_out[0] = scal[0, 0]
    valid_out[0] = scal[1, 0]
    for c in copies:
        c.wait()


def shards(
    pixels, valid_mask, bottom_codes, top_codes, params, first_moment, second_moment, outer_momentum, ema_counts,
    ema_sums, codebooks, *, R,
):
    rows = pixels.shape[0]
    vm = pl.BlockSpec(memory_space=pltpu.VMEM)
    sm = pl.BlockSpec(memory_space=pltpu.SMEM)
    hbm = pl.BlockSpec(memory_space=pl.ANY)
    dma = pltpu.SemaphoreType.DMA
    results = [(SHARE, 128), (SHARE, 1, 128), (SHARE, 1, 128), (SHARE, 128), (1, 2, K), (1, 2, EMB, K), (1, 2, EMB, K)]
    inner = pl.pallas_call(
        functools.partial(kernel, R=R),
        out_shape=tuple(pltpu.VMEM(s, f32) for s in [(8, 128)] + results),
        in_specs=[hbm] * 2 + [vm] * 9,
        out_specs=(vm,) * 8,
        scratch_shapes=scratches(rows, R)
        + [
            pltpu.VMEM((rows, 384), f32), pltpu.VMEM((rows, 384), jnp.int32),
            pltpu.VMEM((8, 128), f32), pltpu.VMEM((N_DP, 8, 128), f32),
            pltpu.VMEM((16, 128), f32), pltpu.VMEM((N_DP, 16, 128), f32),
            pltpu.VMEM((N_DP, 48, 128), f32), pltpu.VMEM((N_DP, 48, 128), f32),
            pltpu.VMEM((N_DP, 8, 512), f32), pltpu.VMEM((N_DP, 8, 512), f32), pltpu.VMEM((N_DP, 8, 512), f32),
            pltpu.VMEM((N_REP, 48, 128), f32), pltpu.VMEM((N_DP, 48, 128), f32), dma((2,)),
        ]
        + [dma((N_DP,))] * 10 + [dma((N_REP,))] * 2,
        compiler_params=pltpu.CompilerParams(
            vmem_limit_bytes=60 * 2**20, collective_id=0, has_side_effects=True
        ),
    )(
        pixels, valid_mask, bottom_codes.reshape(-1, 128), top_codes.reshape(-1, 128), params,
        jnp.swapaxes(first_moment, 0, 1), jnp.swapaxes(second_moment, 0, 1), outer_momentum, ema_counts,
        jnp.swapaxes(ema_sums, 1, 2), jnp.swapaxes(codebooks, 1, 2),
    )
    shape = lambda *s: jax.ShapeDtypeStruct(s, f32)
    loss, valid, params, first, second, mom, counts, sums, books = pl.pallas_call(
        hand_over,
        out_shape=(shape(1), shape(1)) + tuple(shape(*s) for s in results),
        in_specs=[vm] * 8,
        out_specs=(sm, sm) + (hbm,) * 7,
        scratch_shapes=[dma((7,))],
    )(*(pltpu.with_memory_space_constraint(v, pltpu.VMEM) for v in inner))
    return (
        loss, valid, params, jnp.swapaxes(first, 0, 1), jnp.swapaxes(second, 0, 1), mom, counts,
        jnp.swapaxes(sums, 2, 3), jnp.swapaxes(books, 2, 3),
    )


def solution(mesh):
    return jax.shard_map(
        functools.partial(shards, R=256),
        mesh=mesh,
        in_specs=(
            P(("rep", "dp"), None),
            P(("rep", "dp"), None),
            P(("rep", "dp")),
            P(("rep", "dp")),
            P(),
            P("rep", "dp", None),
            P("rep", "dp", None),
            P("dp", None),
            P(),
            P(),
            P(),
        ),
        out_specs=(
            P("rep"),
            P("rep"),
            P("dp", None),
            P("rep", "dp", None),
            P("rep", "dp", None),
            P("dp", None),
            P("rep", None, None),
            P("rep", None, None, None),
            P("rep", None, None, None),
        ),
        check_vma=False,
    )
```

```python
import functools
import jax
import jax.numpy as jnp
from jax import lax
from jax.experimental import pallas as pl
from jax.experimental.pallas import tpu as pltpu
from jax.sharding import PartitionSpec as P

PF = 48
EMB = 64
K = 512
STEP = 10
beta_commit = 0.25
ema_decay = 0.8
laplace_eps = 1e-05
inner_rate = 0.03
beta_first = 0.9
beta_second = 0.999
adam_eps = 1e-08
weight_decay = 0.01
outer_rate = 0.7
outer_moment = 0.9

bf16 = jnp.bfloat16
f32 = jnp.float32
O_ENC, O_RU, O_TI, O_DB, O_DT, O_RD, O_L, O_TO, O_OUT, O_END = 0, 48, 112, 368, 432, 496, 560, 624, 688, 736


def nn(a, b):
    return lax.dot_general(a, b, (((1,), (0,)), ((), ())), preferred_element_type=f32)


def nt(a, b):
    return lax.dot_general(a, b, (((1,), (1,)), ((), ())), preferred_element_type=f32)


def tn(a, b):
    return lax.dot_general(a, b, (((0,), (0,)), ((), ())), preferred_element_type=f32)


def split(v):
    hi = v.astype(bf16)
    return hi, (v - hi.astype(f32)).astype(bf16)


def pair(v):
    hi, lo = split(v)
    return jnp.concatenate([hi, lo], axis=1)


def quad(v):
    hi, lo = split(v)
    return jnp.concatenate([hi, hi, lo, lo], axis=1)


def twice(v):
    return jnp.concatenate([v, v], axis=0)


def silu_and_slope(u):
    w = 1.0 + jnp.tanh(u)
    a = u * w
    return a, w + a * (2.0 - w)


def lanes(parts):
    return jnp.concatenate(parts, axis=1)


def spread_codes(codes, per_row):
    a = codes.shape[0]
    rows = a * 128 // per_row
    span = 128 // per_row
    lo = (codes & 255).astype(f32).astype(bf16)
    hi = (codes >> 8).astype(f32).astype(bf16)
    up = (lax.broadcasted_iota(jnp.int32, (a, rows), 0) == lax.broadcasted_iota(jnp.int32, (a, rows), 1) // span)
    up = up.astype(f32).astype(bf16)
    keep = (
        lax.broadcasted_iota(jnp.int32, (128, rows), 0) // per_row
        == lax.broadcasted_iota(jnp.int32, (128, rows), 1) % span
    )
    pick = (
        lax.broadcasted_iota(jnp.int32, (8, 128), 0)
        == lax.broadcasted_iota(jnp.int32, (8, 128), 1) % per_row
    )
    pick = pick.astype(f32).astype(bf16)
    out = []
    for part in (lo, hi):
        wide = jnp.where(keep, tn(part, up), 0.0).astype(bf16)
        out.append(nn(pick, wide))
    return out


def stack(v):
    hi, lo = split(v)
    return jnp.concatenate([hi, lo], axis=0)


def halves(v):
    n = v.shape[0] // 2
    return v[:n] + v[n:]


def exact(a, b, dims):
    return lax.dot_general(a, b, ((dims), ((), ())), precision=lax.Precision.HIGHEST, preferred_element_type=f32)


WS = {
    "enc_f": (128, 96), "rd_f": (128, 128), "l_f": (128, 192), "ti_f": (128, 512), "to_f": (128, 128), "db_f": (128, 256),
    "dt_f": (128, 256), "out_f": (96, 128), "out_b": (128, 96), "db_b": (128, 128), "dt_b": (128, 128), "to_b": (128, 128),
    "ti_b": (256, 256), "ru_b": (64, 128), "he_b": (128, 256), "book_b": (256, 256), "book_t": (256, 256),
}
KEEP = {
    "x": (48, 8, f32), "xb": (48, 8, bf16), "he": (128, 8, bf16), "de": (128, 8, bf16), "ar": (64, 8, bf16), "dr": (64, 8, bf16),
    "gap_b": (64, 8, bf16), "gl": (64, 8, f32), "both": (128, 8, bf16),
}
KEEP_TOP = {
    "ti": (256, bf16), "ht": (128, bf16), "dt": (128, bf16), "gap_t": (64, f32), "gt": (64, f32),
}
ACC = {
    "e": (128, 48), "he": (128, 128), "ar": (64, 64), "ti": (256, 128), "to": (128, 64), "db": (128, 128), "dt": (128, 128),
    "out": (128, 48), "sum_b": (144, 256), "sum_t": (144, 256),
}


def weights(par, book_ref, w):
    part = par.T
    f = lambda lo, hi: par[lo:hi]
    t = lambda lo, hi: part[:, lo:hi]
    cross = exact(f(O_L, O_TO), f(O_RU, O_TI), ((1,), (1,)))
    w["enc_f"][...] = pair(0.5 * t(O_ENC, O_RU))
    w["rd_f"][...] = stack(0.5 * f(O_RD, O_L))
    w["l_f"][...] = stack(lanes([f(O_L, O_TO), cross]))
    w["ti_f"][...] = pair(0.5 * t(O_TI, O_DB))
    w["to_f"][...] = stack(f(O_TO, O_OUT))
    w["db_f"][...] = quad(0.5 * t(O_DB, O_DT))
    w["dt_f"][...] = quad(0.5 * t(O_DT, O_RD))
    w["out_f"][...] = stack(f(O_OUT, O_END))
    w["out_b"][...] = pair(0.5 * t(O_OUT, O_END))
    w["db_b"][...] = stack(f(O_DB, O_DT))
    w["dt_b"][...] = stack(f(O_DT, O_RD))
    w["to_b"][...] = pair(0.5 * t(O_TO, O_OUT))
    w["ti_b"][...] = pair(f(O_TI, O_DB))
    w["ru_b"][...] = pair(0.5 * exact(f(O_RU, O_TI), f(O_L, O_TO), ((1,), (1,))))
    w["he_b"][...] = pair(0.5 * lanes([t(O_L, O_TO), t(O_RD, O_L)]))
    for level, name in enumerate(("book_b", "book_t")):
        w[name][...] = jnp.concatenate([stack(book_ref[level][:, 256 * a : 256 * a + 256]) for a in (0, 1)], axis=0)


def code_keys(rows_ref, cols_ref, src, per):
    lo, hi = spread_codes(src[...], per)
    rows_ref[0] = lo
    rows_ref[1] = hi
    cols_ref[...] = lo.T


def high_bits(codes, level, n, at, R):
    return lanes([codes[level][0][1, p : p + 1, pl.ds(at, R)] for p in range(n)])


def first(i, size):
    return i * size if isinstance(i, int) else pl.multiple_of(i * size, size)


def hot(equal):
    return jnp.where(equal, jnp.ones((), bf16), jnp.zeros((), bf16))


def encoder(i, R, x_ref, codes, w, keep, acc):
    along = lax.broadcasted_iota(jnp.int32, (R, 256), 1).astype(f32).astype(bf16)
    at = first(i, R)
    tops = pl.ds(first(i, 2 * R), 2 * R)

    def scatter(level, n, latent):
        key = codes[level][1][pl.ds(at, R), :]
        low = jnp.concatenate([
            hot(along == jnp.broadcast_to(key[:, p : p + 1], (R, 256)).astype(bf16)) for p in range(n)
        ], axis=0)
        high = high_bits(codes, level, n, at, R).astype(bf16)
        ones = jnp.broadcast_to(high, latent.shape) * latent
        row = lax.broadcasted_iota(jnp.int32, (16, n * R), 0)
        count = jnp.where(row == 0, 1.0 - high.astype(f32), jnp.where(row == 1, high.astype(f32), 0.0)).astype(bf16)
        return nn(jnp.concatenate([latent - ones, ones, count], axis=0), low)

    xt = x_ref[pl.ds(at, R), :].T
    x = lanes([xt[48 * p : 48 * p + 48] for p in range(8)])
    keep["x"][i] = x
    xb = x.astype(bf16)
    keep["xb"][i] = xb
    he, de = silu_and_slope(nn(w["enc_f"][...], twice(xb)))
    heb = he.astype(bf16)
    keep["he"][i] = heb
    keep["de"][i] = de.astype(bf16)
    ar, dr = silu_and_slope(halves(nn(w["rd_f"][...], heb)))
    arb = ar.astype(bf16)
    keep["ar"][i] = arb
    keep["dr"][i] = dr.astype(bf16)
    lbb = halves(nn(w["l_f"][...], jnp.concatenate([heb, arb], axis=0))).astype(bf16)
    ti = lanes([
        jnp.concatenate([lbb[:, R * p : R * p + R] for p in range(4 * g, 4 * g + 4)], axis=0) for g in (0, 1)
    ])
    keep["ti"][:, tops] = ti
    ht, dt = silu_and_slope(nn(w["ti_f"][...], twice(ti)))
    htb = ht.astype(bf16)
    keep["ht"][:, tops] = htb
    keep["dt"][:, tops] = dt.astype(bf16)
    lt = halves(nn(w["to_f"][...], htb))
    keep["gap_t"][:, tops] = lt
    acc["sum_b"][...] += scatter(0, 8, lbb)
    acc["sum_t"][...] += scatter(1, 2, lt.astype(bf16))


def decoder(i, R, m_ref, codes, w, keep, acc, lacc):
    down = lax.broadcasted_iota(jnp.int32, (256, R), 0).astype(f32).astype(bf16)
    at = first(i, R)
    tops = pl.ds(first(i, 2 * R), 2 * R)

    def gather(level, n, book):
        key = codes[level][0][0, :, pl.ds(at, R)]
        low = lanes([hot(down == key[p : p + 1, :].astype(bf16)) for p in range(n)])
        both = nn(book, low)
        return jnp.where(high_bits(codes, level, n, at, R) > 0.5, both[128:], both[:128]).astype(bf16)

    mt = m_ref[pl.ds(at, R), :].astype(f32).T
    m = lanes([mt[48 * p : 48 * p + 48] for p in range(8)])
    qb2 = gather(0, 8, w["book_b"][...])
    qt2 = gather(1, 2, w["book_t"][...])
    ti = keep["ti"][:, tops]
    lb = lanes([ti[64 * (p % 4) : 64 * (p % 4) + 64, R * (p // 4) : R * (p // 4) + R] for p in range(8)]).astype(f32)
    gap_b = lb - halves(qb2.astype(f32))
    gap_t = keep["gap_t"][:, tops] - halves(qt2.astype(f32))
    keep["gap_b"][i] = gap_b.astype(bf16)
    keep["gap_t"][:, tops] = gap_t
    top = nn(w["dt_f"][...], twice(qt2))
    pre = nn(w["db_f"][...], twice(qb2)) + lanes([top[:, R * (p // 4) : R * (p // 4) + R] for p in range(8)])
    hd, dd = silu_and_slope(pre)
    hdb = hd.astype(bf16)
    err = halves(nn(w["out_f"][...], hdb)) - keep["x"][i]
    me = m * err
    lacc[0:48] += sum((me * err)[:, R * p : R * p + R] for p in range(8))
    lacc[48:112] += sum((gap_b * gap_b)[:, R * p : R * p + R] for p in range(8))
    lacc[112:176] += sum((gap_t * gap_t)[:, R * p : R * p + R] for p in range(2))
    grb = me.astype(bf16)
    acc["out"][...] += nt(hdb, grb)
    gpd = nn(w["out_b"][...], twice(grb)) * dd
    gpdb = gpd.astype(bf16)
    acc["db"][...] += nt(qb2, gpdb)
    gtrb = lanes([sum(gpd[:, R * p : R * p + R] for p in range(4 * g_, 4 * g_ + 4)) for g_ in (0, 1)]).astype(bf16)
    acc["dt"][...] += nt(qt2, gtrb)
    keep["gt"][:, tops] = halves(nn(w["dt_b"][...], gtrb))
    keep["gl"][i] = halves(nn(w["db_b"][...], gpdb))


def top_backward(n, R, kt, w, keep, acc):
    gltb = (keep["gt"][...] + kt * keep["gap_t"][...]).astype(bf16)
    acc["to"][...] = nt(keep["ht"][...], gltb)
    gptb = (nn(w["to_b"][...], twice(gltb)) * keep["dt"][...].astype(f32)).astype(bf16)
    acc["ti"][...] = nt(keep["ti"][...], gptb)
    gti = nn(w["ti_b"][...], twice(gptb))
    for i in range(n):
        for p in range(8):
            at = 2 * R * i + R * (p // 4)
            keep["gl"][i, :, R * p : R * p + R] += gti[64 * (p % 4) : 64 * (p % 4) + 64, at : at + R]


def backward_inner(i, kb, w, keep, acc):
    glbb = (keep["gl"][i] + kb * keep["gap_b"][i].astype(f32)).astype(bf16)
    gprb = (nn(w["ru_b"][...], twice(glbb)) * keep["dr"][i].astype(f32)).astype(bf16)
    both = jnp.concatenate([glbb, gprb], axis=0)
    keep["both"][i] = both
    acc["he"][...] += nt(both, keep["he"][i])
    acc["ar"][...] += nt(glbb, keep["ar"][i])


def backward_outer(i, w, keep, acc):
    gpeb = (nn(w["he_b"][...], twice(keep["both"][i])) * keep["de"][i].astype(f32)).astype(bf16)
    acc["e"][...] += nt(gpeb, keep["xb"][i])


def scratches(rows, R):
    return (
        [pltpu.VMEM(s, bf16) for s in WS.values()]
        + [pltpu.VMEM((rows // R, c, n * R), t) for c, n, t in KEEP.values()]
        + [pltpu.VMEM((c, rows * 2), t) for c, t in KEEP_TOP.values()]
        + [pltpu.VMEM(s, f32) for s in ACC.values()]
        + [pltpu.VMEM((2, 8, rows), f32), pltpu.VMEM((rows, 8), f32)] * 2
        + [pltpu.VMEM((176, R), f32)]
    )


def unscratch(scratch):
    scratch = list(scratch)
    take = lambda names: {k: scratch.pop(0) for k in names}
    w, keep, acc = take(WS), take(list(KEEP) + list(KEEP_TOP)), take(ACC)
    codes = ((scratch.pop(0), scratch.pop(0)), (scratch.pop(0), scratch.pop(0)))
    return w, keep, acc, codes, scratch


def swap_start(axis, n, src_at, buf, sems):
    me = lax.axis_index(axis)

    def go(k, carry):
        peer = lax.rem(me + k, n)
        pltpu.make_async_remote_copy(
            src_ref=src_at(peer), dst_ref=buf.at[me], send_sem=sems[0], recv_sem=sems[1],
            device_id={axis: peer}, device_id_type=pl.DeviceIdType.MESH,
        ).start()
        return carry

    lax.fori_loop(1, n, go, 0)


def swap_wait(axis, n, buf, sems, recv):
    others = buf.at[0 : n - 1]
    copy = pltpu.make_async_remote_copy(
        src_ref=others, dst_ref=others, send_sem=sems[0], recv_sem=sems[1],
        device_id={axis: lax.axis_index(axis)}, device_id_type=pl.DeviceIdType.MESH,
    )
    if recv:
        copy.wait_recv()
    else:
        copy.wait_send()


def total(v):
    return jnp.sum(jnp.sum(v, axis=0, keepdims=True), axis=1, keepdims=True)


def in_order(buf, n):
    out = buf[0]
    for s in range(1, n):
        out = out + buf[s]
    return out

N_DP = 16
N_REP = 8
SHARE = 46
AFTER_DECODER = (8, 9, 15)
AFTER_TOP = (3, 4, 5, 6, 7, 14)
AFTER_INNER = (2, 10, 11, 12, 13)
AFTER_OUTER = (0, 1)


def share_start(shares, src, buf, sems):
    me = lax.axis_index("dp")
    for s in shares:
        @pl.when(me != s)
        def _():
            pltpu.make_async_remote_copy(
                src_ref=src.at[s], dst_ref=buf.at[me], send_sem=sems[0], recv_sem=sems[1],
                device_id={"dp": s}, device_id_type=pl.DeviceIdType.MESH,
            ).start()


def put_rows(ref, at, v):
    end = at + v.shape[0]
    for s in range(N_DP):
        lo, hi = max(at, SHARE * s), min(end, SHARE * s + SHARE)
        if lo < hi:
            ref[s, lo - SHARE * s : hi - SHARE * s] = v[lo - at : hi - at]


def each(n, f):
    if n == 1:
        f(0)
        return

    def go(i, carry):
        f(i)
        return carry

    lax.fori_loop(0, n, go, 0)


def kernel(*refs, R):
    sources, refs = refs[:11], refs[11:]
    (scal_out, params_out, first_out, second_out, mom_out, counts_out, sums_out, books_out), scratch = refs[:8], refs[8:]
    inputs, scratch = scratch[:11], scratch[11:]
    x_ref, m_ref, cb_ref, ct_ref, p_ref, first_ref, second_ref, mom_ref, cnt_ref, ema_ref, book_ref = inputs
    w, keep, acc, codes, scratch = unscratch(scratch)
    (
        lacc, valid_own, valid_all, stat_own, stat_all, grad_own, grad_all, part_own, part_all, sums_all, step_all,
        par_share, in_sems, *sems,
    ) = scratch
    loads = [pltpu.make_async_copy(a, b, in_sems.at[i]) for i, (a, b) in enumerate(zip(sources, inputs))]
    load_x, load_m, load_cb, load_ct, load_p, *load_rest, load_book = loads
    for load in (load_p, load_x, load_cb, load_ct, load_book, load_m, *load_rest):
        load.start()
    sems = [(sems[2 * i], sems[2 * i + 1]) for i in range(6)]
    sem_valid, sem_stat, sem_grad, sem_part, sem_sums, sem_step = sems
    dp = lax.axis_index("dp")
    rep = lax.axis_index("rep")
    rows = x_ref.shape[0]
    n = rows // R

    barrier = pltpu.get_barrier_semaphore()
    for axis, size, me in (("dp", N_DP, dp), ("rep", N_REP, rep)):
        def hello(k, carry):
            pl.semaphore_signal(
                barrier, inc=1, device_id={axis: lax.rem(me + k, size)}, device_id_type=pl.DeviceIdType.MESH
            )
            return carry

        lax.fori_loop(1, size, hello, 0)

    for load in (load_p, load_x, load_cb, load_ct, load_book):
        load.wait()
    weights(p_ref[...], book_ref, w)
    code_keys(*codes[0], cb_ref, 8)
    code_keys(*codes[1], ct_ref, 2)
    for v in acc.values():
        v[...] = jnp.zeros_like(v)
    lacc[...] = jnp.zeros_like(lacc)
    for s in range(N_DP):
        par_share[s, 0:SHARE] = p_ref[SHARE * s : SHARE * s + SHARE]
        grad_own[s] = jnp.zeros((48, 128), f32)
    each(n, lambda i: encoder(i, R, x_ref, codes, w, keep, acc))

    load_m.wait()
    valid_own[...] = jnp.broadcast_to(total(m_ref[...].astype(f32)), (8, 128))
    valid_all[dp] = valid_own[...]
    valid_src = lambda peer: valid_own
    pl.semaphore_wait(barrier, N_DP + N_REP - 2)
    swap_start("dp", N_DP, valid_src, valid_all, sem_valid)

    for d in range(N_DP):
        name, at = ("sum_b", "sum_t")[d // 8], 8 * (d % 8)
        part_own[d] = lanes([acc[name][at : at + 8], acc[name][64 + at : 72 + at]])
    part_src = lambda peer: part_own.at[peer]
    swap_start("dp", N_DP, part_src, part_all, sem_part)
    stat_own[...] = jnp.concatenate(
        [
            acc[name][128 + a : 129 + a, 128 * j : 128 * j + 128]
            for name in ("sum_b", "sum_t") for a in (0, 1) for j in (0, 1)
        ], axis=0
    )
    stat_src = lambda peer: stat_own
    swap_start("dp", N_DP, stat_src, stat_all, sem_stat)
    part_all[dp] = part_own[dp]
    stat_all[dp] = stat_own[...]

    each(n, lambda i: decoder(i, R, m_ref, codes, w, keep, acc, lacc))

    group_rows = rows * 8 * N_DP
    swap_wait("dp", N_DP, valid_all, sem_valid, True)
    count = in_order(valid_all, N_DP)[0:1, 0:1]
    scale = 2.0 / count
    kb = beta_commit / (group_rows * EMB) * count
    kt = beta_commit / (group_rows // 4 * EMB) * count
    lane = lax.broadcasted_iota(jnp.int32, (1, 128), 1)
    losses = jnp.where(lane == 0, total(lacc[0:48]), jnp.where(lane == 1, total(lacc[48:112]), total(lacc[112:176])))
    for s in range(N_DP):
        grad_own[s, SHARE : SHARE + 1] = losses
    put_rows(grad_own, O_DB, halves(acc["db"][...]) * scale)
    put_rows(grad_own, O_DT, halves(acc["dt"][...]) * scale)
    put_rows(grad_own, O_OUT, acc["out"][...].T * scale)
    share_start(AFTER_DECODER, grad_own, grad_all, sem_grad)

    top_backward(n, R, kt, w, keep, acc)
    put_rows(grad_own, O_TI, acc["ti"][...] * scale)
    put_rows(grad_own, O_TO, acc["to"][...].T * scale)
    share_start(AFTER_TOP, grad_own, grad_all, sem_grad)

    each(n, lambda i: backward_inner(i, kb, w, keep, acc))
    cross = acc["ar"][...]
    put_rows(grad_own, O_RU, exact(cross, p_ref[O_L:O_TO], ((0,), (0,))) * scale)
    put_rows(grad_own, O_RD, acc["he"][64:128] * scale)
    put_rows(grad_own, O_L, (acc["he"][0:64] + exact(cross, p_ref[O_RU:O_TI], ((1,), (0,)))) * scale)
    share_start(AFTER_INNER, grad_own, grad_all, sem_grad)

    each(n, lambda i: backward_outer(i, w, keep, acc))
    put_rows(grad_own, O_ENC, acc["e"][...].T * scale)
    share_start(AFTER_OUTER, grad_own, grad_all, sem_grad)
    grad_all[dp] = grad_own[dp]

    for load in load_rest:
        load.wait()
    swap_wait("dp", N_DP, grad_all, sem_grad, True)
    summed = in_order(grad_all, N_DP)
    grads = summed[0:SHARE]
    own = par_share[dp][0:SHARE]
    first_new = beta_first * first_ref[:, 0, :] + (1.0 - beta_first) * grads
    second_new = beta_second * second_ref[:, 0, :] + (1.0 - beta_second) * grads * grads
    bias_first = 1.0 - beta_first**STEP
    bias_second = 1.0 - beta_second**STEP
    step_here = inner_rate * (
        first_new / bias_first / (jnp.sqrt(second_new / bias_second) + adam_eps) + weight_decay * own
    )
    step_all[rep, 0:SHARE] = step_here
    step_all[rep, SHARE:48] = jnp.zeros((48 - SHARE, 128), f32)
    step_src = lambda peer: step_all.at[rep]
    swap_start("rep", N_REP, step_src, step_all, sem_step)
    swap_wait("dp", N_DP, part_all, sem_part, True)
    sums_all[dp] = in_order(part_all, N_DP)
    sums_src = lambda peer: sums_all.at[dp]
    swap_start("dp", N_DP, sums_src, sums_all, sem_sums)

    first_out[:, 0, :] = first_new
    second_out[:, 0, :] = second_new

    swap_wait("dp", N_DP, stat_all, sem_stat, True)
    stats = in_order(stat_all, N_DP)
    seen = jnp.concatenate([lanes([stats[4 * level + j : 4 * level + j + 1] for j in range(4)]) for level in (0, 1)], axis=0)
    counts_new = ema_decay * cnt_ref[...] + (1.0 - ema_decay) * seen
    counts_out[0] = counts_new
    totals = jnp.sum(counts_new, axis=1, keepdims=True)
    smooth = (counts_new + laplace_eps) / (totals + K * laplace_eps) * totals
    terms = summed[SHARE : SHARE + 1]
    loss = terms[:, 0:1] / count + beta_commit * (
        terms[:, 1:2] / (group_rows * EMB) + terms[:, 2:3] / (group_rows // 4 * EMB)
    )
    scal_out[...] = jnp.concatenate([jnp.broadcast_to(loss, (1, 128)), jnp.broadcast_to(count, (1, 128)), jnp.zeros((6, 128), f32)], axis=0)

    swap_wait("dp", N_DP, sums_all, sem_sums, True)
    for level in (0, 1):
        inverse = 1.0 / smooth[level : level + 1]
        for j in range(8):
            rows_j = slice(8 * j, 8 * j + 8)
            sums_new = ema_decay * ema_ref[level, rows_j] + (1.0 - ema_decay) * sums_all[8 * level + j]
            sums_out[0, level, rows_j] = sums_new
            books_out[0, level, rows_j] = sums_new * inverse

    swap_wait("rep", N_REP, step_all, sem_step, True)
    mean_delta = in_order(step_all, N_REP)[0:SHARE] * (1.0 / N_REP)
    momentum_new = outer_moment * mom_ref[...] + mean_delta
    mom_out[...] = momentum_new
    params_out[...] = own - outer_rate * (mean_delta + outer_moment * momentum_new)

    for axis, size, buf, sem in (
        ("dp", N_DP, valid_all, sem_valid), ("dp", N_DP, grad_all, sem_grad), ("dp", N_DP, part_all, sem_part),
        ("dp", N_DP, stat_all, sem_stat), ("rep", N_REP, step_all, sem_step), ("dp", N_DP, sums_all, sem_sums),
    ):
        swap_wait(axis, size, buf, sem, False)


def hand_over(scal, *refs):
    n = (len(refs) - 3) // 2
    ins, (loss_out, valid_out), outs, sems = refs[:n], refs[n : n + 2], refs[n + 2 : -1], refs[-1]
    copies = [pltpu.make_async_copy(a, b, sems.at[i]) for i, (a, b) in enumerate(zip(ins, outs))]
    for c in copies:
        c.start()
    loss_out[0] = scal[0, 0]
    valid_out[0] = scal[1, 0]
    for c in copies:
        c.wait()


def shards(
    pixels, valid_mask, bottom_codes, top_codes, params, first_moment, second_moment, outer_momentum, ema_counts,
    ema_sums, codebooks, *, R,
):
    rows = pixels.shape[0]
    vm = pl.BlockSpec(memory_space=pltpu.VMEM)
    sm = pl.BlockSpec(memory_space=pltpu.SMEM)
    hbm = pl.BlockSpec(memory_space=pl.ANY)
    dma = pltpu.SemaphoreType.DMA
    args = (
        pixels, valid_mask, bottom_codes.reshape(-1, 128), top_codes.reshape(-1, 128), params,
        jnp.swapaxes(first_moment, 0, 1), jnp.swapaxes(second_moment, 0, 1), outer_momentum, ema_counts,
        jnp.swapaxes(ema_sums, 1, 2), jnp.swapaxes(codebooks, 1, 2),
    )
    results = [(SHARE, 128), (SHARE, 1, 128), (SHARE, 1, 128), (SHARE, 128), (1, 2, K), (1, 2, EMB, K), (1, 2, EMB, K)]
    inner = pl.pallas_call(
        functools.partial(kernel, R=R),
        out_shape=tuple(pltpu.VMEM(s, f32) for s in [(8, 128)] + results),
        in_specs=[hbm] * 11,
        out_specs=(vm,) * 8,
        scratch_shapes=[pltpu.VMEM(v.shape, v.dtype) for v in args]
        + scratches(rows, R)
        + [
            pltpu.VMEM((8, 128), f32), pltpu.VMEM((N_DP, 8, 128), f32),
            pltpu.VMEM((8, 128), f32), pltpu.VMEM((N_DP, 8, 128), f32),
            pltpu.VMEM((N_DP, 48, 128), f32), pltpu.VMEM((N_DP, 48, 128), f32),
            pltpu.VMEM((N_DP, 8, 512), f32), pltpu.VMEM((N_DP, 8, 512), f32), pltpu.VMEM((N_DP, 8, 512), f32),
            pltpu.VMEM((N_REP, 48, 128), f32), pltpu.VMEM((N_DP, 48, 128), f32), dma((11,)),
        ]
        + [dma] * 12,
        compiler_params=pltpu.CompilerParams(
            vmem_limit_bytes=60 * 2**20, collective_id=0, has_side_effects=True
        ),
    )(*args)
    shape = lambda *s: jax.ShapeDtypeStruct(s, f32)
    loss, valid, params, first, second, mom, counts, sums, books = pl.pallas_call(
        hand_over,
        out_shape=(shape(1), shape(1)) + tuple(shape(*s) for s in results),
        in_specs=[vm] * 8,
        out_specs=(sm, sm) + (hbm,) * 7,
        scratch_shapes=[dma((7,))],
    )(*(pltpu.with_memory_space_constraint(v, pltpu.VMEM) for v in inner))
    return (
        loss, valid, params, jnp.swapaxes(first, 0, 1), jnp.swapaxes(second, 0, 1), mom, counts,
        jnp.swapaxes(sums, 2, 3), jnp.swapaxes(books, 2, 3),
    )


def solution(mesh):
    return jax.shard_map(
        functools.partial(shards, R=1024),
        mesh=mesh,
        in_specs=(
            P(("rep", "dp"), None),
            P(("rep", "dp"), None),
            P(("rep", "dp")),
            P(("rep", "dp")),
            P(),
            P("rep", "dp", None),
            P("rep", "dp", None),
            P("dp", None),
            P(),
            P(),
            P(),
        ),
        out_specs=(
            P("rep"),
            P("rep"),
            P("dp", None),
            P("rep", "dp", None),
            P("rep", "dp", None),
            P("dp", None),
            P("rep", None, None),
            P("rep", None, None, None),
            P("rep", None, None, None),
        ),
        check_vma=False,
    )
```

```python
import functools
import jax
import jax.numpy as jnp
from jax import lax
from jax.experimental import pallas as pl
from jax.experimental.pallas import tpu as pltpu
from jax.sharding import PartitionSpec as P

PF = 48
EMB = 64
K = 512
STEP = 10
beta_commit = 0.25
ema_decay = 0.8
laplace_eps = 1e-05
inner_rate = 0.03
beta_first = 0.9
beta_second = 0.999
adam_eps = 1e-08
weight_decay = 0.01
outer_rate = 0.7
outer_moment = 0.9

bf16 = jnp.bfloat16
f32 = jnp.float32
O_ENC, O_RU, O_TI, O_DB, O_DT, O_RD, O_L, O_TO, O_OUT, O_END = 0, 48, 112, 368, 432, 496, 560, 624, 688, 736


def nn(a, b):
    return lax.dot_general(a, b, (((1,), (0,)), ((), ())), preferred_element_type=f32)


def nt(a, b):
    return lax.dot_general(a, b, (((1,), (1,)), ((), ())), preferred_element_type=f32)


def tn(a, b):
    return lax.dot_general(a, b, (((0,), (0,)), ((), ())), preferred_element_type=f32)


def split(v):
    hi = v.astype(bf16)
    return hi, (v - hi.astype(f32)).astype(bf16)


def pair(v):
    hi, lo = split(v)
    return jnp.concatenate([hi, lo], axis=1)


def quad(v):
    hi, lo = split(v)
    return jnp.concatenate([hi, hi, lo, lo], axis=1)


def twice(v):
    return jnp.concatenate([v, v], axis=0)


def silu_and_slope(u):
    w = 1.0 + jnp.tanh(u)
    a = u * w
    return a, w + a * (2.0 - w)


def lanes(parts):
    return jnp.concatenate(parts, axis=1)


def spread_codes(codes, per_row):
    a = codes.shape[0]
    rows = a * 128 // per_row
    span = 128 // per_row
    lo = (codes & 255).astype(f32).astype(bf16)
    hi = (codes >> 8).astype(f32).astype(bf16)
    up = (lax.broadcasted_iota(jnp.int32, (a, rows), 0) == lax.broadcasted_iota(jnp.int32, (a, rows), 1) // span)
    up = up.astype(f32).astype(bf16)
    keep = (
        lax.broadcasted_iota(jnp.int32, (128, rows), 0) // per_row
        == lax.broadcasted_iota(jnp.int32, (128, rows), 1) % span
    )
    pick = (
        lax.broadcasted_iota(jnp.int32, (8, 128), 0)
        == lax.broadcasted_iota(jnp.int32, (8, 128), 1) % per_row
    )
    pick = pick.astype(f32).astype(bf16)
    out = []
    for part in (lo, hi):
        wide = jnp.where(keep, tn(part, up), 0.0).astype(bf16)
        out.append(nn(pick, wide))
    return out


def stack(v):
    hi, lo = split(v)
    return jnp.concatenate([hi, lo], axis=0)


def halves(v):
    n = v.shape[0] // 2
    return v[:n] + v[n:]


def exact(a, b, dims):
    return lax.dot_general(a, b, ((dims), ((), ())), precision=lax.Precision.HIGHEST, preferred_element_type=f32)


WS = {
    "enc_f": (128, 96), "rd_f": (128, 128), "l_f": (128, 192), "ti_f": (128, 512), "to_f": (128, 128), "db_f": (128, 256),
    "dt_f": (128, 256), "out_f": (96, 128), "out_b": (128, 96), "db_b": (128, 128), "dt_b": (128, 128), "to_b": (128, 128),
    "ti_b": (256, 256), "ru_b": (64, 128), "he_b": (128, 256), "book_b": (256, 256), "book_t": (256, 256),
}
KEEP = {
    "x": (48, 8, f32), "xb": (48, 8, bf16), "he": (128, 8, bf16), "de": (128, 8, bf16), "ar": (64, 8, bf16), "dr": (64, 8, bf16),
    "gap_b": (64, 8, bf16), "gl": (64, 8, f32), "both": (128, 8, bf16), "hd": (128, 8, bf16), "gr": (48, 8, bf16),
    "gpd": (128, 8, bf16), "qb": (128, 8, bf16),
}
KEEP_TOP = {
    "ti": (256, bf16), "ht": (128, bf16), "dt": (128, bf16), "gap_t": (64, f32), "gt": (64, f32), "qt": (128, bf16), "gtr": (128, bf16),
    "glt": (64, bf16), "gpt": (128, bf16),
}
ACC = {
    "e": (128, 48), "he": (128, 128), "ar": (64, 64), "db": (128, 128), "out": (128, 48), "sum_b": (144, 256), "sum_t": (144, 256),
}


def weights(par, book_ref, w):
    part = par.T
    f = lambda lo, hi: par[lo:hi]
    t = lambda lo, hi: part[:, lo:hi]
    cross = exact(f(O_L, O_TO), f(O_RU, O_TI), ((1,), (1,)))
    w["enc_f"][...] = pair(0.5 * t(O_ENC, O_RU))
    w["rd_f"][...] = stack(0.5 * f(O_RD, O_L))
    w["l_f"][...] = stack(lanes([f(O_L, O_TO), cross]))
    w["ti_f"][...] = pair(0.5 * t(O_TI, O_DB))
    w["to_f"][...] = stack(f(O_TO, O_OUT))
    w["db_f"][...] = quad(0.5 * t(O_DB, O_DT))
    w["dt_f"][...] = quad(0.5 * t(O_DT, O_RD))
    w["out_f"][...] = stack(f(O_OUT, O_END))
    w["out_b"][...] = pair(0.5 * t(O_OUT, O_END))
    w["db_b"][...] = stack(f(O_DB, O_DT))
    w["dt_b"][...] = stack(f(O_DT, O_RD))
    w["to_b"][...] = pair(0.5 * t(O_TO, O_OUT))
    w["ti_b"][...] = pair(f(O_TI, O_DB))
    w["ru_b"][...] = pair(0.5 * exact(f(O_RU, O_TI), f(O_L, O_TO), ((1,), (1,))))
    w["he_b"][...] = pair(0.5 * lanes([t(O_L, O_TO), t(O_RD, O_L)]))
    for level, name in enumerate(("book_b", "book_t")):
        w[name][...] = jnp.concatenate([stack(book_ref[level][:, 256 * a : 256 * a + 256]) for a in (0, 1)], axis=0)


def code_keys(rows_ref, cols_ref, src, per):
    lo, hi = spread_codes(src[...], per)
    rows_ref[0] = lo
    rows_ref[1] = hi
    cols_ref[...] = lo.T


def high_bits(codes, level, n, at, R):
    return lanes([codes[level][0][1, p : p + 1, pl.ds(at, R)] for p in range(n)])


def first(i, size):
    return i * size if isinstance(i, int) else pl.multiple_of(i * size, size)


def hot(equal):
    return jnp.where(equal, jnp.ones((), bf16), jnp.zeros((), bf16))


def encoder(i, R, x_ref, codes, w, keep, acc):
    along = lax.broadcasted_iota(jnp.int32, (R, 256), 1).astype(f32).astype(bf16)
    at = first(i, R)
    tops = pl.ds(first(i, 2 * R), 2 * R)

    def scatter(level, n, latent):
        key = codes[level][1][pl.ds(at, R), :]
        low = jnp.concatenate([
            hot(along == jnp.broadcast_to(key[:, p : p + 1], (R, 256)).astype(bf16)) for p in range(n)
        ], axis=0)
        high = high_bits(codes, level, n, at, R).astype(bf16)
        ones = jnp.broadcast_to(high, latent.shape) * latent
        row = lax.broadcasted_iota(jnp.int32, (16, n * R), 0)
        count = jnp.where(row == 0, 1.0 - high.astype(f32), jnp.where(row == 1, high.astype(f32), 0.0)).astype(bf16)
        return nn(jnp.concatenate([latent - ones, ones, count], axis=0), low)

    xt = x_ref[pl.ds(at, R), :].T
    x = lanes([xt[48 * p : 48 * p + 48] for p in range(8)])
    keep["x"][i] = x
    xb = x.astype(bf16)
    keep["xb"][i] = xb
    he, de = silu_and_slope(nn(w["enc_f"][...], twice(xb)))
    heb = he.astype(bf16)
    keep["he"][i] = heb
    keep["de"][i] = de.astype(bf16)
    ar, dr = silu_and_slope(halves(nn(w["rd_f"][...], heb)))
    arb = ar.astype(bf16)
    keep["ar"][i] = arb
    keep["dr"][i] = dr.astype(bf16)
    lbb = halves(nn(w["l_f"][...], jnp.concatenate([heb, arb], axis=0))).astype(bf16)
    ti = lanes([
        jnp.concatenate([lbb[:, R * p : R * p + R] for p in range(4 * g, 4 * g + 4)], axis=0) for g in (0, 1)
    ])
    keep["ti"][:, tops] = ti
    ht, dt = silu_and_slope(nn(w["ti_f"][...], twice(ti)))
    htb = ht.astype(bf16)
    keep["ht"][:, tops] = htb
    keep["dt"][:, tops] = dt.astype(bf16)
    lt = halves(nn(w["to_f"][...], htb))
    keep["gap_t"][:, tops] = lt
    acc["sum_b"][...] += scatter(0, 8, lbb)
    acc["sum_t"][...] += scatter(1, 2, lt.astype(bf16))


def decoder(i, R, m_ref, codes, w, keep, acc, lacc):
    down = lax.broadcasted_iota(jnp.int32, (256, R), 0).astype(f32).astype(bf16)
    at = first(i, R)
    tops = pl.ds(first(i, 2 * R), 2 * R)

    def gather(level, n, book):
        key = codes[level][0][0, :, pl.ds(at, R)]
        low = lanes([hot(down == key[p : p + 1, :].astype(bf16)) for p in range(n)])
        both = nn(book, low)
        return jnp.where(high_bits(codes, level, n, at, R) > 0.5, both[128:], both[:128]).astype(bf16)

    mt = m_ref[pl.ds(at, R), :].astype(f32).T
    m = lanes([mt[48 * p : 48 * p + 48] for p in range(8)])
    qb2 = gather(0, 8, w["book_b"][...])
    qt2 = gather(1, 2, w["book_t"][...])
    ti = keep["ti"][:, tops]
    lb = lanes([ti[64 * (p % 4) : 64 * (p % 4) + 64, R * (p // 4) : R * (p // 4) + R] for p in range(8)]).astype(f32)
    gap_b = lb - halves(qb2.astype(f32))
    gap_t = keep["gap_t"][:, tops] - halves(qt2.astype(f32))
    keep["gap_b"][i] = gap_b.astype(bf16)
    keep["gap_t"][:, tops] = gap_t
    top = nn(w["dt_f"][...], twice(qt2))
    pre = nn(w["db_f"][...], twice(qb2)) + lanes([top[:, R * (p // 4) : R * (p // 4) + R] for p in range(8)])
    hd, dd = silu_and_slope(pre)
    hdb = hd.astype(bf16)
    err = halves(nn(w["out_f"][...], hdb)) - keep["x"][i]
    me = m * err
    lacc[0:48] += sum((me * err)[:, R * p : R * p + R] for p in range(8))
    lacc[48:112] += sum((gap_b * gap_b)[:, R * p : R * p + R] for p in range(8))
    lacc[112:176] += sum((gap_t * gap_t)[:, R * p : R * p + R] for p in range(2))
    grb = me.astype(bf16)
    gpd = nn(w["out_b"][...], twice(grb)) * dd
    gpdb = gpd.astype(bf16)
    gtrb = lanes([sum(gpd[:, R * p : R * p + R] for p in range(4 * g_, 4 * g_ + 4)) for g_ in (0, 1)]).astype(bf16)
    keep["gt"][:, tops] = halves(nn(w["dt_b"][...], gtrb))
    keep["gl"][i] = halves(nn(w["db_b"][...], gpdb))
    keep["hd"][i] = hdb
    keep["gr"][i] = grb
    keep["gpd"][i] = gpdb
    keep["qb"][i] = qb2
    keep["qt"][:, tops] = qt2
    keep["gtr"][:, tops] = gtrb


def top_backward(n, R, kt, w, keep):
    gltb = (keep["gt"][...] + kt * keep["gap_t"][...]).astype(bf16)
    keep["glt"][...] = gltb
    gptb = (nn(w["to_b"][...], twice(gltb)) * keep["dt"][...].astype(f32)).astype(bf16)
    keep["gpt"][...] = gptb
    gti = nn(w["ti_b"][...], twice(gptb))
    for i in range(n):
        for p in range(8):
            at = 2 * R * i + R * (p // 4)
            keep["gl"][i, :, R * p : R * p + R] += gti[64 * (p % 4) : 64 * (p % 4) + 64, at : at + R]


def backward_inner(i, kb, w, keep, acc):
    glbb = (keep["gl"][i] + kb * keep["gap_b"][i].astype(f32)).astype(bf16)
    gprb = (nn(w["ru_b"][...], twice(glbb)) * keep["dr"][i].astype(f32)).astype(bf16)
    both = jnp.concatenate([glbb, gprb], axis=0)
    keep["both"][i] = both
    acc["ar"][...] += nt(glbb, keep["ar"][i])


def backward_outer(i, w, keep, acc):
    gpeb = (nn(w["he_b"][...], twice(keep["both"][i])) * keep["de"][i].astype(f32)).astype(bf16)
    acc["e"][...] += nt(gpeb, keep["xb"][i])


def add(ref, v):
    ref[...] += v


def scratches(rows, R):
    return (
        [pltpu.VMEM(s, bf16) for s in WS.values()]
        + [pltpu.VMEM((rows // R, c, n * R), t) for c, n, t in KEEP.values()]
        + [pltpu.VMEM((c, rows * 2), t) for c, t in KEEP_TOP.values()]
        + [pltpu.VMEM(s, f32) for s in ACC.values()]
        + [pltpu.VMEM((2, 8, rows), f32), pltpu.VMEM((rows, 8), f32)] * 2
        + [pltpu.VMEM((176, R), f32)]
    )


def unscratch(scratch):
    scratch = list(scratch)
    take = lambda names: {k: scratch.pop(0) for k in names}
    w, keep, acc = take(WS), take(list(KEEP) + list(KEEP_TOP)), take(ACC)
    codes = ((scratch.pop(0), scratch.pop(0)), (scratch.pop(0), scratch.pop(0)))
    return w, keep, acc, codes, scratch


def swap_start(axis, n, src_at, buf, sems):
    me = lax.axis_index(axis)

    def go(k, carry):
        peer = lax.rem(me + k, n)
        pltpu.make_async_remote_copy(
            src_ref=src_at(peer), dst_ref=buf.at[me], send_sem=sems[0], recv_sem=sems[1],
            device_id={axis: peer}, device_id_type=pl.DeviceIdType.MESH,
        ).start()
        return carry

    lax.fori_loop(1, n, go, 0)


def swap_wait(axis, n, buf, sems, recv):
    others = buf.at[0 : n - 1]
    copy = pltpu.make_async_remote_copy(
        src_ref=others, dst_ref=others, send_sem=sems[0], recv_sem=sems[1],
        device_id={axis: lax.axis_index(axis)}, device_id_type=pl.DeviceIdType.MESH,
    )
    if recv:
        copy.wait_recv()
    else:
        copy.wait_send()


def total(v):
    return jnp.sum(jnp.sum(v, axis=0, keepdims=True), axis=1, keepdims=True)


def in_order(buf, n):
    out = buf[0]
    for s in range(1, n):
        out = out + buf[s]
    return out

N_DP = 16
N_REP = 8
SHARE = 46
def share_start(shares, src, buf, sems):
    me = lax.axis_index("dp")
    for s in shares:
        @pl.when(me != s)
        def _():
            pltpu.make_async_remote_copy(
                src_ref=src.at[s], dst_ref=buf.at[me], send_sem=sems[0], recv_sem=sems[1],
                device_id={"dp": s}, device_id_type=pl.DeviceIdType.MESH,
            ).start()


def put_rows(ref, at, v):
    end = at + v.shape[0]
    for s in range(N_DP):
        lo, hi = max(at, SHARE * s), min(end, SHARE * s + SHARE)
        if lo < hi:
            ref[s, lo - SHARE * s : hi - SHARE * s] = v[lo - at : hi - at]


def each(n, f):
    if n == 1:
        f(0)
        return

    def go(i, carry):
        f(i)
        return carry

    lax.fori_loop(0, n, go, 0)


def kernel(*refs, R):
    sources, refs = refs[:11], refs[11:]
    (scal_out, params_out, first_out, second_out, mom_out, counts_out, sums_out, books_out), scratch = refs[:8], refs[8:]
    inputs, scratch = scratch[:11], scratch[11:]
    x_ref, m_ref, cb_ref, ct_ref, p_ref, first_ref, second_ref, mom_ref, cnt_ref, ema_ref, book_ref = inputs
    w, keep, acc, codes, scratch = unscratch(scratch)
    (
        lacc, valid_own, valid_all, stat_own, stat_all, grad_own, grad_all, part_own, part_all, sums_all, step_all,
        par_share, in_sems, *sems,
    ) = scratch
    loads = [pltpu.make_async_copy(a, b, in_sems.at[i]) for i, (a, b) in enumerate(zip(sources, inputs))]
    load_x, load_m, load_cb, load_ct, load_p, *load_rest, load_book = loads
    for load in (load_p, load_x, load_cb, load_ct, load_book, load_m, *load_rest):
        load.start()
    sems = [(sems[2 * i], sems[2 * i + 1]) for i in range(6)]
    sem_valid, sem_stat, sem_grad, sem_part, sem_sums, sem_step = sems
    dp = lax.axis_index("dp")
    rep = lax.axis_index("rep")
    rows = x_ref.shape[0]
    n = rows // R

    barrier = pltpu.get_barrier_semaphore()
    for axis, size, me in (("dp", N_DP, dp), ("rep", N_REP, rep)):
        def hello(k, carry):
            pl.semaphore_signal(
                barrier, inc=1, device_id={axis: lax.rem(me + k, size)}, device_id_type=pl.DeviceIdType.MESH
            )
            return carry

        lax.fori_loop(1, size, hello, 0)

    for load in (load_p, load_book, load_cb, load_ct):
        load.wait()
    weights(p_ref[...], book_ref, w)
    code_keys(*codes[0], cb_ref, 8)
    code_keys(*codes[1], ct_ref, 2)
    for v in acc.values():
        v[...] = jnp.zeros_like(v)
    lacc[...] = jnp.zeros_like(lacc)
    load_x.wait()
    each(n, lambda i: encoder(i, R, x_ref, codes, w, keep, acc))

    load_m.wait()
    valid_own[...] = jnp.broadcast_to(total(m_ref[...].astype(f32)), (8, 128))
    valid_all[dp] = valid_own[...]
    valid_src = lambda peer: valid_own
    pl.semaphore_wait(barrier, N_DP + N_REP - 2)
    swap_start("dp", N_DP, valid_src, valid_all, sem_valid)

    for d in range(N_DP):
        name, at = ("sum_b", "sum_t")[d // 8], 8 * (d % 8)
        part_own[d] = lanes([acc[name][at : at + 8], acc[name][64 + at : 72 + at]])
    part_src = lambda peer: part_own.at[peer]
    swap_start("dp", N_DP, part_src, part_all, sem_part)
    stat_own[...] = jnp.concatenate(
        [
            acc[name][128 + a : 129 + a, 128 * j : 128 * j + 128]
            for name in ("sum_b", "sum_t") for a in (0, 1) for j in (0, 1)
        ], axis=0
    )
    stat_src = lambda peer: stat_own
    swap_start("dp", N_DP, stat_src, stat_all, sem_stat)
    part_all[dp] = part_own[dp]
    stat_all[dp] = stat_own[...]

    each(n, lambda i: decoder(i, R, m_ref, codes, w, keep, acc, lacc))

    group_rows = rows * 8 * N_DP
    swap_wait("dp", N_DP, valid_all, sem_valid, True)
    count = in_order(valid_all, N_DP)[0:1, 0:1]
    scale = 2.0 / count
    kb = beta_commit / (group_rows * EMB) * count
    kt = beta_commit / (group_rows // 4 * EMB) * count
    lane = lax.broadcasted_iota(jnp.int32, (1, 128), 1)
    losses = jnp.where(lane == 0, total(lacc[0:48]), jnp.where(lane == 1, total(lacc[48:112]), total(lacc[112:176])))
    for s in range(N_DP):
        grad_own[s, SHARE:48] = jnp.broadcast_to(losses, (48 - SHARE, 128))
    top_backward(n, R, kt, w, keep)
    each(n, lambda i: backward_inner(i, kb, w, keep, acc))
    each(n, lambda i: backward_outer(i, w, keep, acc))
    cross = acc["ar"][...]
    put_rows(grad_own, O_ENC, acc["e"][...].T * scale)
    put_rows(grad_own, O_RU, exact(cross, p_ref[O_L:O_TO], ((0,), (0,))) * scale)
    share_start((0, 1), grad_own, grad_all, sem_grad)
    put_rows(grad_own, O_TI, nt(keep["ti"][...], keep["gpt"][...]) * scale)
    share_start((2, 3, 4, 5, 6, 7), grad_own, grad_all, sem_grad)
    each(n, lambda i: add(acc["db"], nt(keep["qb"][i], keep["gpd"][i])))
    put_rows(grad_own, O_DB, halves(acc["db"][...]) * scale)
    put_rows(grad_own, O_DT, halves(nt(keep["qt"][...], keep["gtr"][...])) * scale)
    share_start((8, 9), grad_own, grad_all, sem_grad)
    each(n, lambda i: add(acc["he"], nt(keep["both"][i], keep["he"][i])))
    put_rows(grad_own, O_RD, acc["he"][64:128] * scale)
    put_rows(grad_own, O_L, (acc["he"][0:64] + exact(cross, p_ref[O_RU:O_TI], ((1,), (0,)))) * scale)
    put_rows(grad_own, O_TO, nt(keep["ht"][...], keep["glt"][...]).T * scale)
    share_start((12, 13, 10, 11), grad_own, grad_all, sem_grad)
    each(n, lambda i: add(acc["out"], nt(keep["hd"][i], keep["gr"][i])))
    put_rows(grad_own, O_OUT, acc["out"][...].T * scale)
    share_start((14, 15), grad_own, grad_all, sem_grad)
    grad_all[dp] = grad_own[dp]

    for load in load_rest:
        load.wait()
    for s in range(N_DP):
        par_share[s, 0:SHARE] = p_ref[SHARE * s : SHARE * s + SHARE]
    swap_wait("dp", N_DP, part_all, sem_part, True)
    sums_all[dp] = in_order(part_all, N_DP)
    swap_wait("dp", N_DP, stat_all, sem_stat, True)
    stats = in_order(stat_all, N_DP)
    seen = jnp.concatenate([lanes([stats[4 * level + j : 4 * level + j + 1] for j in range(4)]) for level in (0, 1)], axis=0)
    counts_new = ema_decay * cnt_ref[...] + (1.0 - ema_decay) * seen
    counts_out[0] = counts_new
    totals = jnp.sum(counts_new, axis=1, keepdims=True)
    smooth = (counts_new + laplace_eps) / (totals + K * laplace_eps) * totals
    swap_wait("dp", N_DP, grad_all, sem_grad, True)
    summed = in_order(grad_all, N_DP)
    grads = summed[0:SHARE]
    own = par_share[dp][0:SHARE]
    first_new = beta_first * first_ref[:, 0, :] + (1.0 - beta_first) * grads
    second_new = beta_second * second_ref[:, 0, :] + (1.0 - beta_second) * grads * grads
    bias_first = 1.0 - beta_first**STEP
    bias_second = 1.0 - beta_second**STEP
    step_here = inner_rate * (
        first_new / bias_first / (jnp.sqrt(second_new / bias_second) + adam_eps) + weight_decay * own
    )
    step_all[rep, 0:SHARE] = step_here
    step_all[rep, SHARE:48] = jnp.zeros((48 - SHARE, 128), f32)
    step_src = lambda peer: step_all.at[rep]
    swap_start("rep", N_REP, step_src, step_all, sem_step)
    sums_src = lambda peer: sums_all.at[dp]
    swap_start("dp", N_DP, sums_src, sums_all, sem_sums)

    first_out[:, 0, :] = first_new
    second_out[:, 0, :] = second_new

    terms = summed[SHARE : SHARE + 1]
    loss = terms[:, 0:1] / count + beta_commit * (
        terms[:, 1:2] / (group_rows * EMB) + terms[:, 2:3] / (group_rows // 4 * EMB)
    )
    scal_out[...] = jnp.concatenate([jnp.broadcast_to(loss, (1, 128)), jnp.broadcast_to(count, (1, 128)), jnp.zeros((6, 128), f32)], axis=0)

    swap_wait("dp", N_DP, sums_all, sem_sums, True)
    for level in (0, 1):
        inverse = 1.0 / smooth[level : level + 1]
        for j in range(8):
            rows_j = slice(8 * j, 8 * j + 8)
            sums_new = ema_decay * ema_ref[level, rows_j] + (1.0 - ema_decay) * sums_all[8 * level + j]
            sums_out[0, level, rows_j] = sums_new
            books_out[0, level, rows_j] = sums_new * inverse

    swap_wait("rep", N_REP, step_all, sem_step, True)
    mean_delta = in_order(step_all, N_REP)[0:SHARE] * (1.0 / N_REP)
    momentum_new = outer_moment * mom_ref[...] + mean_delta
    mom_out[...] = momentum_new
    params_out[...] = own - outer_rate * (mean_delta + outer_moment * momentum_new)

    for axis, size, buf, sem in (
        ("dp", N_DP, valid_all, sem_valid), ("dp", N_DP, grad_all, sem_grad), ("dp", N_DP, part_all, sem_part),
        ("dp", N_DP, stat_all, sem_stat), ("rep", N_REP, step_all, sem_step), ("dp", N_DP, sums_all, sem_sums),
    ):
        swap_wait(axis, size, buf, sem, False)


def hand_over(scal, *refs):
    n = (len(refs) - 3) // 2
    ins, (loss_out, valid_out), outs, sems = refs[:n], refs[n : n + 2], refs[n + 2 : -1], refs[-1]
    copies = [pltpu.make_async_copy(a, b, sems.at[i]) for i, (a, b) in enumerate(zip(ins, outs))]
    for c in copies:
        c.start()
    loss_out[0] = scal[0, 0]
    valid_out[0] = scal[1, 0]
    for c in copies:
        c.wait()


def shards(
    pixels, valid_mask, bottom_codes, top_codes, params, first_moment, second_moment, outer_momentum, ema_counts,
    ema_sums, codebooks, *, R,
):
    rows = pixels.shape[0]
    vm = pl.BlockSpec(memory_space=pltpu.VMEM)
    sm = pl.BlockSpec(memory_space=pltpu.SMEM)
    hbm = pl.BlockSpec(memory_space=pl.ANY)
    dma = pltpu.SemaphoreType.DMA
    args = (
        pixels, valid_mask, bottom_codes.reshape(-1, 128), top_codes.reshape(-1, 128), params,
        jnp.swapaxes(first_moment, 0, 1), jnp.swapaxes(second_moment, 0, 1), outer_momentum, ema_counts,
        jnp.swapaxes(ema_sums, 1, 2), jnp.swapaxes(codebooks, 1, 2),
    )
    results = [(SHARE, 128), (SHARE, 1, 128), (SHARE, 1, 128), (SHARE, 128), (1, 2, K), (1, 2, EMB, K), (1, 2, EMB, K)]
    inner = pl.pallas_call(
        functools.partial(kernel, R=R),
        out_shape=tuple(pltpu.VMEM(s, f32) for s in [(8, 128)] + results),
        in_specs=[hbm] * 11,
        out_specs=(vm,) * 8,
        scratch_shapes=[pltpu.VMEM(v.shape, v.dtype) for v in args]
        + scratches(rows, R)
        + [
            pltpu.VMEM((8, 128), f32), pltpu.VMEM((N_DP, 8, 128), f32),
            pltpu.VMEM((8, 128), f32), pltpu.VMEM((N_DP, 8, 128), f32),
            pltpu.VMEM((N_DP, 48, 128), f32), pltpu.VMEM((N_DP, 48, 128), f32),
            pltpu.VMEM((N_DP, 8, 512), f32), pltpu.VMEM((N_DP, 8, 512), f32), pltpu.VMEM((N_DP, 8, 512), f32),
            pltpu.VMEM((N_REP, 48, 128), f32), pltpu.VMEM((N_DP, 48, 128), f32), dma((11,)),
        ]
        + [dma] * 12,
        compiler_params=pltpu.CompilerParams(
            vmem_limit_bytes=60 * 2**20, collective_id=0, has_side_effects=True
        ),
    )(*args)
    shape = lambda *s: jax.ShapeDtypeStruct(s, f32)
    loss, valid, params, first, second, mom, counts, sums, books = pl.pallas_call(
        hand_over,
        out_shape=(shape(1), shape(1)) + tuple(shape(*s) for s in results),
        in_specs=[vm] * 8,
        out_specs=(sm, sm) + (hbm,) * 7,
        scratch_shapes=[dma((7,))],
    )(*(pltpu.with_memory_space_constraint(v, pltpu.VMEM) for v in inner))
    return (
        loss, valid, params, jnp.swapaxes(first, 0, 1), jnp.swapaxes(second, 0, 1), mom, counts,
        jnp.swapaxes(sums, 2, 3), jnp.swapaxes(books, 2, 3),
    )


def solution(mesh):
    return jax.shard_map(
        functools.partial(shards, R=1024),
        mesh=mesh,
        in_specs=(
            P(("rep", "dp"), None),
            P(("rep", "dp"), None),
            P(("rep", "dp")),
            P(("rep", "dp")),
            P(),
            P("rep", "dp", None),
            P("rep", "dp", None),
            P("dp", None),
            P(),
            P(),
            P(),
        ),
        out_specs=(
            P("rep"),
            P("rep"),
            P("dp", None),
            P("rep", "dp", None),
            P("rep", "dp", None),
            P("dp", None),
            P("rep", None, None),
            P("rep", None, None, None),
            P("rep", None, None, None),
        ),
        check_vma=False,
    )
```

```python
import functools
import jax
import jax.numpy as jnp
from jax import lax
from jax.experimental import pallas as pl
from jax.experimental.pallas import tpu as pltpu
from jax.sharding import PartitionSpec as P

PF = 48
EMB = 64
K = 512
STEP = 10
beta_commit = 0.25
ema_decay = 0.8
laplace_eps = 1e-05
inner_rate = 0.03
beta_first = 0.9
beta_second = 0.999
adam_eps = 1e-08
weight_decay = 0.01
outer_rate = 0.7
outer_moment = 0.9

bf16 = jnp.bfloat16
f32 = jnp.float32
O_ENC, O_RU, O_TI, O_DB, O_DT, O_RD, O_L, O_TO, O_OUT, O_END = 0, 48, 112, 368, 432, 496, 560, 624, 688, 736


def nn(a, b):
    return lax.dot_general(a, b, (((1,), (0,)), ((), ())), preferred_element_type=f32)


def nt(a, b):
    return lax.dot_general(a, b, (((1,), (1,)), ((), ())), preferred_element_type=f32)


def tn(a, b):
    return lax.dot_general(a, b, (((0,), (0,)), ((), ())), preferred_element_type=f32)


def split(v):
    hi = v.astype(bf16)
    return hi, (v - hi.astype(f32)).astype(bf16)


def pair(v):
    hi, lo = split(v)
    return jnp.concatenate([hi, lo], axis=1)


def quad(v):
    hi, lo = split(v)
    return jnp.concatenate([hi, hi, lo, lo], axis=1)


def twice(v):
    return jnp.concatenate([v, v], axis=0)


def silu_and_slope(u):
    w = 1.0 + jnp.tanh(u)
    a = u * w
    return a, w + a * (2.0 - w)


def lanes(parts):
    return jnp.concatenate(parts, axis=1)


def spread_codes(codes, per_row):
    a = codes.shape[0]
    rows = a * 128 // per_row
    span = 128 // per_row
    lo = (codes & 255).astype(f32).astype(bf16)
    hi = (codes >> 8).astype(f32).astype(bf16)
    up = (lax.broadcasted_iota(jnp.int32, (a, rows), 0) == lax.broadcasted_iota(jnp.int32, (a, rows), 1) // span)
    up = up.astype(f32).astype(bf16)
    keep = (
        lax.broadcasted_iota(jnp.int32, (128, rows), 0) // per_row
        == lax.broadcasted_iota(jnp.int32, (128, rows), 1) % span
    )
    pick = (
        lax.broadcasted_iota(jnp.int32, (8, 128), 0)
        == lax.broadcasted_iota(jnp.int32, (8, 128), 1) % per_row
    )
    pick = pick.astype(f32).astype(bf16)
    out = []
    for part in (lo, hi):
        wide = jnp.where(keep, tn(part, up), 0.0).astype(bf16)
        out.append(nn(pick, wide))
    return out


def stack(v):
    hi, lo = split(v)
    return jnp.concatenate([hi, lo], axis=0)


def halves(v):
    n = v.shape[0] // 2
    return v[:n] + v[n:]


def exact(a, b, dims):
    return lax.dot_general(a, b, ((dims), ((), ())), precision=lax.Precision.HIGHEST, preferred_element_type=f32)


WS = {
    "enc_f": (128, 96), "rd_f": (128, 128), "l_f": (128, 192), "ti_f": (128, 512), "to_f": (128, 128), "db_f": (128, 256),
    "dt_f": (128, 256), "out_f": (96, 128), "out_b": (128, 96), "db_b": (64, 256), "dt_b": (128, 128), "to_b": (128, 128),
    "ti_b": (256, 256), "ru_b": (64, 128), "he_b": (128, 256), "book_b": (256, 256), "book_t": (256, 256),
}
KEEP = {
    "x": (48, 8, f32), "xb": (48, 8, bf16), "he": (128, 8, bf16), "de": (128, 8, bf16), "ar": (64, 8, bf16), "dr": (64, 8, bf16),
    "gap_b": (64, 8, bf16), "gl": (64, 8, f32), "both": (128, 8, bf16), "hd": (128, 8, bf16), "gr": (48, 8, bf16),
    "gpd": (128, 8, bf16), "qb": (128, 8, bf16),
}
KEEP_TOP = {
    "ti": (256, bf16), "ht": (128, bf16), "dt": (128, bf16), "gap_t": (64, f32), "gt": (64, f32), "qt": (128, bf16), "gtr": (128, bf16),
    "glt": (64, bf16), "gpt": (128, bf16),
}
ACC = {
    "e": (128, 48), "he": (128, 128), "ar": (64, 64), "db": (128, 128), "out": (128, 48), "sum_b": (144, 256), "sum_t": (144, 256),
}


def weights(par, book_ref, w):
    part = par.T
    f = lambda lo, hi: par[lo:hi]
    t = lambda lo, hi: part[:, lo:hi]
    cross = exact(f(O_L, O_TO), f(O_RU, O_TI), ((1,), (1,)))
    w["enc_f"][...] = pair(0.5 * t(O_ENC, O_RU))
    w["rd_f"][...] = stack(0.5 * f(O_RD, O_L))
    w["l_f"][...] = stack(lanes([f(O_L, O_TO), cross]))
    w["ti_f"][...] = pair(0.5 * t(O_TI, O_DB))
    w["to_f"][...] = stack(f(O_TO, O_OUT))
    w["db_f"][...] = quad(0.5 * t(O_DB, O_DT))
    w["dt_f"][...] = quad(0.5 * t(O_DT, O_RD))
    w["out_f"][...] = stack(f(O_OUT, O_END))
    w["out_b"][...] = pair(0.5 * t(O_OUT, O_END))
    w["db_b"][...] = pair(f(O_DB, O_DT))
    w["dt_b"][...] = stack(f(O_DT, O_RD))
    w["to_b"][...] = pair(0.5 * t(O_TO, O_OUT))
    w["ti_b"][...] = pair(f(O_TI, O_DB))
    w["ru_b"][...] = pair(0.5 * exact(f(O_RU, O_TI), f(O_L, O_TO), ((1,), (1,))))
    w["he_b"][...] = pair(0.5 * lanes([t(O_L, O_TO), t(O_RD, O_L)]))
    for level, name in enumerate(("book_b", "book_t")):
        w[name][...] = jnp.concatenate([stack(book_ref[level][:, 256 * a : 256 * a + 256]) for a in (0, 1)], axis=0)


def code_keys(rows_ref, cols_ref, src, per):
    lo, hi = spread_codes(src[...], per)
    rows_ref[0] = lo
    rows_ref[1] = hi
    cols_ref[...] = lo.T


def high_bits(codes, level, n, at, R):
    return lanes([codes[level][0][1, p : p + 1, pl.ds(at, R)] for p in range(n)])


def first(i, size):
    return i * size if isinstance(i, int) else pl.multiple_of(i * size, size)


def hot(equal):
    return jnp.where(equal, jnp.ones((), bf16), jnp.zeros((), bf16))


def encoder(i, R, x_ref, codes, w, keep, acc):
    along = lax.broadcasted_iota(jnp.int32, (R, 256), 1).astype(f32).astype(bf16)
    at = first(i, R)
    tops = pl.ds(first(i, 2 * R), 2 * R)

    def scatter(level, n, latent):
        key = codes[level][1][pl.ds(at, R), :]
        low = jnp.concatenate([
            hot(along == jnp.broadcast_to(key[:, p : p + 1], (R, 256)).astype(bf16)) for p in range(n)
        ], axis=0)
        high = high_bits(codes, level, n, at, R).astype(bf16)
        ones = jnp.broadcast_to(high, latent.shape) * latent
        row = lax.broadcasted_iota(jnp.int32, (16, n * R), 0)
        count = jnp.where(row == 0, 1.0 - high.astype(f32), jnp.where(row == 1, high.astype(f32), 0.0)).astype(bf16)
        return nn(jnp.concatenate([latent - ones, ones, count], axis=0), low)

    xt = x_ref[pl.ds(at, R), :].T
    x = lanes([xt[48 * p : 48 * p + 48] for p in range(8)])
    keep["x"][i] = x
    xb = x.astype(bf16)
    keep["xb"][i] = xb
    he, de = silu_and_slope(nn(w["enc_f"][...], twice(xb)))
    heb = he.astype(bf16)
    keep["he"][i] = heb
    keep["de"][i] = de.astype(bf16)
    ar, dr = silu_and_slope(halves(nn(w["rd_f"][...], heb)))
    arb = ar.astype(bf16)
    keep["ar"][i] = arb
    keep["dr"][i] = dr.astype(bf16)
    lbb = halves(nn(w["l_f"][...], jnp.concatenate([heb, arb], axis=0))).astype(bf16)
    ti = lanes([
        jnp.concatenate([lbb[:, R * p : R * p + R] for p in range(4 * g, 4 * g + 4)], axis=0) for g in (0, 1)
    ])
    keep["ti"][:, tops] = ti
    ht, dt = silu_and_slope(nn(w["ti_f"][...], twice(ti)))
    htb = ht.astype(bf16)
    keep["ht"][:, tops] = htb
    keep["dt"][:, tops] = dt.astype(bf16)
    lt = halves(nn(w["to_f"][...], htb))
    keep["gap_t"][:, tops] = lt
    acc["sum_b"][...] += scatter(0, 8, lbb)
    acc["sum_t"][...] += scatter(1, 2, lt.astype(bf16))


def decoder(i, R, m_ref, codes, w, keep, acc, lacc):
    down = lax.broadcasted_iota(jnp.int32, (256, R), 0).astype(f32).astype(bf16)
    at = first(i, R)
    tops = pl.ds(first(i, 2 * R), 2 * R)

    def gather(level, n, book):
        key = codes[level][0][0, :, pl.ds(at, R)]
        low = lanes([hot(down == key[p : p + 1, :].astype(bf16)) for p in range(n)])
        both = nn(book, low)
        return jnp.where(high_bits(codes, level, n, at, R) > 0.5, both[128:], both[:128]).astype(bf16)

    mt = m_ref[pl.ds(at, R), :].astype(f32).T
    m = lanes([mt[48 * p : 48 * p + 48] for p in range(8)])
    qb2 = gather(0, 8, w["book_b"][...])
    qt2 = gather(1, 2, w["book_t"][...])
    ti = keep["ti"][:, tops]
    lb = lanes([ti[64 * (p % 4) : 64 * (p % 4) + 64, R * (p // 4) : R * (p // 4) + R] for p in range(8)]).astype(f32)
    gap_b = lb - halves(qb2.astype(f32))
    gap_t = keep["gap_t"][:, tops] - halves(qt2.astype(f32))
    keep["gap_b"][i] = gap_b.astype(bf16)
    keep["gap_t"][:, tops] = gap_t
    top = nn(w["dt_f"][...], twice(qt2))
    pre = nn(w["db_f"][...], twice(qb2)) + lanes([top[:, R * (p // 4) : R * (p // 4) + R] for p in range(8)])
    hd, dd = silu_and_slope(pre)
    hdb = hd.astype(bf16)
    err = halves(nn(w["out_f"][...], hdb)) - keep["x"][i]
    me = m * err
    lacc[0:48] += sum((me * err)[:, R * p : R * p + R] for p in range(8))
    lacc[48:112] += sum((gap_b * gap_b)[:, R * p : R * p + R] for p in range(8))
    lacc[112:176] += sum((gap_t * gap_t)[:, R * p : R * p + R] for p in range(2))
    grb = me.astype(bf16)
    gpd = nn(w["out_b"][...], twice(grb)) * dd
    gpdb = gpd.astype(bf16)
    gtrb = lanes([sum(gpd[:, R * p : R * p + R] for p in range(4 * g_, 4 * g_ + 4)) for g_ in (0, 1)]).astype(bf16)
    keep["gt"][:, tops] = halves(nn(w["dt_b"][...], gtrb))
    keep["gl"][i] = nn(w["db_b"][...], twice(gpdb))
    keep["hd"][i] = hdb
    keep["gr"][i] = grb
    keep["gpd"][i] = gpdb
    keep["qb"][i] = qb2
    keep["qt"][:, tops] = qt2
    keep["gtr"][:, tops] = gtrb


def top_backward(n, R, kt, w, keep):
    gltb = (keep["gt"][...] + kt * keep["gap_t"][...]).astype(bf16)
    keep["glt"][...] = gltb
    gptb = (nn(w["to_b"][...], twice(gltb)) * keep["dt"][...].astype(f32)).astype(bf16)
    keep["gpt"][...] = gptb
    gti = nn(w["ti_b"][...], twice(gptb))
    for i in range(n):
        for p in range(8):
            at = 2 * R * i + R * (p // 4)
            keep["gl"][i, :, R * p : R * p + R] += gti[64 * (p % 4) : 64 * (p % 4) + 64, at : at + R]


def backward_inner(i, kb, w, keep, acc):
    glbb = (keep["gl"][i] + kb * keep["gap_b"][i].astype(f32)).astype(bf16)
    gprb = (nn(w["ru_b"][...], twice(glbb)) * keep["dr"][i].astype(f32)).astype(bf16)
    both = jnp.concatenate([glbb, gprb], axis=0)
    keep["both"][i] = both
    acc["ar"][...] += nt(glbb, keep["ar"][i])


def backward_outer(i, w, keep, acc):
    gpeb = (nn(w["he_b"][...], twice(keep["both"][i])) * keep["de"][i].astype(f32)).astype(bf16)
    acc["e"][...] += nt(gpeb, keep["xb"][i])


def add(ref, v):
    ref[...] += v


def scratches(rows, R):
    return (
        [pltpu.VMEM(s, bf16) for s in WS.values()]
        + [pltpu.VMEM((rows // R, c, n * R), t) for c, n, t in KEEP.values()]
        + [pltpu.VMEM((c, rows * 2), t) for c, t in KEEP_TOP.values()]
        + [pltpu.VMEM(s, f32) for s in ACC.values()]
        + [pltpu.VMEM((2, 8, rows), f32), pltpu.VMEM((rows, 8), f32)] * 2
        + [pltpu.VMEM((176, R), f32)]
    )


def unscratch(scratch):
    scratch = list(scratch)
    take = lambda names: {k: scratch.pop(0) for k in names}
    w, keep, acc = take(WS), take(list(KEEP) + list(KEEP_TOP)), take(ACC)
    codes = ((scratch.pop(0), scratch.pop(0)), (scratch.pop(0), scratch.pop(0)))
    return w, keep, acc, codes, scratch


def swap_start(axis, n, src_at, buf, sems):
    me = lax.axis_index(axis)

    def go(peer, carry):
        @pl.when(peer != me)
        def _():
            pltpu.make_async_remote_copy(
                src_ref=src_at(peer), dst_ref=buf.at[me], send_sem=sems[0], recv_sem=sems[1],
                device_id={axis: peer}, device_id_type=pl.DeviceIdType.MESH,
            ).start()

        return carry

    lax.fori_loop(0, n, go, 0)


def swap_wait(axis, n, buf, sems, recv):
    others = buf.at[0 : n - 1]
    copy = pltpu.make_async_remote_copy(
        src_ref=others, dst_ref=others, send_sem=sems[0], recv_sem=sems[1],
        device_id={axis: lax.axis_index(axis)}, device_id_type=pl.DeviceIdType.MESH,
    )
    if recv:
        copy.wait_recv()
    else:
        copy.wait_send()


def total(v):
    while v.shape[0] % 16 == 0:
        v = halves(v)
    return jnp.sum(jnp.sum(v, axis=0, keepdims=True), axis=1, keepdims=True)


def in_order(buf, n):
    out = buf[0]
    for s in range(1, n):
        out = out + buf[s]
    return out

N_DP = 16
N_REP = 8
SHARE = 46
def share_start(shares, src, buf, sems):
    me = lax.axis_index("dp")
    for s in shares:
        @pl.when(me != s)
        def _():
            pltpu.make_async_remote_copy(
                src_ref=src.at[s], dst_ref=buf.at[me], send_sem=sems[0], recv_sem=sems[1],
                device_id={"dp": s}, device_id_type=pl.DeviceIdType.MESH,
            ).start()


def put_rows(ref, at, v):
    end = at + v.shape[0]
    for s in range(N_DP):
        lo, hi = max(at, SHARE * s), min(end, SHARE * s + SHARE)
        if lo < hi:
            ref[s, lo - SHARE * s : hi - SHARE * s] = v[lo - at : hi - at]


def each(n, f):
    if n == 1:
        f(0)
        return

    def go(i, carry):
        f(i)
        return carry

    lax.fori_loop(0, n, go, 0)


def kernel(*refs, R):
    sources, refs = refs[:11], refs[11:]
    (scal_out, params_out, first_out, second_out, mom_out, counts_out, sums_out, books_out), scratch = refs[:8], refs[8:]
    inputs, scratch = scratch[:11], scratch[11:]
    x_ref, m_ref, cb_ref, ct_ref, p_ref, first_ref, second_ref, mom_ref, cnt_ref, ema_ref, book_ref = inputs
    w, keep, acc, codes, scratch = unscratch(scratch)
    (
        lacc, valid_own, valid_all, stat_own, stat_all, grad_own, grad_all, part_own, part_all, sums_all, step_all,
        par_share, in_sems, *sems,
    ) = scratch
    loads = [pltpu.make_async_copy(a, b, in_sems.at[i]) for i, (a, b) in enumerate(zip(sources, inputs))]
    load_x, load_m, load_cb, load_ct, load_p, *load_rest, load_book = loads
    for load in (load_p, load_x, load_cb, load_ct, load_book, load_m, *load_rest):
        load.start()
    sems = [(sems[2 * i], sems[2 * i + 1]) for i in range(6)]
    sem_valid, sem_stat, sem_grad, sem_part, sem_sums, sem_step = sems
    dp = lax.axis_index("dp")
    rep = lax.axis_index("rep")
    rows = x_ref.shape[0]
    n = rows // R

    barrier = pltpu.get_barrier_semaphore()
    for axis, size, me in (("dp", N_DP, dp), ("rep", N_REP, rep)):
        def hello(k, carry):
            pl.semaphore_signal(
                barrier, inc=1, device_id={axis: lax.rem(me + k, size)}, device_id_type=pl.DeviceIdType.MESH
            )
            return carry

        lax.fori_loop(1, size, hello, 0)

    for load in (load_p, load_book, load_cb, load_ct):
        load.wait()
    weights(p_ref[...], book_ref, w)
    code_keys(*codes[0], cb_ref, 8)
    code_keys(*codes[1], ct_ref, 2)
    for v in acc.values():
        v[...] = jnp.zeros_like(v)
    lacc[...] = jnp.zeros_like(lacc)
    load_x.wait()
    each(n, lambda i: encoder(i, R, x_ref, codes, w, keep, acc))

    load_m.wait()
    valid_own[...] = jnp.broadcast_to(total(m_ref[...].astype(f32)), (8, 128))
    valid_all[dp] = valid_own[...]
    valid_src = lambda peer: valid_own
    pl.semaphore_wait(barrier, N_DP + N_REP - 2)
    swap_start("dp", N_DP, valid_src, valid_all, sem_valid)

    for d in range(N_DP):
        name, at = ("sum_b", "sum_t")[d // 8], 8 * (d % 8)
        part_own[d] = lanes([acc[name][at : at + 8], acc[name][64 + at : 72 + at]])
    part_src = lambda peer: part_own.at[peer]
    swap_start("dp", N_DP, part_src, part_all, sem_part)
    stat_own[...] = jnp.concatenate(
        [
            acc[name][128 + a : 129 + a, 128 * j : 128 * j + 128]
            for name in ("sum_b", "sum_t") for a in (0, 1) for j in (0, 1)
        ], axis=0
    )
    stat_src = lambda peer: stat_own
    swap_start("dp", N_DP, stat_src, stat_all, sem_stat)
    part_all[dp] = part_own[dp]
    stat_all[dp] = stat_own[...]

    each(n, lambda i: decoder(i, R, m_ref, codes, w, keep, acc, lacc))

    group_rows = rows * 8 * N_DP
    swap_wait("dp", N_DP, valid_all, sem_valid, True)
    count = in_order(valid_all, N_DP)[0:1, 0:1]
    scale = 2.0 / count
    kb = beta_commit / (group_rows * EMB) * count
    kt = beta_commit / (group_rows // 4 * EMB) * count
    lane = lax.broadcasted_iota(jnp.int32, (1, 128), 1)
    losses = jnp.where(lane == 0, total(lacc[0:48]), jnp.where(lane == 1, total(lacc[48:112]), total(lacc[112:176])))
    for s in range(N_DP):
        grad_own[s, SHARE:48] = jnp.broadcast_to(losses, (48 - SHARE, 128))
    top_backward(n, R, kt, w, keep)
    each(n, lambda i: backward_inner(i, kb, w, keep, acc))
    each(n, lambda i: backward_outer(i, w, keep, acc))
    cross = acc["ar"][...]
    put_rows(grad_own, O_ENC, acc["e"][...].T * scale)
    put_rows(grad_own, O_RU, exact(cross, p_ref[O_L:O_TO], ((0,), (0,))) * scale)
    share_start((0, 1), grad_own, grad_all, sem_grad)
    put_rows(grad_own, O_TI, nt(keep["ti"][...], keep["gpt"][...]) * scale)
    share_start((2, 3, 4, 5, 6, 7), grad_own, grad_all, sem_grad)
    each(n, lambda i: add(acc["db"], nt(keep["qb"][i], keep["gpd"][i])))
    put_rows(grad_own, O_DB, halves(acc["db"][...]) * scale)
    put_rows(grad_own, O_DT, halves(nt(keep["qt"][...], keep["gtr"][...])) * scale)
    each(n, lambda i: add(acc["he"], nt(keep["both"][i], keep["he"][i])))
    put_rows(grad_own, O_RD, acc["he"][64:128] * scale)
    put_rows(grad_own, O_L, (acc["he"][0:64] + exact(cross, p_ref[O_RU:O_TI], ((1,), (0,)))) * scale)
    put_rows(grad_own, O_TO, nt(keep["ht"][...], keep["glt"][...]).T * scale)
    share_start((8, 9, 12, 13, 10, 11), grad_own, grad_all, sem_grad)
    each(n, lambda i: add(acc["out"], nt(keep["hd"][i], keep["gr"][i])))
    put_rows(grad_own, O_OUT, acc["out"][...].T * scale)
    share_start((14, 15), grad_own, grad_all, sem_grad)
    grad_all[dp] = grad_own[dp]

    for load in load_rest:
        load.wait()
    for s in range(N_DP):
        par_share[s, 0:SHARE] = p_ref[SHARE * s : SHARE * s + SHARE]
    swap_wait("dp", N_DP, part_all, sem_part, True)
    sums_all[dp] = in_order(part_all, N_DP)
    swap_wait("dp", N_DP, stat_all, sem_stat, True)
    stats = in_order(stat_all, N_DP)
    seen = jnp.concatenate([lanes([stats[4 * level + j : 4 * level + j + 1] for j in range(4)]) for level in (0, 1)], axis=0)
    counts_new = ema_decay * cnt_ref[...] + (1.0 - ema_decay) * seen
    counts_out[0] = counts_new
    totals = jnp.sum(counts_new, axis=1, keepdims=True)
    smooth = (counts_new + laplace_eps) / (totals + K * laplace_eps) * totals
    swap_wait("dp", N_DP, grad_all, sem_grad, True)
    summed = in_order(grad_all, N_DP)
    grads = summed[0:SHARE]
    own = par_share[dp][0:SHARE]
    first_new = beta_first * first_ref[:, 0, :] + (1.0 - beta_first) * grads
    second_new = beta_second * second_ref[:, 0, :] + (1.0 - beta_second) * grads * grads
    bias_first = 1.0 - beta_first**STEP
    bias_second = 1.0 - beta_second**STEP
    step_here = inner_rate * (
        first_new / bias_first / (jnp.sqrt(second_new / bias_second) + adam_eps) + weight_decay * own
    )
    step_all[rep, 0:SHARE] = step_here
    step_all[rep, SHARE:48] = jnp.zeros((48 - SHARE, 128), f32)
    step_src = lambda peer: step_all.at[rep]
    swap_start("rep", N_REP, step_src, step_all, sem_step)
    sums_src = lambda peer: sums_all.at[dp]
    swap_start("dp", N_DP, sums_src, sums_all, sem_sums)

    first_out[:, 0, :] = first_new
    second_out[:, 0, :] = second_new

    terms = summed[SHARE : SHARE + 1]
    loss = terms[:, 0:1] / count + beta_commit * (
        terms[:, 1:2] / (group_rows * EMB) + terms[:, 2:3] / (group_rows // 4 * EMB)
    )
    scal_out[...] = jnp.concatenate([jnp.broadcast_to(loss, (1, 128)), jnp.broadcast_to(count, (1, 128)), jnp.zeros((6, 128), f32)], axis=0)

    swap_wait("dp", N_DP, sums_all, sem_sums, True)
    for level in (0, 1):
        inverse = 1.0 / smooth[level : level + 1]
        for j in range(8):
            rows_j = slice(8 * j, 8 * j + 8)
            sums_new = ema_decay * ema_ref[level, rows_j] + (1.0 - ema_decay) * sums_all[8 * level + j]
            sums_out[0, level, rows_j] = sums_new
            books_out[0, level, rows_j] = sums_new * inverse

    swap_wait("rep", N_REP, step_all, sem_step, True)
    mean_delta = in_order(step_all, N_REP)[0:SHARE] * (1.0 / N_REP)
    momentum_new = outer_moment * mom_ref[...] + mean_delta
    mom_out[...] = momentum_new
    params_out[...] = own - outer_rate * (mean_delta + outer_moment * momentum_new)

    for axis, size, buf, sem in (
        ("dp", N_DP, valid_all, sem_valid), ("dp", N_DP, grad_all, sem_grad), ("dp", N_DP, part_all, sem_part),
        ("dp", N_DP, stat_all, sem_stat), ("rep", N_REP, step_all, sem_step), ("dp", N_DP, sums_all, sem_sums),
    ):
        swap_wait(axis, size, buf, sem, False)


def hand_over(scal, *refs):
    n = (len(refs) - 3) // 2
    ins, (loss_out, valid_out), outs, sems = refs[:n], refs[n : n + 2], refs[n + 2 : -1], refs[-1]
    copies = [pltpu.make_async_copy(a, b, sems.at[i]) for i, (a, b) in enumerate(zip(ins, outs))]
    for c in copies:
        c.start()
    loss_out[0] = scal[0, 0]
    valid_out[0] = scal[1, 0]
    for c in copies:
        c.wait()


def shards(
    pixels, valid_mask, bottom_codes, top_codes, params, first_moment, second_moment, outer_momentum, ema_counts,
    ema_sums, codebooks, *, R,
):
    rows = pixels.shape[0]
    vm = pl.BlockSpec(memory_space=pltpu.VMEM)
    sm = pl.BlockSpec(memory_space=pltpu.SMEM)
    hbm = pl.BlockSpec(memory_space=pl.ANY)
    dma = pltpu.SemaphoreType.DMA
    args = (
        pixels, valid_mask, bottom_codes.reshape(-1, 128), top_codes.reshape(-1, 128), params,
        jnp.swapaxes(first_moment, 0, 1), jnp.swapaxes(second_moment, 0, 1), outer_momentum, ema_counts,
        jnp.swapaxes(ema_sums, 1, 2), jnp.swapaxes(codebooks, 1, 2),
    )
    results = [(SHARE, 128), (SHARE, 1, 128), (SHARE, 1, 128), (SHARE, 128), (1, 2, K), (1, 2, EMB, K), (1, 2, EMB, K)]
    inner = pl.pallas_call(
        functools.partial(kernel, R=R),
        out_shape=tuple(pltpu.VMEM(s, f32) for s in [(8, 128)] + results),
        in_specs=[hbm] * 11,
        out_specs=(vm,) * 8,
        scratch_shapes=[pltpu.VMEM(v.shape, v.dtype) for v in args]
        + scratches(rows, R)
        + [
            pltpu.VMEM((8, 128), f32), pltpu.VMEM((N_DP, 8, 128), f32),
            pltpu.VMEM((8, 128), f32), pltpu.VMEM((N_DP, 8, 128), f32),
            pltpu.VMEM((N_DP, 48, 128), f32), pltpu.VMEM((N_DP, 48, 128), f32),
            pltpu.VMEM((N_DP, 8, 512), f32), pltpu.VMEM((N_DP, 8, 512), f32), pltpu.VMEM((N_DP, 8, 512), f32),
            pltpu.VMEM((N_REP, 48, 128), f32), pltpu.VMEM((N_DP, 48, 128), f32), dma((11,)),
        ]
        + [dma] * 12,
        compiler_params=pltpu.CompilerParams(
            vmem_limit_bytes=60 * 2**20, collective_id=0, has_side_effects=True
        ),
    )(*args)
    shape = lambda *s: jax.ShapeDtypeStruct(s, f32)
    loss, valid, params, first, second, mom, counts, sums, books = pl.pallas_call(
        hand_over,
        out_shape=(shape(1), shape(1)) + tuple(shape(*s) for s in results),
        in_specs=[vm] * 8,
        out_specs=(sm, sm) + (hbm,) * 7,
        scratch_shapes=[dma((7,))],
    )(*(pltpu.with_memory_space_constraint(v, pltpu.VMEM) for v in inner))
    return (
        loss, valid, params, jnp.swapaxes(first, 0, 1), jnp.swapaxes(second, 0, 1), mom, counts,
        jnp.swapaxes(sums, 2, 3), jnp.swapaxes(books, 2, 3),
    )


def solution(mesh):
    return jax.shard_map(
        functools.partial(shards, R=1024),
        mesh=mesh,
        in_specs=(
            P(("rep", "dp"), None),
            P(("rep", "dp"), None),
            P(("rep", "dp")),
            P(("rep", "dp")),
            P(),
            P("rep", "dp", None),
            P("rep", "dp", None),
            P("dp", None),
            P(),
            P(),
            P(),
        ),
        out_specs=(
            P("rep"),
            P("rep"),
            P("dp", None),
            P("rep", "dp", None),
            P("rep", "dp", None),
            P("dp", None),
            P("rep", None, None),
            P("rep", None, None, None),
            P("rep", None, None, None),
        ),
        check_vma=False,
    )
```

```python
import functools
import jax
import jax.numpy as jnp
from jax import lax
from jax.experimental import pallas as pl
from jax.experimental.pallas import tpu as pltpu
from jax.sharding import PartitionSpec as P

PF = 48
EMB = 64
K = 512
STEP = 10
beta_commit = 0.25
ema_decay = 0.8
laplace_eps = 1e-05
inner_rate = 0.03
beta_first = 0.9
beta_second = 0.999
adam_eps = 1e-08
weight_decay = 0.01
outer_rate = 0.7
outer_moment = 0.9

bf16 = jnp.bfloat16
f32 = jnp.float32
O_ENC, O_RU, O_TI, O_DB, O_DT, O_RD, O_L, O_TO, O_OUT, O_END = 0, 48, 112, 368, 432, 496, 560, 624, 688, 736


def nn(a, b):
    return lax.dot_general(a, b, (((1,), (0,)), ((), ())), preferred_element_type=f32)


def nt(a, b):
    return lax.dot_general(a, b, (((1,), (1,)), ((), ())), preferred_element_type=f32)


def tn(a, b):
    return lax.dot_general(a, b, (((0,), (0,)), ((), ())), preferred_element_type=f32)


def split(v):
    hi = v.astype(bf16)
    return hi, (v - hi.astype(f32)).astype(bf16)


def pair(v):
    hi, lo = split(v)
    return jnp.concatenate([hi, lo], axis=1)


def quad(v):
    hi, lo = split(v)
    return jnp.concatenate([hi, hi, lo, lo], axis=1)


def twice(v):
    return jnp.concatenate([v, v], axis=0)


def silu_and_slope(u):
    w = 1.0 + jnp.tanh(u)
    a = u * w
    return a, w + a * (2.0 - w)


def lanes(parts):
    return jnp.concatenate(parts, axis=1)


def spread_codes(codes, per_row):
    a = codes.shape[0]
    rows = a * 128 // per_row
    span = 128 // per_row
    lo = (codes & 255).astype(f32).astype(bf16)
    hi = (codes >> 8).astype(f32).astype(bf16)
    up = (lax.broadcasted_iota(jnp.int32, (a, rows), 0) == lax.broadcasted_iota(jnp.int32, (a, rows), 1) // span)
    up = up.astype(f32).astype(bf16)
    keep = (
        lax.broadcasted_iota(jnp.int32, (128, rows), 0) // per_row
        == lax.broadcasted_iota(jnp.int32, (128, rows), 1) % span
    )
    pick = (
        lax.broadcasted_iota(jnp.int32, (8, 128), 0)
        == lax.broadcasted_iota(jnp.int32, (8, 128), 1) % per_row
    )
    pick = pick.astype(f32).astype(bf16)
    out = []
    for part in (lo, hi):
        wide = jnp.where(keep, tn(part, up), 0.0).astype(bf16)
        out.append(nn(pick, wide))
    return out


def stack(v):
    hi, lo = split(v)
    return jnp.concatenate([hi, lo], axis=0)


def halves(v):
    n = v.shape[0] // 2
    return v[:n] + v[n:]


def exact(a, b, dims):
    return lax.dot_general(a, b, ((dims), ((), ())), precision=lax.Precision.HIGHEST, preferred_element_type=f32)


WS = {
    "enc_f": (128, 96), "rd_f": (128, 128), "l_f": (128, 192), "ti_f": (128, 512), "to_f": (128, 128), "db_f": (128, 256),
    "dt_f": (128, 256), "out_f": (96, 128), "out_b": (128, 96), "db_b": (64, 256), "dt_b": (128, 128), "to_b": (128, 128),
    "ti_b": (256, 256), "ru_b": (64, 128), "he_b": (128, 256), "book_b": (256, 256), "book_t": (256, 256),
}
KEEP = {
    "x": (48, 8, f32), "xb": (48, 8, bf16), "he": (128, 8, bf16), "de": (128, 8, bf16), "ar": (64, 8, bf16), "dr": (64, 8, bf16),
    "gap_b": (64, 8, bf16), "gl": (64, 8, f32), "both": (128, 8, bf16), "hd": (128, 8, bf16), "gr": (48, 8, bf16),
    "gpd": (128, 8, bf16), "qb": (128, 8, bf16),
}
KEEP_TOP = {
    "ti": (256, bf16), "ht": (128, bf16), "dt": (128, bf16), "gap_t": (64, f32), "gt": (64, f32), "qt": (128, bf16), "gtr": (128, bf16),
    "glt": (64, bf16), "gpt": (128, bf16),
}
ACC = {
    "e": (128, 48), "he": (128, 128), "ar": (64, 64), "db": (128, 128), "out": (128, 48), "sum_b": (144, 256), "sum_t": (144, 256),
}


def weights(par, book_ref, w):
    part = par.T
    f = lambda lo, hi: par[lo:hi]
    t = lambda lo, hi: part[:, lo:hi]
    cross = exact(f(O_L, O_TO), f(O_RU, O_TI), ((1,), (1,)))
    w["enc_f"][...] = pair(0.5 * t(O_ENC, O_RU))
    w["rd_f"][...] = stack(0.5 * f(O_RD, O_L))
    w["l_f"][...] = stack(lanes([f(O_L, O_TO), cross]))
    w["ti_f"][...] = pair(0.5 * t(O_TI, O_DB))
    w["to_f"][...] = stack(f(O_TO, O_OUT))
    w["db_f"][...] = quad(0.5 * t(O_DB, O_DT))
    w["dt_f"][...] = quad(0.5 * t(O_DT, O_RD))
    w["out_f"][...] = stack(f(O_OUT, O_END))
    w["out_b"][...] = pair(0.5 * t(O_OUT, O_END))
    w["db_b"][...] = pair(f(O_DB, O_DT))
    w["dt_b"][...] = stack(f(O_DT, O_RD))
    w["to_b"][...] = pair(0.5 * t(O_TO, O_OUT))
    w["ti_b"][...] = pair(f(O_TI, O_DB))
    w["ru_b"][...] = pair(0.5 * exact(f(O_RU, O_TI), f(O_L, O_TO), ((1,), (1,))))
    w["he_b"][...] = pair(0.5 * lanes([t(O_L, O_TO), t(O_RD, O_L)]))
    for level, name in enumerate(("book_b", "book_t")):
        w[name][...] = jnp.concatenate([stack(book_ref[level][:, 256 * a : 256 * a + 256]) for a in (0, 1)], axis=0)


def code_keys(rows_ref, cols_ref, src, per):
    lo, hi = spread_codes(src[...], per)
    rows_ref[0] = lo
    rows_ref[1] = hi
    cols_ref[...] = lo.T


def high_bits(codes, level, n, at, R):
    return lanes([codes[level][0][1, p : p + 1, pl.ds(at, R)] for p in range(n)])


def first(i, size):
    return i * size if isinstance(i, int) else pl.multiple_of(i * size, size)


def hot(equal):
    return jnp.where(equal, jnp.ones((), bf16), jnp.zeros((), bf16))


def encoder(i, R, x_ref, codes, w, keep, acc):
    along = lax.broadcasted_iota(jnp.int32, (R, 256), 1).astype(f32).astype(bf16)
    at = first(i, R)
    tops = pl.ds(first(i, 2 * R), 2 * R)

    def scatter(level, n, latent):
        key = codes[level][1][pl.ds(at, R), :]
        low = jnp.concatenate([
            hot(along == jnp.broadcast_to(key[:, p : p + 1], (R, 256)).astype(bf16)) for p in range(n)
        ], axis=0)
        high = high_bits(codes, level, n, at, R).astype(bf16)
        ones = jnp.broadcast_to(high, latent.shape) * latent
        row = lax.broadcasted_iota(jnp.int32, (16, n * R), 0)
        count = jnp.where(row == 0, 1.0 - high.astype(f32), jnp.where(row == 1, high.astype(f32), 0.0)).astype(bf16)
        return nn(jnp.concatenate([latent - ones, ones, count], axis=0), low)

    xt = x_ref[pl.ds(at, R), :].T
    x = lanes([xt[48 * p : 48 * p + 48] for p in range(8)])
    keep["x"][i] = x
    xb = x.astype(bf16)
    keep["xb"][i] = xb
    he, de = silu_and_slope(nn(w["enc_f"][...], twice(xb)))
    heb = he.astype(bf16)
    keep["he"][i] = heb
    keep["de"][i] = de.astype(bf16)
    ar, dr = silu_and_slope(halves(nn(w["rd_f"][...], heb)))
    arb = ar.astype(bf16)
    keep["ar"][i] = arb
    keep["dr"][i] = dr.astype(bf16)
    lbb = halves(nn(w["l_f"][...], jnp.concatenate([heb, arb], axis=0))).astype(bf16)
    ti = lanes([
        jnp.concatenate([lbb[:, R * p : R * p + R] for p in range(4 * g, 4 * g + 4)], axis=0) for g in (0, 1)
    ])
    keep["ti"][:, tops] = ti
    ht, dt = silu_and_slope(nn(w["ti_f"][...], twice(ti)))
    htb = ht.astype(bf16)
    keep["ht"][:, tops] = htb
    keep["dt"][:, tops] = dt.astype(bf16)
    lt = halves(nn(w["to_f"][...], htb))
    keep["gap_t"][:, tops] = lt
    acc["sum_b"][...] += scatter(0, 8, lbb)
    acc["sum_t"][...] += scatter(1, 2, lt.astype(bf16))


def decoder(i, R, m_ref, codes, w, keep, acc, lacc):
    down = lax.broadcasted_iota(jnp.int32, (256, R), 0).astype(f32).astype(bf16)
    at = first(i, R)
    tops = pl.ds(first(i, 2 * R), 2 * R)

    def gather(level, n, book):
        key = codes[level][0][0, :, pl.ds(at, R)]
        low = lanes([hot(down == key[p : p + 1, :].astype(bf16)) for p in range(n)])
        both = nn(book, low)
        return jnp.where(high_bits(codes, level, n, at, R) > 0.5, both[128:], both[:128]).astype(bf16)

    mt = m_ref[pl.ds(at, R), :].astype(f32).T
    m = lanes([mt[48 * p : 48 * p + 48] for p in range(8)])
    qb2 = gather(0, 8, w["book_b"][...])
    qt2 = gather(1, 2, w["book_t"][...])
    ti = keep["ti"][:, tops]
    lb = lanes([ti[64 * (p % 4) : 64 * (p % 4) + 64, R * (p // 4) : R * (p // 4) + R] for p in range(8)]).astype(f32)
    gap_b = lb - halves(qb2.astype(f32))
    gap_t = keep["gap_t"][:, tops] - halves(qt2.astype(f32))
    keep["gap_b"][i] = gap_b.astype(bf16)
    keep["gap_t"][:, tops] = gap_t
    top = nn(w["dt_f"][...], twice(qt2))
    pre = nn(w["db_f"][...], twice(qb2)) + lanes([top[:, R * (p // 4) : R * (p // 4) + R] for p in range(8)])
    hd, dd = silu_and_slope(pre)
    hdb = hd.astype(bf16)
    err = halves(nn(w["out_f"][...], hdb)) - keep["x"][i]
    me = m * err
    lacc[0:48] += sum((me * err)[:, R * p : R * p + R] for p in range(8))
    lacc[48:112] += sum((gap_b * gap_b)[:, R * p : R * p + R] for p in range(8))
    lacc[112:176] += sum((gap_t * gap_t)[:, R * p : R * p + R] for p in range(2))
    grb = me.astype(bf16)
    gpd = nn(w["out_b"][...], twice(grb)) * dd
    gpdb = gpd.astype(bf16)
    gtrb = lanes([sum(gpd[:, R * p : R * p + R] for p in range(4 * g_, 4 * g_ + 4)) for g_ in (0, 1)]).astype(bf16)
    keep["gt"][:, tops] = halves(nn(w["dt_b"][...], gtrb))
    keep["gl"][i] = nn(w["db_b"][...], twice(gpdb))
    keep["hd"][i] = hdb
    keep["gr"][i] = grb
    keep["gpd"][i] = gpdb
    keep["qb"][i] = qb2
    keep["qt"][:, tops] = qt2
    keep["gtr"][:, tops] = gtrb


def top_backward(n, R, kt, w, keep):
    gltb = (keep["gt"][...] + kt * keep["gap_t"][...]).astype(bf16)
    keep["glt"][...] = gltb
    gptb = (nn(w["to_b"][...], twice(gltb)) * keep["dt"][...].astype(f32)).astype(bf16)
    keep["gpt"][...] = gptb
    gti = nn(w["ti_b"][...], twice(gptb))
    for i in range(n):
        for p in range(8):
            at = 2 * R * i + R * (p // 4)
            keep["gl"][i, :, R * p : R * p + R] += gti[64 * (p % 4) : 64 * (p % 4) + 64, at : at + R]


def backward_inner(i, kb, w, keep, acc):
    glbb = (keep["gl"][i] + kb * keep["gap_b"][i].astype(f32)).astype(bf16)
    gprb = (nn(w["ru_b"][...], twice(glbb)) * keep["dr"][i].astype(f32)).astype(bf16)
    both = jnp.concatenate([glbb, gprb], axis=0)
    keep["both"][i] = both
    acc["ar"][...] += nt(glbb, keep["ar"][i])


def backward_outer(i, w, keep, acc):
    gpeb = (nn(w["he_b"][...], twice(keep["both"][i])) * keep["de"][i].astype(f32)).astype(bf16)
    acc["e"][...] += nt(gpeb, keep["xb"][i])


def add(ref, v):
    ref[...] += v


def scratches(rows, R):
    return (
        [pltpu.VMEM(s, bf16) for s in WS.values()]
        + [pltpu.VMEM((rows // R, c, n * R), t) for c, n, t in KEEP.values()]
        + [pltpu.VMEM((c, rows * 2), t) for c, t in KEEP_TOP.values()]
        + [pltpu.VMEM(s, f32) for s in ACC.values()]
        + [pltpu.VMEM((2, 8, rows), f32), pltpu.VMEM((rows, 8), f32)] * 2
        + [pltpu.VMEM((176, R), f32)]
    )


def unscratch(scratch):
    scratch = list(scratch)
    take = lambda names: {k: scratch.pop(0) for k in names}
    w, keep, acc = take(WS), take(list(KEEP) + list(KEEP_TOP)), take(ACC)
    codes = ((scratch.pop(0), scratch.pop(0)), (scratch.pop(0), scratch.pop(0)))
    return w, keep, acc, codes, scratch


def swap_start(axis, n, src_at, buf, sems, at=0):
    me = lax.axis_index(axis)

    def go(peer, carry):
        @pl.when(peer != me)
        def _():
            pltpu.make_async_remote_copy(
                src_ref=src_at(peer), dst_ref=buf.at[me], send_sem=sems[0], recv_sem=sems[1],
                device_id={axis: peer}, device_id_type=pl.DeviceIdType.MESH,
            ).start()

        return carry

    lax.fori_loop(at, n, go, 0)


def swap_wait(axis, n, buf, sems, recv):
    others = buf.at[0 : n - 1]
    copy = pltpu.make_async_remote_copy(
        src_ref=others, dst_ref=others, send_sem=sems[0], recv_sem=sems[1],
        device_id={axis: lax.axis_index(axis)}, device_id_type=pl.DeviceIdType.MESH,
    )
    if recv:
        copy.wait_recv()
    else:
        copy.wait_send()


def total(v):
    while v.shape[0] % 16 == 0:
        v = halves(v)
    return jnp.sum(jnp.sum(v, axis=0, keepdims=True), axis=1, keepdims=True)


def in_order(buf, n):
    out = buf[0]
    for s in range(1, n):
        out = out + buf[s]
    return out

N_DP = 16
N_REP = 8
SHARE = 46
FIRST = 1
def share_start(shares, src, buf, sems):
    me = lax.axis_index("dp")
    for s in shares:
        @pl.when(me != s)
        def _():
            pltpu.make_async_remote_copy(
                src_ref=src.at[s], dst_ref=buf.at[me], send_sem=sems[0], recv_sem=sems[1],
                device_id={"dp": s}, device_id_type=pl.DeviceIdType.MESH,
            ).start()


def put_rows(ref, at, v):
    end = at + v.shape[0]
    for s in range(N_DP):
        lo, hi = max(at, SHARE * s), min(end, SHARE * s + SHARE)
        if lo < hi:
            ref[s, lo - SHARE * s : hi - SHARE * s] = v[lo - at : hi - at]


def each(n, f):
    if n == 1:
        f(0)
        return

    def go(i, carry):
        f(i)
        return carry

    lax.fori_loop(0, n, go, 0)


def kernel(*refs, R):
    sources, refs = refs[:11], refs[11:]
    (scal_out, params_out, first_out, second_out, mom_out, counts_out, sums_out, books_out), scratch = refs[:8], refs[8:]
    inputs, scratch = scratch[:11], scratch[11:]
    x_ref, m_ref, cb_ref, ct_ref, p_ref, first_ref, second_ref, mom_ref, cnt_ref, ema_ref, book_ref = inputs
    w, keep, acc, codes, scratch = unscratch(scratch)
    (
        lacc, valid_own, valid_all, stat_own, stat_all, grad_own, grad_all, part_own, part_all, sums_all, step_all,
        par_share, in_sems, *sems,
    ) = scratch
    loads = [pltpu.make_async_copy(a, b, in_sems.at[i]) for i, (a, b) in enumerate(zip(sources, inputs))]
    load_x, load_m, load_cb, load_ct, load_p, *load_rest, load_book = loads
    for load in (load_p, load_x, load_cb, load_ct, load_book, load_m, *load_rest):
        load.start()
    sems = [(sems[2 * i], sems[2 * i + 1]) for i in range(6)]
    sem_valid, sem_stat, sem_grad, sem_part, sem_sums, sem_step = sems
    dp = lax.axis_index("dp")
    rep = lax.axis_index("rep")
    rows = x_ref.shape[0]
    n = rows // R

    barrier = pltpu.get_barrier_semaphore()
    for axis, size, me in (("dp", N_DP, dp), ("rep", N_REP, rep)):
        def hello(k, carry):
            pl.semaphore_signal(
                barrier, inc=1, device_id={axis: lax.rem(me + k, size)}, device_id_type=pl.DeviceIdType.MESH
            )
            return carry

        lax.fori_loop(1, size, hello, 0)

    for load in (load_p, load_book, load_cb, load_ct):
        load.wait()
    weights(p_ref[...], book_ref, w)
    code_keys(*codes[0], cb_ref, 8)
    code_keys(*codes[1], ct_ref, 2)
    for v in acc.values():
        v[...] = jnp.zeros_like(v)
    lacc[...] = jnp.zeros_like(lacc)
    load_x.wait()
    each(n, lambda i: encoder(i, R, x_ref, codes, w, keep, acc))

    load_m.wait()
    valid_own[...] = jnp.broadcast_to(total(m_ref[...].astype(f32)), (8, 128))
    valid_all[dp] = valid_own[...]
    valid_src = lambda peer: valid_own
    pl.semaphore_wait(barrier, N_DP + N_REP - 2)
    swap_start("dp", N_DP, valid_src, valid_all, sem_valid)

    for d in range(N_DP):
        name, at = ("sum_b", "sum_t")[d // 8], 8 * (d % 8)
        part_own[d] = lanes([acc[name][at : at + 8], acc[name][64 + at : 72 + at]])
    part_src = lambda peer: part_own.at[peer]
    swap_start("dp", N_DP, part_src, part_all, sem_part)
    stat_own[...] = jnp.concatenate(
        [
            acc[name][128 + a : 129 + a, 128 * j : 128 * j + 128]
            for name in ("sum_b", "sum_t") for a in (0, 1) for j in (0, 1)
        ], axis=0
    )
    stat_src = lambda peer: stat_own
    swap_start("dp", N_DP, stat_src, stat_all, sem_stat)
    part_all[dp] = part_own[dp]
    stat_all[dp] = stat_own[...]

    each(n, lambda i: decoder(i, R, m_ref, codes, w, keep, acc, lacc))

    group_rows = rows * 8 * N_DP
    swap_wait("dp", N_DP, valid_all, sem_valid, True)
    count = in_order(valid_all, N_DP)[0:1, 0:1]
    scale = 2.0 / count
    kb = beta_commit / (group_rows * EMB) * count
    kt = beta_commit / (group_rows // 4 * EMB) * count
    lane = lax.broadcasted_iota(jnp.int32, (1, 128), 1)
    losses = jnp.where(lane == 0, total(lacc[0:48]), jnp.where(lane == 1, total(lacc[48:112]), total(lacc[112:176])))
    for s in range(N_DP):
        grad_own[s, SHARE:48] = jnp.broadcast_to(losses, (48 - SHARE, 128))
    top_backward(n, R, kt, w, keep)
    each(n, lambda i: backward_inner(i, kb, w, keep, acc))
    each(n, lambda i: backward_outer(i, w, keep, acc))
    cross = acc["ar"][...]
    put_rows(grad_own, O_ENC, acc["e"][...].T * scale)
    put_rows(grad_own, O_RU, exact(cross, p_ref[O_L:O_TO], ((0,), (0,))) * scale)
    share_start((0, 1), grad_own, grad_all, sem_grad)
    put_rows(grad_own, O_TI, nt(keep["ti"][...], keep["gpt"][...]) * scale)
    share_start((2, 3, 4, 5, 6, 7), grad_own, grad_all, sem_grad)
    each(n, lambda i: add(acc["db"], nt(keep["qb"][i], keep["gpd"][i])))
    put_rows(grad_own, O_DB, halves(acc["db"][...]) * scale)
    put_rows(grad_own, O_DT, halves(nt(keep["qt"][...], keep["gtr"][...])) * scale)
    each(n, lambda i: add(acc["he"], nt(keep["both"][i], keep["he"][i])))
    put_rows(grad_own, O_RD, acc["he"][64:128] * scale)
    put_rows(grad_own, O_L, (acc["he"][0:64] + exact(cross, p_ref[O_RU:O_TI], ((1,), (0,)))) * scale)
    put_rows(grad_own, O_TO, nt(keep["ht"][...], keep["glt"][...]).T * scale)
    share_start((8, 9, 12, 13, 10, 11), grad_own, grad_all, sem_grad)
    each(n, lambda i: add(acc["out"], nt(keep["hd"][i], keep["gr"][i])))
    put_rows(grad_own, O_OUT, acc["out"][...].T * scale)
    share_start((14, 15), grad_own, grad_all, sem_grad)
    grad_all[dp] = grad_own[dp]

    for load in load_rest:
        load.wait()
    for s in range(N_DP):
        par_share[s, 0:SHARE] = p_ref[SHARE * s : SHARE * s + SHARE]
    swap_wait("dp", N_DP, part_all, sem_part, True)
    sums_all[dp] = in_order(part_all, N_DP)
    sums_src = lambda peer: sums_all.at[dp]
    swap_start("dp", FIRST, sums_src, sums_all, sem_sums)
    swap_wait("dp", N_DP, stat_all, sem_stat, True)
    stats = in_order(stat_all, N_DP)
    seen = jnp.concatenate([lanes([stats[4 * level + j : 4 * level + j + 1] for j in range(4)]) for level in (0, 1)], axis=0)
    counts_new = ema_decay * cnt_ref[...] + (1.0 - ema_decay) * seen
    counts_out[0] = counts_new
    totals = jnp.sum(counts_new, axis=1, keepdims=True)
    smooth = (counts_new + laplace_eps) / (totals + K * laplace_eps) * totals
    swap_wait("dp", N_DP, grad_all, sem_grad, True)
    summed = in_order(grad_all, N_DP)
    grads = summed[0:SHARE]
    own = par_share[dp][0:SHARE]
    first_new = beta_first * first_ref[:, 0, :] + (1.0 - beta_first) * grads
    second_new = beta_second * second_ref[:, 0, :] + (1.0 - beta_second) * grads * grads
    bias_first = 1.0 - beta_first**STEP
    bias_second = 1.0 - beta_second**STEP
    step_here = inner_rate * (
        first_new / bias_first / (jnp.sqrt(second_new / bias_second) + adam_eps) + weight_decay * own
    )
    step_all[rep, 0:SHARE] = step_here
    step_all[rep, SHARE:48] = jnp.zeros((48 - SHARE, 128), f32)
    step_src = lambda peer: step_all.at[rep]
    swap_start("rep", N_REP, step_src, step_all, sem_step)
    swap_start("dp", N_DP, sums_src, sums_all, sem_sums, FIRST)

    first_out[:, 0, :] = first_new
    second_out[:, 0, :] = second_new

    terms = summed[SHARE : SHARE + 1]
    loss = terms[:, 0:1] / count + beta_commit * (
        terms[:, 1:2] / (group_rows * EMB) + terms[:, 2:3] / (group_rows // 4 * EMB)
    )
    scal_out[...] = jnp.concatenate([jnp.broadcast_to(loss, (1, 128)), jnp.broadcast_to(count, (1, 128)), jnp.zeros((6, 128), f32)], axis=0)

    swap_wait("dp", N_DP, sums_all, sem_sums, True)
    for level in (0, 1):
        inverse = 1.0 / smooth[level : level + 1]
        for j in range(8):
            rows_j = slice(8 * j, 8 * j + 8)
            sums_new = ema_decay * ema_ref[level, rows_j] + (1.0 - ema_decay) * sums_all[8 * level + j]
            sums_out[0, level, rows_j] = sums_new
            books_out[0, level, rows_j] = sums_new * inverse

    swap_wait("rep", N_REP, step_all, sem_step, True)
    mean_delta = in_order(step_all, N_REP)[0:SHARE] * (1.0 / N_REP)
    momentum_new = outer_moment * mom_ref[...] + mean_delta
    mom_out[...] = momentum_new
    params_out[...] = own - outer_rate * (mean_delta + outer_moment * momentum_new)

    for axis, size, buf, sem in (
        ("dp", N_DP, valid_all, sem_valid), ("dp", N_DP, grad_all, sem_grad), ("dp", N_DP, part_all, sem_part),
        ("dp", N_DP, stat_all, sem_stat), ("rep", N_REP, step_all, sem_step), ("dp", N_DP, sums_all, sem_sums),
    ):
        swap_wait(axis, size, buf, sem, False)


def hand_over(scal, *refs):
    n = (len(refs) - 3) // 2
    ins, (loss_out, valid_out), outs, sems = refs[:n], refs[n : n + 2], refs[n + 2 : -1], refs[-1]
    copies = [pltpu.make_async_copy(a, b, sems.at[i]) for i, (a, b) in enumerate(zip(ins, outs))]
    for c in copies:
        c.start()
    loss_out[0] = scal[0, 0]
    valid_out[0] = scal[1, 0]
    for c in copies:
        c.wait()


def shards(
    pixels, valid_mask, bottom_codes, top_codes, params, first_moment, second_moment, outer_momentum, ema_counts,
    ema_sums, codebooks, *, R,
):
    rows = pixels.shape[0]
    vm = pl.BlockSpec(memory_space=pltpu.VMEM)
    sm = pl.BlockSpec(memory_space=pltpu.SMEM)
    hbm = pl.BlockSpec(memory_space=pl.ANY)
    dma = pltpu.SemaphoreType.DMA
    args = (
        pixels, valid_mask, bottom_codes.reshape(-1, 128), top_codes.reshape(-1, 128), params,
        jnp.swapaxes(first_moment, 0, 1), jnp.swapaxes(second_moment, 0, 1), outer_momentum, ema_counts,
        jnp.swapaxes(ema_sums, 1, 2), jnp.swapaxes(codebooks, 1, 2),
    )
    results = [(SHARE, 128), (SHARE, 1, 128), (SHARE, 1, 128), (SHARE, 128), (1, 2, K), (1, 2, EMB, K), (1, 2, EMB, K)]
    inner = pl.pallas_call(
        functools.partial(kernel, R=R),
        out_shape=tuple(pltpu.VMEM(s, f32) for s in [(8, 128)] + results),
        in_specs=[hbm] * 11,
        out_specs=(vm,) * 8,
        scratch_shapes=[pltpu.VMEM(v.shape, v.dtype) for v in args]
        + scratches(rows, R)
        + [
            pltpu.VMEM((8, 128), f32), pltpu.VMEM((N_DP, 8, 128), f32),
            pltpu.VMEM((8, 128), f32), pltpu.VMEM((N_DP, 8, 128), f32),
            pltpu.VMEM((N_DP, 48, 128), f32), pltpu.VMEM((N_DP, 48, 128), f32),
            pltpu.VMEM((N_DP, 8, 512), f32), pltpu.VMEM((N_DP, 8, 512), f32), pltpu.VMEM((N_DP, 8, 512), f32),
            pltpu.VMEM((N_REP, 48, 128), f32), pltpu.VMEM((N_DP, 48, 128), f32), dma((11,)),
        ]
        + [dma] * 12,
        compiler_params=pltpu.CompilerParams(
            vmem_limit_bytes=60 * 2**20, collective_id=0, has_side_effects=True
        ),
    )(*args)
    shape = lambda *s: jax.ShapeDtypeStruct(s, f32)
    loss, valid, params, first, second, mom, counts, sums, books = pl.pallas_call(
        hand_over,
        out_shape=(shape(1), shape(1)) + tuple(shape(*s) for s in results),
        in_specs=[vm] * 8,
        out_specs=(sm, sm) + (hbm,) * 7,
        scratch_shapes=[dma((7,))],
    )(*(pltpu.with_memory_space_constraint(v, pltpu.VMEM) for v in inner))
    return (
        loss, valid, params, jnp.swapaxes(first, 0, 1), jnp.swapaxes(second, 0, 1), mom, counts,
        jnp.swapaxes(sums, 2, 3), jnp.swapaxes(books, 2, 3),
    )


def solution(mesh):
    return jax.shard_map(
        functools.partial(shards, R=1024),
        mesh=mesh,
        in_specs=(
            P(("rep", "dp"), None),
            P(("rep", "dp"), None),
            P(("rep", "dp")),
            P(("rep", "dp")),
            P(),
            P("rep", "dp", None),
            P("rep", "dp", None),
            P("dp", None),
            P(),
            P(),
            P(),
        ),
        out_specs=(
            P("rep"),
            P("rep"),
            P("dp", None),
            P("rep", "dp", None),
            P("rep", "dp", None),
            P("dp", None),
            P("rep", None, None),
            P("rep", None, None, None),
            P("rep", None, None, None),
        ),
        check_vma=False,
    )
```

```python
import functools
import jax
import jax.numpy as jnp
from jax import lax
from jax.experimental import pallas as pl
from jax.experimental.pallas import tpu as pltpu
from jax.sharding import PartitionSpec as P

PF = 48
EMB = 64
K = 512
STEP = 10
beta_commit = 0.25
ema_decay = 0.8
laplace_eps = 1e-05
inner_rate = 0.03
beta_first = 0.9
beta_second = 0.999
adam_eps = 1e-08
weight_decay = 0.01
outer_rate = 0.7
outer_moment = 0.9

bf16 = jnp.bfloat16
f32 = jnp.float32
O_ENC, O_RU, O_TI, O_DB, O_DT, O_RD, O_L, O_TO, O_OUT, O_END = 0, 48, 112, 368, 432, 496, 560, 624, 688, 736


def nn(a, b):
    return lax.dot_general(a, b, (((1,), (0,)), ((), ())), preferred_element_type=f32)


def nt(a, b):
    return lax.dot_general(a, b, (((1,), (1,)), ((), ())), preferred_element_type=f32)


def tn(a, b):
    return lax.dot_general(a, b, (((0,), (0,)), ((), ())), preferred_element_type=f32)


def split(v):
    hi = v.astype(bf16)
    return hi, (v - hi.astype(f32)).astype(bf16)


def pair(v):
    hi, lo = split(v)
    return jnp.concatenate([hi, lo], axis=1)


def quad(v):
    hi, lo = split(v)
    return jnp.concatenate([hi, hi, lo, lo], axis=1)


def twice(v):
    return jnp.concatenate([v, v], axis=0)


def silu_and_slope(u):
    w = 1.0 + jnp.tanh(u)
    a = u * w
    return a, w + a * (2.0 - w)


def lanes(parts):
    return jnp.concatenate(parts, axis=1)


def spread_codes(codes, per_row):
    a = codes.shape[0]
    rows = a * 128 // per_row
    span = 128 // per_row
    lo = (codes & 255).astype(f32).astype(bf16)
    hi = (codes >> 8).astype(f32).astype(bf16)
    up = (lax.broadcasted_iota(jnp.int32, (a, rows), 0) == lax.broadcasted_iota(jnp.int32, (a, rows), 1) // span)
    up = up.astype(f32).astype(bf16)
    keep = (
        lax.broadcasted_iota(jnp.int32, (128, rows), 0) // per_row
        == lax.broadcasted_iota(jnp.int32, (128, rows), 1) % span
    )
    pick = (
        lax.broadcasted_iota(jnp.int32, (8, 128), 0)
        == lax.broadcasted_iota(jnp.int32, (8, 128), 1) % per_row
    )
    pick = pick.astype(f32).astype(bf16)
    out = []
    for part in (lo, hi):
        wide = jnp.where(keep, tn(part, up), 0.0).astype(bf16)
        out.append(nn(pick, wide))
    return out


def stack(v):
    hi, lo = split(v)
    return jnp.concatenate([hi, lo], axis=0)


def halves(v):
    n = v.shape[0] // 2
    return v[:n] + v[n:]


def exact(a, b, dims):
    return lax.dot_general(a, b, ((dims), ((), ())), precision=lax.Precision.HIGHEST, preferred_element_type=f32)


WS = {
    "enc_f": (128, 96), "rd_f": (128, 128), "l_f": (128, 192), "ti_f": (128, 512), "to_f": (128, 128), "db_f": (128, 256),
    "dt_f": (128, 256), "out_f": (96, 128), "out_b": (128, 96), "db_b": (64, 256), "dt_b": (128, 128), "to_b": (128, 128),
    "ti_b": (256, 256), "ru_b": (64, 128), "he_b": (128, 256), "book_b": (256, 256), "book_t": (256, 256),
}
KEEP = {
    "x": (48, 8, f32), "xb": (48, 8, bf16), "he": (128, 8, bf16), "de": (128, 8, bf16), "ar": (64, 8, bf16), "dr": (64, 8, bf16),
    "gap_b": (64, 8, bf16), "gl": (64, 8, f32), "both": (128, 8, bf16), "hd": (128, 8, bf16), "gr": (48, 8, bf16),
    "gpd": (128, 8, bf16), "qb": (128, 8, bf16),
}
KEEP_TOP = {
    "ti": (256, bf16), "ht": (128, bf16), "dt": (128, bf16), "gap_t": (64, f32), "gt": (64, f32), "qt": (128, bf16), "gtr": (128, bf16),
    "glt": (64, bf16), "gpt": (128, bf16),
}
ACC = {
    "e": (128, 48), "he": (128, 128), "ar": (64, 64), "db": (128, 128), "out": (128, 48), "sum_b": (144, 256), "sum_t": (144, 256),
}


def weights(par, book_ref, w):
    part = par.T
    f = lambda lo, hi: par[lo:hi]
    t = lambda lo, hi: part[:, lo:hi]
    cross = exact(f(O_L, O_TO), f(O_RU, O_TI), ((1,), (1,)))
    w["enc_f"][...] = pair(0.5 * t(O_ENC, O_RU))
    w["rd_f"][...] = stack(0.5 * f(O_RD, O_L))
    w["l_f"][...] = stack(lanes([f(O_L, O_TO), cross]))
    w["ti_f"][...] = pair(0.5 * t(O_TI, O_DB))
    w["to_f"][...] = stack(f(O_TO, O_OUT))
    w["db_f"][...] = quad(0.5 * t(O_DB, O_DT))
    w["dt_f"][...] = quad(0.5 * t(O_DT, O_RD))
    w["out_f"][...] = stack(f(O_OUT, O_END))
    w["out_b"][...] = pair(0.5 * t(O_OUT, O_END))
    w["db_b"][...] = pair(f(O_DB, O_DT))
    w["dt_b"][...] = stack(f(O_DT, O_RD))
    w["to_b"][...] = pair(0.5 * t(O_TO, O_OUT))
    w["ti_b"][...] = pair(f(O_TI, O_DB))
    w["ru_b"][...] = pair(0.5 * exact(f(O_RU, O_TI), f(O_L, O_TO), ((1,), (1,))))
    w["he_b"][...] = pair(0.5 * lanes([t(O_L, O_TO), t(O_RD, O_L)]))
    for level, name in enumerate(("book_b", "book_t")):
        w[name][...] = jnp.concatenate([stack(book_ref[level][:, 256 * a : 256 * a + 256]) for a in (0, 1)], axis=0)


def code_keys(rows_ref, cols_ref, src, per):
    lo, hi = spread_codes(src[...], per)
    rows_ref[0] = lo
    rows_ref[1] = hi
    cols_ref[...] = lo.T


def high_bits(codes, level, n, at, R):
    return lanes([codes[level][0][1, p : p + 1, pl.ds(at, R)] for p in range(n)])


def first(i, size):
    return i * size if isinstance(i, int) else pl.multiple_of(i * size, size)


def hot(equal):
    return jnp.where(equal, jnp.ones((), bf16), jnp.zeros((), bf16))


def encoder(i, R, x_ref, codes, w, keep, acc):
    along = lax.broadcasted_iota(jnp.int32, (R, 256), 1).astype(f32).astype(bf16)
    at = first(i, R)
    tops = pl.ds(first(i, 2 * R), 2 * R)

    def scatter(level, n, latent):
        key = codes[level][1][pl.ds(at, R), :]
        low = jnp.concatenate([
            hot(along == jnp.broadcast_to(key[:, p : p + 1], (R, 256)).astype(bf16)) for p in range(n)
        ], axis=0)
        high = high_bits(codes, level, n, at, R).astype(bf16)
        ones = jnp.broadcast_to(high, latent.shape) * latent
        row = lax.broadcasted_iota(jnp.int32, (16, n * R), 0)
        count = jnp.where(row == 0, 1.0 - high.astype(f32), jnp.where(row == 1, high.astype(f32), 0.0)).astype(bf16)
        return nn(jnp.concatenate([latent - ones, ones, count], axis=0), low)

    xt = x_ref[pl.ds(at, R), :].T
    x = lanes([xt[48 * p : 48 * p + 48] for p in range(8)])
    keep["x"][i] = x
    xb = x.astype(bf16)
    keep["xb"][i] = xb
    he, de = silu_and_slope(nn(w["enc_f"][...], twice(xb)))
    heb = he.astype(bf16)
    keep["he"][i] = heb
    keep["de"][i] = de.astype(bf16)
    ar, dr = silu_and_slope(halves(nn(w["rd_f"][...], heb)))
    arb = ar.astype(bf16)
    keep["ar"][i] = arb
    keep["dr"][i] = dr.astype(bf16)
    lbb = halves(nn(w["l_f"][...], jnp.concatenate([heb, arb], axis=0))).astype(bf16)
    ti = lanes([
        jnp.concatenate([lbb[:, R * p : R * p + R] for p in range(4 * g, 4 * g + 4)], axis=0) for g in (0, 1)
    ])
    keep["ti"][:, tops] = ti
    ht, dt = silu_and_slope(nn(w["ti_f"][...], twice(ti)))
    htb = ht.astype(bf16)
    keep["ht"][:, tops] = htb
    keep["dt"][:, tops] = dt.astype(bf16)
    lt = halves(nn(w["to_f"][...], htb))
    keep["gap_t"][:, tops] = lt
    acc["sum_b"][...] += scatter(0, 8, lbb)
    acc["sum_t"][...] += scatter(1, 2, lt.astype(bf16))


def decoder(i, R, m_ref, codes, w, keep, acc, lacc):
    down = lax.broadcasted_iota(jnp.int32, (256, R), 0).astype(f32).astype(bf16)
    at = first(i, R)
    tops = pl.ds(first(i, 2 * R), 2 * R)

    def gather(level, n, book):
        key = codes[level][0][0, :, pl.ds(at, R)]
        low = lanes([hot(down == key[p : p + 1, :].astype(bf16)) for p in range(n)])
        both = nn(book, low)
        return jnp.where(high_bits(codes, level, n, at, R) > 0.5, both[128:], both[:128]).astype(bf16)

    mt = m_ref[pl.ds(at, R), :].astype(f32).T
    m = lanes([mt[48 * p : 48 * p + 48] for p in range(8)])
    qb2 = gather(0, 8, w["book_b"][...])
    qt2 = gather(1, 2, w["book_t"][...])
    ti = keep["ti"][:, tops]
    lb = lanes([ti[64 * (p % 4) : 64 * (p % 4) + 64, R * (p // 4) : R * (p // 4) + R] for p in range(8)]).astype(f32)
    gap_b = lb - halves(qb2.astype(f32))
    gap_t = keep["gap_t"][:, tops] - halves(qt2.astype(f32))
    keep["gap_b"][i] = gap_b.astype(bf16)
    keep["gap_t"][:, tops] = gap_t
    top = nn(w["dt_f"][...], twice(qt2))
    pre = nn(w["db_f"][...], twice(qb2)) + lanes([top[:, R * (p // 4) : R * (p // 4) + R] for p in range(8)])
    hd, dd = silu_and_slope(pre)
    hdb = hd.astype(bf16)
    err = halves(nn(w["out_f"][...], hdb)) - keep["x"][i]
    me = m * err
    lacc[0:48] += sum((me * err)[:, R * p : R * p + R] for p in range(8))
    lacc[48:112] += sum((gap_b * gap_b)[:, R * p : R * p + R] for p in range(8))
    lacc[112:176] += sum((gap_t * gap_t)[:, R * p : R * p + R] for p in range(2))
    grb = me.astype(bf16)
    gpd = nn(w["out_b"][...], twice(grb)) * dd
    gpdb = gpd.astype(bf16)
    gtrb = lanes([sum(gpd[:, R * p : R * p + R] for p in range(4 * g_, 4 * g_ + 4)) for g_ in (0, 1)]).astype(bf16)
    keep["gt"][:, tops] = halves(nn(w["dt_b"][...], gtrb))
    keep["gl"][i] = nn(w["db_b"][...], twice(gpdb))
    keep["hd"][i] = hdb
    keep["gr"][i] = grb
    keep["gpd"][i] = gpdb
    keep["qb"][i] = qb2
    keep["qt"][:, tops] = qt2
    keep["gtr"][:, tops] = gtrb


def top_backward(n, R, kt, w, keep):
    gltb = (keep["gt"][...] + kt * keep["gap_t"][...]).astype(bf16)
    keep["glt"][...] = gltb
    gptb = (nn(w["to_b"][...], twice(gltb)) * keep["dt"][...].astype(f32)).astype(bf16)
    keep["gpt"][...] = gptb
    gti = nn(w["ti_b"][...], twice(gptb))
    for i in range(n):
        for p in range(8):
            at = 2 * R * i + R * (p // 4)
            keep["gl"][i, :, R * p : R * p + R] += gti[64 * (p % 4) : 64 * (p % 4) + 64, at : at + R]


def backward_inner(i, kb, w, keep, acc):
    glbb = (keep["gl"][i] + kb * keep["gap_b"][i].astype(f32)).astype(bf16)
    gprb = (nn(w["ru_b"][...], twice(glbb)) * keep["dr"][i].astype(f32)).astype(bf16)
    both = jnp.concatenate([glbb, gprb], axis=0)
    keep["both"][i] = both
    acc["ar"][...] += nt(glbb, keep["ar"][i])


def backward_outer(i, w, keep, acc):
    gpeb = (nn(w["he_b"][...], twice(keep["both"][i])) * keep["de"][i].astype(f32)).astype(bf16)
    acc["e"][...] += nt(gpeb, keep["xb"][i])


def add(ref, v):
    ref[...] += v


def scratches(rows, R):
    return (
        [pltpu.VMEM(s, bf16) for s in WS.values()]
        + [pltpu.VMEM((rows // R, c, n * R), t) for c, n, t in KEEP.values()]
        + [pltpu.VMEM((c, rows * 2), t) for c, t in KEEP_TOP.values()]
        + [pltpu.VMEM(s, f32) for s in ACC.values()]
        + [pltpu.VMEM((2, 8, rows), f32), pltpu.VMEM((rows, 8), f32)] * 2
        + [pltpu.VMEM((176, R), f32)]
    )


def unscratch(scratch):
    scratch = list(scratch)
    take = lambda names: {k: scratch.pop(0) for k in names}
    w, keep, acc = take(WS), take(list(KEEP) + list(KEEP_TOP)), take(ACC)
    codes = ((scratch.pop(0), scratch.pop(0)), (scratch.pop(0), scratch.pop(0)))
    return w, keep, acc, codes, scratch


def swap_start(axis, n, src_at, buf, sems, at=0):
    me = lax.axis_index(axis)

    def go(peer, carry):
        @pl.when(peer != me)
        def _():
            pltpu.make_async_remote_copy(
                src_ref=src_at(peer), dst_ref=buf.at[me], send_sem=sems[0], recv_sem=sems[1],
                device_id={axis: peer}, device_id_type=pl.DeviceIdType.MESH,
            ).start()

        return carry

    lax.fori_loop(at, n, go, 0)


def swap_wait(axis, n, buf, sems, recv):
    others = buf.at[0 : n - 1]
    copy = pltpu.make_async_remote_copy(
        src_ref=others, dst_ref=others, send_sem=sems[0], recv_sem=sems[1],
        device_id={axis: lax.axis_index(axis)}, device_id_type=pl.DeviceIdType.MESH,
    )
    if recv:
        copy.wait_recv()
    else:
        copy.wait_send()


def total(v):
    while v.shape[0] % 16 == 0:
        v = halves(v)
    return jnp.sum(jnp.sum(v, axis=0, keepdims=True), axis=1, keepdims=True)


def in_order(buf, n):
    out = buf[0]
    for s in range(1, n):
        out = out + buf[s]
    return out

N_DP = 16
N_REP = 8
SHARE = 46
FIRST = 1
def share_start(shares, src, buf, sems):
    me = lax.axis_index("dp")
    for s in shares:
        @pl.when(me != s)
        def _():
            pltpu.make_async_remote_copy(
                src_ref=src.at[s], dst_ref=buf.at[me], send_sem=sems[0], recv_sem=sems[1],
                device_id={"dp": s}, device_id_type=pl.DeviceIdType.MESH,
            ).start()


def put_rows(ref, at, v):
    end = at + v.shape[0]
    for s in range(N_DP):
        lo, hi = max(at, SHARE * s), min(end, SHARE * s + SHARE)
        if lo < hi:
            ref[s, lo - SHARE * s : hi - SHARE * s] = v[lo - at : hi - at]


def each(n, f):
    if n == 1:
        f(0)
        return

    def go(i, carry):
        f(i)
        return carry

    lax.fori_loop(0, n, go, 0)


def kernel(*refs, R):
    sources, refs = refs[:11], refs[11:]
    (scal_out, params_out, first_out, second_out, mom_out, counts_out, sums_out, books_out), scratch = refs[:8], refs[8:]
    inputs, scratch = scratch[:11], scratch[11:]
    x_ref, m_ref, cb_ref, ct_ref, p_ref, first_ref, second_ref, mom_ref, cnt_ref, ema_ref, book_ref = inputs
    w, keep, acc, codes, scratch = unscratch(scratch)
    (
        lacc, valid_own, valid_all, grad_own, grad_all, part_own, part_all, sums_all, step_all,
        par_share, in_sems, *sems,
    ) = scratch
    loads = [pltpu.make_async_copy(a, b, in_sems.at[i]) for i, (a, b) in enumerate(zip(sources, inputs))]
    load_x, load_m, load_cb, load_ct, load_p, *load_rest, load_book = loads
    for load in (load_p, load_x, load_cb, load_ct, load_book, load_m, *load_rest):
        load.start()
    sems = [(sems[2 * i], sems[2 * i + 1]) for i in range(5)]
    sem_valid, sem_grad, sem_part, sem_sums, sem_step = sems
    dp = lax.axis_index("dp")
    rep = lax.axis_index("rep")
    rows = x_ref.shape[0]
    n = rows // R

    barrier = pltpu.get_barrier_semaphore()
    for axis, size, me in (("dp", N_DP, dp), ("rep", N_REP, rep)):
        def hello(k, carry):
            pl.semaphore_signal(
                barrier, inc=1, device_id={axis: lax.rem(me + k, size)}, device_id_type=pl.DeviceIdType.MESH
            )
            return carry

        lax.fori_loop(1, size, hello, 0)

    for load in (load_p, load_book, load_cb, load_ct):
        load.wait()
    weights(p_ref[...], book_ref, w)
    code_keys(*codes[0], cb_ref, 8)
    code_keys(*codes[1], ct_ref, 2)
    for v in acc.values():
        v[...] = jnp.zeros_like(v)
    lacc[...] = jnp.zeros_like(lacc)
    load_x.wait()
    each(n, lambda i: encoder(i, R, x_ref, codes, w, keep, acc))

    load_m.wait()
    valid = jnp.broadcast_to(total(m_ref[...].astype(f32)), (8, 128))
    valid_own[...] = jnp.concatenate(
        [
            acc[name][128 + a : 129 + a, 128 * j : 128 * j + 128]
            for name in ("sum_b", "sum_t") for a in (0, 1) for j in (0, 1)
        ] + [valid], axis=0
    )
    valid_all[dp] = valid_own[...]
    valid_src = lambda peer: valid_own
    pl.semaphore_wait(barrier, N_DP + N_REP - 2)
    swap_start("dp", N_DP, valid_src, valid_all, sem_valid)

    for d in range(N_DP):
        name, at = ("sum_b", "sum_t")[d // 8], 8 * (d % 8)
        part_own[d] = lanes([acc[name][at : at + 8], acc[name][64 + at : 72 + at]])
    part_src = lambda peer: part_own.at[peer]
    swap_start("dp", N_DP, part_src, part_all, sem_part)
    part_all[dp] = part_own[dp]

    each(n, lambda i: decoder(i, R, m_ref, codes, w, keep, acc, lacc))

    group_rows = rows * 8 * N_DP
    swap_wait("dp", N_DP, valid_all, sem_valid, True)
    stats = in_order(valid_all, N_DP)
    count = stats[8:9, 0:1]
    scale = 2.0 / count
    kb = beta_commit / (group_rows * EMB) * count
    kt = beta_commit / (group_rows // 4 * EMB) * count
    lane = lax.broadcasted_iota(jnp.int32, (1, 128), 1)
    losses = jnp.where(lane == 0, total(lacc[0:48]), jnp.where(lane == 1, total(lacc[48:112]), total(lacc[112:176])))
    for s in range(N_DP):
        grad_own[s, SHARE:48] = jnp.broadcast_to(losses, (48 - SHARE, 128))
    top_backward(n, R, kt, w, keep)
    each(n, lambda i: backward_inner(i, kb, w, keep, acc))
    each(n, lambda i: backward_outer(i, w, keep, acc))
    cross = acc["ar"][...]
    put_rows(grad_own, O_ENC, acc["e"][...].T * scale)
    put_rows(grad_own, O_RU, exact(cross, p_ref[O_L:O_TO], ((0,), (0,))) * scale)
    share_start((0, 1), grad_own, grad_all, sem_grad)
    put_rows(grad_own, O_TI, nt(keep["ti"][...], keep["gpt"][...]) * scale)
    share_start((2, 3, 4, 5, 6, 7), grad_own, grad_all, sem_grad)
    each(n, lambda i: add(acc["db"], nt(keep["qb"][i], keep["gpd"][i])))
    put_rows(grad_own, O_DB, halves(acc["db"][...]) * scale)
    put_rows(grad_own, O_DT, halves(nt(keep["qt"][...], keep["gtr"][...])) * scale)
    each(n, lambda i: add(acc["he"], nt(keep["both"][i], keep["he"][i])))
    put_rows(grad_own, O_RD, acc["he"][64:128] * scale)
    put_rows(grad_own, O_L, (acc["he"][0:64] + exact(cross, p_ref[O_RU:O_TI], ((1,), (0,)))) * scale)
    put_rows(grad_own, O_TO, nt(keep["ht"][...], keep["glt"][...]).T * scale)
    share_start((8, 9, 12, 13, 10, 11), grad_own, grad_all, sem_grad)
    each(n, lambda i: add(acc["out"], nt(keep["hd"][i], keep["gr"][i])))
    put_rows(grad_own, O_OUT, acc["out"][...].T * scale)
    share_start((14, 15), grad_own, grad_all, sem_grad)
    grad_all[dp] = grad_own[dp]

    for load in load_rest:
        load.wait()
    for s in range(N_DP):
        par_share[s, 0:SHARE] = p_ref[SHARE * s : SHARE * s + SHARE]
    swap_wait("dp", N_DP, part_all, sem_part, True)
    sums_all[dp] = in_order(part_all, N_DP)
    sums_src = lambda peer: sums_all.at[dp]
    swap_start("dp", FIRST, sums_src, sums_all, sem_sums)
    seen = jnp.concatenate([lanes([stats[4 * level + j : 4 * level + j + 1] for j in range(4)]) for level in (0, 1)], axis=0)
    counts_new = ema_decay * cnt_ref[...] + (1.0 - ema_decay) * seen
    counts_out[0] = counts_new
    totals = jnp.sum(counts_new, axis=1, keepdims=True)
    smooth = (counts_new + laplace_eps) / (totals + K * laplace_eps) * totals
    swap_wait("dp", N_DP, grad_all, sem_grad, True)
    summed = in_order(grad_all, N_DP)
    grads = summed[0:SHARE]
    own = par_share[dp][0:SHARE]
    first_new = beta_first * first_ref[:, 0, :] + (1.0 - beta_first) * grads
    second_new = beta_second * second_ref[:, 0, :] + (1.0 - beta_second) * grads * grads
    bias_first = 1.0 - beta_first**STEP
    bias_second = 1.0 - beta_second**STEP
    step_here = inner_rate * (
        first_new / bias_first / (jnp.sqrt(second_new / bias_second) + adam_eps) + weight_decay * own
    )
    step_all[rep, 0:SHARE] = step_here
    step_all[rep, SHARE:48] = jnp.zeros((48 - SHARE, 128), f32)
    step_src = lambda peer: step_all.at[rep]
    swap_start("rep", N_REP, step_src, step_all, sem_step)
    swap_start("dp", N_DP, sums_src, sums_all, sem_sums, FIRST)

    first_out[:, 0, :] = first_new
    second_out[:, 0, :] = second_new

    terms = summed[SHARE : SHARE + 1]
    loss = terms[:, 0:1] / count + beta_commit * (
        terms[:, 1:2] / (group_rows * EMB) + terms[:, 2:3] / (group_rows // 4 * EMB)
    )
    scal_out[...] = jnp.concatenate([jnp.broadcast_to(loss, (1, 128)), jnp.broadcast_to(count, (1, 128)), jnp.zeros((6, 128), f32)], axis=0)

    swap_wait("dp", N_DP, sums_all, sem_sums, True)
    for level in (0, 1):
        inverse = 1.0 / smooth[level : level + 1]
        for j in range(8):
            rows_j = slice(8 * j, 8 * j + 8)
            sums_new = ema_decay * ema_ref[level, rows_j] + (1.0 - ema_decay) * sums_all[8 * level + j]
            sums_out[0, level, rows_j] = sums_new
            books_out[0, level, rows_j] = sums_new * inverse

    swap_wait("rep", N_REP, step_all, sem_step, True)
    mean_delta = in_order(step_all, N_REP)[0:SHARE] * (1.0 / N_REP)
    momentum_new = outer_moment * mom_ref[...] + mean_delta
    mom_out[...] = momentum_new
    params_out[...] = own - outer_rate * (mean_delta + outer_moment * momentum_new)

    for axis, size, buf, sem in (
        ("dp", N_DP, valid_all, sem_valid), ("dp", N_DP, grad_all, sem_grad), ("dp", N_DP, part_all, sem_part),
        ("rep", N_REP, step_all, sem_step), ("dp", N_DP, sums_all, sem_sums),
    ):
        swap_wait(axis, size, buf, sem, False)


def hand_over(scal, *refs):
    n = (len(refs) - 3) // 2
    ins, (loss_out, valid_out), outs, sems = refs[:n], refs[n : n + 2], refs[n + 2 : -1], refs[-1]
    copies = [pltpu.make_async_copy(a, b, sems.at[i]) for i, (a, b) in enumerate(zip(ins, outs))]
    for c in copies:
        c.start()
    loss_out[0] = scal[0, 0]
    valid_out[0] = scal[1, 0]
    for c in copies:
        c.wait()


def shards(
    pixels, valid_mask, bottom_codes, top_codes, params, first_moment, second_moment, outer_momentum, ema_counts,
    ema_sums, codebooks, *, R,
):
    rows = pixels.shape[0]
    vm = pl.BlockSpec(memory_space=pltpu.VMEM)
    sm = pl.BlockSpec(memory_space=pltpu.SMEM)
    hbm = pl.BlockSpec(memory_space=pl.ANY)
    dma = pltpu.SemaphoreType.DMA
    args = (
        pixels, valid_mask, bottom_codes.reshape(-1, 128), top_codes.reshape(-1, 128), params,
        jnp.swapaxes(first_moment, 0, 1), jnp.swapaxes(second_moment, 0, 1), outer_momentum, ema_counts,
        jnp.swapaxes(ema_sums, 1, 2), jnp.swapaxes(codebooks, 1, 2),
    )
    results = [(SHARE, 128), (SHARE, 1, 128), (SHARE, 1, 128), (SHARE, 128), (1, 2, K), (1, 2, EMB, K), (1, 2, EMB, K)]
    inner = pl.pallas_call(
        functools.partial(kernel, R=R),
        out_shape=tuple(pltpu.VMEM(s, f32) for s in [(8, 128)] + results),
        in_specs=[hbm] * 11,
        out_specs=(vm,) * 8,
        scratch_shapes=[pltpu.VMEM(v.shape, v.dtype) for v in args]
        + scratches(rows, R)
        + [
            pltpu.VMEM((16, 128), f32), pltpu.VMEM((N_DP, 16, 128), f32),
            pltpu.VMEM((N_DP, 48, 128), f32), pltpu.VMEM((N_DP, 48, 128), f32),
            pltpu.VMEM((N_DP, 8, 512), f32), pltpu.VMEM((N_DP, 8, 512), f32), pltpu.VMEM((N_DP, 8, 512), f32),
            pltpu.VMEM((N_REP, 48, 128), f32), pltpu.VMEM((N_DP, 48, 128), f32), dma((11,)),
        ]
        + [dma] * 10,
        compiler_params=pltpu.CompilerParams(
            vmem_limit_bytes=60 * 2**20, collective_id=0, has_side_effects=True
        ),
    )(*args)
    shape = lambda *s: jax.ShapeDtypeStruct(s, f32)
    loss, valid, params, first, second, mom, counts, sums, books = pl.pallas_call(
        hand_over,
        out_shape=(shape(1), shape(1)) + tuple(shape(*s) for s in results),
        in_specs=[vm] * 8,
        out_specs=(sm, sm) + (hbm,) * 7,
        scratch_shapes=[dma((7,))],
    )(*(pltpu.with_memory_space_constraint(v, pltpu.VMEM) for v in inner))
    return (
        loss, valid, params, jnp.swapaxes(first, 0, 1), jnp.swapaxes(second, 0, 1), mom, counts,
        jnp.swapaxes(sums, 2, 3), jnp.swapaxes(books, 2, 3),
    )


def solution(mesh):
    return jax.shard_map(
        functools.partial(shards, R=1024),
        mesh=mesh,
        in_specs=(
            P(("rep", "dp"), None),
            P(("rep", "dp"), None),
            P(("rep", "dp")),
            P(("rep", "dp")),
            P(),
            P("rep", "dp", None),
            P("rep", "dp", None),
            P("dp", None),
            P(),
            P(),
            P(),
        ),
        out_specs=(
            P("rep"),
            P("rep"),
            P("dp", None),
            P("rep", "dp", None),
            P("rep", "dp", None),
            P("dp", None),
            P("rep", None, None),
            P("rep", None, None, None),
            P("rep", None, None, None),
        ),
        check_vma=False,
    )
```
